32 devices in a mesh: region: 8 (over z, x), order: 4 (over y, core).
Axes of the slice: x: 2, y: 2, z: 4, core: 2. Of those that a mesh axis runs over, the one named last changes fastest.
Arguments:
- runoff: float32 [240, 32, 1024], P(None, None, ('region', 'order')), may hold values from 0.01 to 2
- send_rows: int32 [8, 4, 32], P('region', 'order'), may hold values from 0 to 31
- remap_index: int32 [4096, 4], P(('region', 'order')), may hold values from 0 to 31
- remap_weight: float32 [4096, 4], P(('region', 'order')), may hold values from 0.05 to 1
- class_id: int32 [4096, 1], P(('region', 'order')), may hold values from 0 to 7; in each aligned block of 128 rows (0 to 127, 128 to 255, ...) at most 32 rows name the same one
- kernel_shape: float32 [8, 240], replicated, may hold values from 0.5 to 2
- kernel_rate: float32 [8], replicated, may hold values from 0.01 to 0.3
- outlets: int32 [8, 4, 32], P('region', 'order'), may hold values from 0 to 127, as said below
- incidence: int32 [8, 4, 32, 128], P('region', 'order'), may hold values from 0 to 1, as said below
Outputs:
- outflow: bfloat16 [240, 32, 4096], P(None, None, ('region', 'order'))
The draws below stay inside these ranges and needn't reach their ends.
Inputs may be any that keep to these rules, and one draw needn't show every extreme that they name: `send_rows`: row of the sending device's own grid rows. `class_id`: no class is named by more than 32 reaches of one device; on some device a class has exactly 32. `outlets`: the 32 outlet numbers of one device are distinct. `incidence`: each row has exactly one 1; no column of one device has more than one 1.
All inputs are finite; a program needn't handle non-finite values.
Results may differ from the reference program's by a relative error of at most 0.0038.
Values may be sent and summed in bfloat16 or wider, within the bound.
No kernel may reach another device: no remote copies, remote signals or barrier semaphores. Data moves between devices by JAX's collectives and lax.ppermute only.
A program may use at most 128 MiB of HBM per device.

```python
import math
import jax
import jax.numpy as jnp
import numpy as np
from jax import lax

H = 240
M = 32
K = 4
NCLASS = 8
OUT = 32
SLOT = 4
GRID_DEV = 32
CAT = 128
CAP = 32
RECV = 32
GRID = 1024
CATS = 4096
N_REGION = 8
N_ORDER = 4


def network(key):
    base_key = jax.random.fold_in(key, 11)
    first_key, second_key, third_key = jax.random.split(base_key, 3)
    device_count = N_REGION * N_ORDER
    through = OUT - OUT // 8
    orders = jax.vmap(lambda one_key: jax.random.permutation(one_key, CAT))(jax.random.split(first_key, device_count))
    outlet_ids = orders[:, :OUT]
    picks = jax.vmap(lambda one_key: jax.random.permutation(one_key, OUT))(jax.random.split(second_key, device_count))
    chosen = jnp.take_along_axis(outlet_ids, picks[:, :through], axis=1)
    others = orders[:, OUT:2 * OUT - through]
    targets = jnp.concatenate([chosen, others], axis=1)
    mixing = jax.vmap(lambda one_key: jax.random.permutation(one_key, OUT))(jax.random.split(third_key, device_count))
    targets = jnp.take_along_axis(targets, mixing, axis=1)
    return (outlet_ids.reshape(N_REGION, N_ORDER, OUT), targets.reshape(N_REGION, N_ORDER, OUT))


def draw_outlets(key, part):
    return network(key)[0].astype(jnp.int32)


def draw_incidence(key, part):
    targets = network(key)[1]
    return (targets[..., None] == jnp.arange(CAT)[None, None, None, :]).astype(jnp.int32)


def place_ends(entries, own_key, smallest, largest):
    longest = entries.shape.index(max(entries.shape))
    spots = []
    for shift in (0, 1):
        where = [jax.random.randint(jax.random.fold_in(own_key, axis), (), 0, length) for axis, length in enumerate(entries.shape)]
        where[longest] = (where[longest] + shift) % entries.shape[longest]
        spots.append(tuple(where))
    return entries.at[spots[0]].set(smallest).at[spots[1]].set(largest)


def shard_levels(rng, shape, pieces, low, largest):
    level = 1.0
    for position, shards_of in pieces:
        steps = jax.random.uniform(jax.random.fold_in(jax.random.fold_in(rng, 6), position), (shards_of,), jnp.float32, low / len(pieces), largest / len(pieces))
        level = level * jnp.repeat(jnp.exp(steps), shape[position] // shards_of).reshape((-1,) + (1,) * (len(shape) - 1 - position))
    return level


def assign_block(own_key, own, number, rows, number_of, top, limit, lean):
    sequence = jax.random.permutation(own_key, number_of)
    packed, usual = portions_of(number_of, rows * top, limit, lean, True), portions_of(number_of, rows * top, limit, lean, False)
    places = jnp.arange(number_of)

    def named(tallies, turn):
        used = int((tallies > 0).sum())
        fixed = max(1, used // 4)
        shifted = fixed + (places - fixed + turn * (used - fixed)) % max(1, number_of - fixed)
        return jnp.zeros((number_of,), jnp.int32).at[sequence[jnp.where(places < fixed, places, shifted)]].set(jnp.asarray(tallies, jnp.int32))

    tallies = jnp.where(number % 4 == 0, named(packed, number // 4), named(usual, number - number // 4 - 1))
    mixed = jax.random.permutation(jax.random.fold_in(own, 3), number_of)
    donor, taker = mixed[0:number_of // 2 * 2:2], mixed[1:number_of // 2 * 2:2]
    slack = jnp.minimum(tallies[donor] - 1, limit - tallies[taker]) // 2
    slack = jnp.where((donor == sequence[0]) | (taker == sequence[0]) | (tallies[taker] == 0), 0, jnp.maximum(slack, 0))
    shifted = jax.random.randint(jax.random.fold_in(own, 4), (number_of // 2,), 0, 1 << 20) % (slack + 1)
    tallies = tallies.at[donor].add(-shifted).at[taker].add(shifted)
    labels = jnp.searchsorted(jnp.cumsum(tallies), jnp.arange(rows * top), side="right").astype(jnp.int32)
    grid = labels.reshape(top, rows).T
    grid = grid[jax.random.permutation(jax.random.fold_in(own, 1), rows)]
    turn = jax.random.randint(jax.random.fold_in(own, 2), (rows, 1), 0, top)
    return jnp.take_along_axis(grid, (jnp.arange(top)[None, :] + turn) % top, axis=1)


def portions_of(number_of, total, reach, slope, full):
    loads = [(1 << 20) // math.isqrt(rank ** slope) + 1 for rank in range(1, number_of + 1)]
    largest = reach if full else min(reach, max(-(-total // number_of), total * loads[0] // sum(loads)))
    least = 1 if total - largest >= number_of - 1 else 0
    holding, surplus = [largest] + [least] * (number_of - 1), total - largest - least * (number_of - 1)
    while surplus > 0:
        movable = [i for i in range(1, number_of) if holding[i] < largest] or [i for i in range(1, number_of) if holding[i] < reach]
        mass, left = sum([loads[i] for i in movable]), surplus
        for i in movable:
            extra = min(reach - holding[i], max(1, left * loads[i] // mass), surplus)
            holding[i] = holding[i] + extra
            surplus = surplus - extra
    return np.array(holding)


def setup_inputs(seed: int = 0) -> dict:
    keys = jax.random.split(jax.random.key(seed), 10)
    runoff = jnp.clip(jnp.exp(math.log(2.0) - 5.2983174 * jax.random.uniform(keys[0], (H, M, GRID), jnp.float32) ** shard_levels(keys[0], (H, M, GRID), ((2, 32),), -0.2, 0.2)), 0.01, 2.0)
    send_rows = place_ends(jax.random.randint(keys[1], (N_REGION, N_ORDER, RECV), 0, GRID_DEV), jax.random.fold_in(keys[1], 1), 0, GRID_DEV - 1).astype(jnp.int32)
    remap_index = place_ends(jax.random.randint(keys[2], (CATS, K), 0, RECV), jax.random.fold_in(keys[2], 1), 0, RECV - 1).astype(jnp.int32)
    remap_weight = jnp.clip(jnp.exp(math.log(1.0) - 2.9957323 * jax.random.uniform(keys[3], (CATS, K), jnp.float32) ** shard_levels(keys[3], (CATS, K), ((0, 32),), -0.2, 0.2)), 0.05, 1.0)
    class_id_keys = jax.random.split(jax.random.fold_in(keys[4], 1), CATS // CAT)
    class_id_turns = jax.random.permutation(jax.random.fold_in(keys[4], 3), CATS // CAT)
    class_id = jax.vmap(lambda own, number: assign_block(jax.random.fold_in(keys[4], 2), own, number, CAT, NCLASS, 1, CAP, 2))(class_id_keys, class_id_turns).reshape((CATS, 1))
    kernel_shape = jnp.clip(jnp.exp(jax.random.uniform(keys[5], (NCLASS, H), jnp.float32, math.log(0.5), math.log(2.0))), 0.5, 2.0)
    kernel_rate = jnp.clip(jnp.exp(jax.random.uniform(keys[6], (NCLASS,), jnp.float32, math.log(0.01), math.log(0.3))), 0.01, 0.3)
    outlets = draw_outlets(jax.random.fold_in(keys[9], 71), 0)
    incidence = draw_incidence(jax.random.fold_in(keys[9], 71), 0)
    return {"runoff": runoff, "send_rows": send_rows, "remap_index": remap_index, "remap_weight": remap_weight, "class_id": class_id, "kernel_shape": kernel_shape, "kernel_rate": kernel_rate, "outlets": outlets, "incidence": incidence}


def kernels(kernel_shape, kernel_rate):
    lag_hours = jnp.arange(H, dtype=jnp.float32)
    kernel = kernel_rate[:, None] * kernel_shape * jnp.exp(-kernel_rate[:, None] * lag_hours[None, :])
    rounded = lax.optimization_barrier(kernel.astype(jnp.bfloat16))
    return rounded.astype(jnp.float32)


def convolve(signal, kernel_rows):
    length = 2 * H
    signal_freq = jnp.fft.rfft(signal, n=length, axis=0)
    kernel_freq = jnp.fft.rfft(kernel_rows.T, n=length, axis=0)
    return jnp.fft.irfft(signal_freq * kernel_freq[:, None, :], n=length, axis=0)[:H]


def reference(runoff, send_rows, remap_index, remap_weight, class_id, kernel_shape, kernel_rate, outlets, incidence):
    kernel_table = kernels(kernel_shape, kernel_rate)
    grid_rows = runoff.reshape(H, M, N_REGION, N_ORDER, GRID_DEV)
    index_all = remap_index.reshape(N_REGION, N_ORDER, CAT, K)
    weight_all = remap_weight.reshape(N_REGION, N_ORDER, CAT, K)
    class_all = class_id.reshape(N_REGION, N_ORDER, CAT)
    source_region = jnp.arange(N_REGION, dtype=jnp.int32)[:, None, None]
    source_level = jnp.arange(N_ORDER, dtype=jnp.int32)[None, :, None]
    reach_ids = jnp.arange(CAT, dtype=jnp.int32)

    def one_level(panel, inputs):
        received, index, weight, classes, outlet_ids, links = inputs
        lateral = jnp.zeros((H, M, CAT), jnp.float32)
        for column in range(K):
            lateral = lateral + weight[:, column] * jnp.take(received, index[:, column], axis=2)
        lateral = lax.optimization_barrier(lateral.astype(jnp.bfloat16)).astype(jnp.float32)
        base_flow = convolve(lateral, kernel_table[classes])
        targets = jnp.sum(links * reach_ids[None, :], axis=1).astype(jnp.int32)
        routed = convolve(panel.astype(jnp.float32), kernel_table[classes[targets]])
        total = base_flow.at[:, :, targets].add(routed)
        return total[:, :, outlet_ids].astype(jnp.bfloat16), total.astype(jnp.bfloat16)

    def one_region(region):
        chosen = lax.dynamic_slice_in_dim(send_rows, region * SLOT, SLOT, 2)
        gathered = grid_rows[:, :, source_region, source_level, chosen]
        gathered = jnp.transpose(gathered, (3, 0, 1, 2, 4)).reshape(N_ORDER, H, M, RECV)
        start = jnp.zeros((H, M, OUT), jnp.bfloat16)
        inputs = (gathered, index_all[region], weight_all[region], class_all[region], outlets[region], incidence[region])
        unused, flows = lax.scan(one_level, start, inputs)
        return flows

    every = lax.map(one_region, jnp.arange(N_REGION, dtype=jnp.int32))
    return jnp.transpose(every, (2, 3, 0, 1, 4)).reshape(H, M, N_REGION * N_ORDER * CAT)
```

```python
import functools
import jax
import jax.numpy as jnp
from jax import lax
from jax.experimental import pallas as pl
from jax.experimental.pallas import tpu as pltpu
from jax.sharding import Mesh, PartitionSpec as P

BF = jnp.bfloat16
F32 = jnp.float32
MB = 8
LANES = 128
VMEM_LIMIT = 56 * 1024 * 1024


def iota(shape, dim):
    return lax.broadcasted_iota(jnp.int32, shape, dim)


def mm(a, b):
    return jnp.dot(a, b, preferred_element_type=F32)


def tmm(a, b):
    return lax.dot_general(a, b, (((0,), (0,)), ((), ())), preferred_element_type=F32)


def one_hot(condition):
    return jnp.where(condition, 1.0, 0.0).astype(BF)


def split(value):
    high = value.astype(BF)
    return high, (value - high.astype(F32)).astype(BF)


def call(kernel, out_shape, flops, **extra):
    nbytes = sum(s.size * s.dtype.itemsize for s in jax.tree.leaves(out_shape))
    return pl.pallas_call(
        kernel,
        out_shape=out_shape,
        compiler_params=pltpu.CompilerParams(vmem_limit_bytes=VMEM_LIMIT),
        cost_estimate=pl.CostEstimate(flops=flops, bytes_accessed=2 * nbytes, transcendentals=0),
        **extra,
    )


def vmem(count):
    return [pl.BlockSpec(memory_space=pltpu.VMEM)] * count


SCALAR = pl.BlockSpec(memory_space=pltpu.SMEM)


def convolve(table, value, classes, class_count, padded):
    pad = padded - value.shape[0]
    if pad:
        value = jnp.concatenate([value, jnp.zeros((pad, value.shape[1]), BF)], axis=0)
    parts = [value * one_hot(classes == float(k)) for k in range(class_count)]
    return mm(table, jnp.concatenate(parts, axis=0))


def pack_kernel(slot, x_ref, rows_ref, idx_ref, w_ref, cls_ref, outl_ref, inc_ref, send_ref, raw_ref):
    members, grid, hours = x_ref.shape
    regions = send_ref.shape[0]
    per = MB * slot
    count = regions * per
    recv = rows_ref.shape[1]
    row = iota((count, recv), 0)
    wanted = (row // per) * slot + row % slot
    rows = rows_ref[...].astype(F32)
    chosen = jnp.sum(jnp.where(iota((count, recv), 1) == wanted, rows, 0.0), axis=1, keepdims=True)
    lane = iota((count, MB * grid), 1)
    member = (iota((count, MB * grid), 0) // slot) % MB
    select = one_hot((lane // grid == member) & ((lane % grid).astype(F32) == chosen))
    half = members // 2
    for block in range(members // MB):
        x = x_ref[block * MB : (block + 1) * MB].reshape(MB * grid, hours).astype(BF)
        y = mm(select, x).astype(BF).reshape(regions, per, hours)
        core, inner = divmod(block, half // MB)
        send_ref[:, core, inner * per : (inner + 1) * per, :] = y
    raw_ref[...] = jnp.zeros_like(raw_ref)
    raw_ref[0 : idx_ref.shape[0], :] = idx_ref[...].astype(F32)
    raw_ref[8 : 8 + w_ref.shape[0], :] = w_ref[...]
    raw_ref[16:17, :] = cls_ref[...].astype(F32)
    raw_ref[24:25, 0 : outl_ref.shape[1]] = outl_ref[...].astype(F32)
    raw_ref[32:, :] = inc_ref[...].astype(F32)


def prep_kernel(
    slot, columns, core_ref, own_ref, other_ref, rate_ref, shape_ref,
    table_ref, mix_ref, pass_ref, cls_out_ref, wide_ref, link_ref, cls_target_ref, cls_own_ref,
):
    core = core_ref[0]
    class_count, hours = shape_ref.shape
    padded = table_ref.shape[1] // class_count
    kap = mix_ref.shape[2]
    recv = kap // MB
    per = MB * slot
    outs = own_ref.shape[0] - 32
    reaches = own_ref.shape[1]
    wide = MB * outs

    lag = iota((class_count, hours), 1).astype(F32)
    rate = rate_ref[...]
    hydro = (rate * shape_ref[...] * jnp.exp(-rate * lag)).astype(BF)
    reverse = one_hot((iota((hours, padded), 0) + iota((hours, padded), 1)) % padded == 0)
    turned = mm(hydro, reverse)
    early = iota((padded, padded), 0)
    late = iota((padded, padded), 1)
    for k in range(class_count):
        rolled = pltpu.roll(
            jnp.broadcast_to(turned[k : k + 1, :], (padded, padded)), 0, 1, stride=1, stride_axis=0
        )
        rolled = jnp.where(late <= early, rolled, 0.0)
        table_ref[:, k * padded : (k + 1) * padded] = rolled[:hours].astype(BF)

    row_p = iota((kap, recv), 0)
    expand = one_hot((row_p // per) * slot + row_p % slot == iota((kap, recv), 1))
    tile = one_hot(iota((reaches, wide), 0) == iota((reaches, wide), 1) % outs)
    member = (iota((kap, wide), 0) // slot) % MB
    lane_member = iota((kap, wide), 1) // outs

    def weights(raw):
        total = jnp.zeros((recv, reaches), F32)
        for j in range(columns):
            hit = iota((recv, reaches), 0).astype(F32) == raw[j : j + 1, :]
            total = total + jnp.where(hit, raw[8 + j : 9 + j, :], 0.0)
        return split(total)

    for level in range(2):
        mine = core == level
        raw = jnp.where(mine, own_ref[...], other_ref[...])
        outlet_lanes = mm(raw[24:32, :].astype(BF), tile)[0:1, :]
        pick = one_hot(iota((reaches, wide), 0).astype(F32) == outlet_lanes)
        for part, weight in enumerate(weights(raw)):
            spread = mm(expand, mm(weight, pick).astype(BF))
            mix_ref[level, part] = jnp.where(member == lane_member, spread, 0.0).astype(BF)
        moved = mm(raw[32:, :].astype(BF), pick)
        moved = jnp.concatenate([moved] * MB, axis=0)
        here = iota((wide, wide), 0) // outs == iota((wide, wide), 1) // outs
        pass_ref[level] = jnp.where(here, moved, 0.0).astype(BF)
        cls_out_ref[level] = mm(raw[16:24, :].astype(BF), pick)

    own = own_ref[...]
    for part, weight in enumerate(weights(own)):
        spread = mm(expand, weight)
        owner = (iota((kap, reaches), 0) // slot) % MB
        for m in range(MB):
            wide_ref[part, :, m * reaches : (m + 1) * reaches] = jnp.where(owner == m, spread, 0.0).astype(BF)
    links = own[32:, :].astype(BF)
    cls_own_ref[...] = own[16:24, :]
    target = lax.dot_general(
        own[16:24, :].astype(BF),
        jnp.concatenate([links] * MB, axis=0),
        (((1,), (1,)), ((), ())),
        preferred_element_type=F32,
    )
    cls_target_ref[...] = target
    group = link_ref.shape[0] // outs
    stacked = jnp.concatenate([own[32:, :]] * group, axis=0)
    owner = iota((group * outs, reaches), 0) // outs
    for m in range(group):
        link_ref[:, m * reaches : (m + 1) * reaches] = jnp.where(owner == m, stacked, 0.0).astype(BF)


def head_kernel(
    class_count, core_ref, rows_ref, table_ref, mix_ref, pass_ref, cls_ref,
    even_ref, odd_ref, panel_ref, own_ref, send_ref,
):
    core = core_ref[0]
    padded = table_ref.shape[1] // class_count
    regions, _, total, hours = rows_ref.shape
    blocks = even_ref.shape[0]
    per = total // blocks
    for block in range(blocks):
        rows = []
        lateral = []
        for level in range(2):
            one = rows_ref[:, level, block * per : (block + 1) * per, :].reshape(regions * per, hours)
            rows.append(one)
            lateral.append((tmm(one, mix_ref[level, 0]) + tmm(one, mix_ref[level, 1])).astype(BF))
        first = core == 0
        own_ref[block] = jnp.where(first, rows[0], rows[1])
        send_ref[block] = jnp.where(first, rows[1], rows[0])
        even = convolve(table_ref[...], lateral[0], cls_ref[0, 0:1, :], class_count, padded)
        odd = convolve(table_ref[...], lateral[1], cls_ref[1, 0:1, :], class_count, padded)
        even_ref[block] = even
        odd_ref[block] = odd
        inflow = mm(even.astype(BF), pass_ref[1]).astype(BF)
        panel = odd + convolve(table_ref[...], inflow, cls_ref[1, 0:1, :], class_count, padded)
        panel_ref[block] = panel.astype(BF)


def hop_kernel(
    class_count, core_ref, inflow_ref, table_ref, pass_ref, cls_ref, even_ref, odd_ref,
    panel_ref, own_ref, send_ref,
):
    core = core_ref[0]
    padded = table_ref.shape[1] // class_count
    for block in range(even_ref.shape[0]):
        arrived = inflow_ref[block]
        moved = mm(arrived, pass_ref[0]).astype(BF)
        even = even_ref[block] + convolve(table_ref[...], moved, cls_ref[0, 0:1, :], class_count, padded)
        even = even.astype(BF)
        first = core == 0
        own_ref[block] = jnp.where(first, arrived, even)
        send_ref[block] = jnp.where(first, even, arrived)
        if panel_ref is not None:
            moved = mm(even, pass_ref[1]).astype(BF)
            odd = odd_ref[block] + convolve(
                table_ref[...], moved, cls_ref[1, 0:1, :], class_count, padded
            )
            panel_ref[block] = odd.astype(BF)


def last_hop_kernel(
    class_count, core_ref, inflow_ref, table_ref, pass_ref, cls_ref, even_ref, own_ref, send_ref
):
    hop_kernel(
        class_count, core_ref, inflow_ref, table_ref, pass_ref, cls_ref, even_ref, None,
        None, own_ref, send_ref,
    )


def base_kernel(class_count, rows_ref, table_ref, wide_ref, cls_ref, base_ref):
    padded = table_ref.shape[1] // class_count
    reaches = cls_ref.shape[1]
    rows = rows_ref[0]
    classes = cls_ref[0:1, :]
    pair = max(1, 256 // reaches)
    width = pair * reaches
    classes = jnp.concatenate([classes] * pair, axis=1)
    for start in range(0, base_ref.shape[2], width):
        lateral = tmm(rows, wide_ref[0, :, start : start + width])
        lateral = lateral + tmm(rows, wide_ref[1, :, start : start + width])
        base_ref[0, :, start : start + width] = convolve(
            table_ref[...], lateral.astype(BF), classes, class_count, padded
        )


def final_kernel(class_count, place_ref, inflow_ref, base_ref, table_ref, link_ref, cls_ref, *rest):
    out_ref, scratch = rest[-2:]
    padded = table_ref.shape[1] // class_count
    blocks, hours, _ = inflow_ref.shape
    members = out_ref.shape[1]
    reaches = out_ref.shape[2]
    lanes, width = link_ref.shape
    links = jnp.concatenate([link_ref[...]] * 2, axis=0)
    for block in range(blocks):
        routed = convolve(table_ref[...], inflow_ref[block], cls_ref[0:1, :], class_count, padded)
        high, low = split(routed)
        for part in range(routed.shape[1] // lanes):
            cut = slice(part * lanes, (part + 1) * lanes)
            spread = mm(jnp.concatenate([high[:, cut], low[:, cut]], axis=1), links)
            total = spread + base_ref[block, :, part * width : (part + 1) * width]
            for j in range(width // reaches):
                member = block * MB + part * (width // reaches) + j
                scratch[pl.ds(member, hours, stride=members), :] = total[
                    :, j * reaches : (j + 1) * reaches
                ]
    out_ref[...] = scratch[...].reshape(hours, members, reaches).astype(BF)


def local(
    runoff, send_rows, remap_index, remap_weight, class_id, kernel_shape, kernel_rate, outlets, incidence
):
    hours, members, grid = runoff.shape
    regions = lax.axis_size("region")
    pairs = lax.axis_size("pair")
    class_count = kernel_shape.shape[0]
    reaches, columns = remap_index.shape
    recv = send_rows.size
    slot = recv // regions
    outs = outlets.size
    half = members // 2
    blocks = half // MB
    padded = -(-hours // LANES) * LANES
    per = MB * slot
    kap = regions * per
    wide = MB * outs
    group = max(1, LANES // outs)
    core = lax.axis_index("core").astype(jnp.int32)
    core_arg = core.reshape(1)
    swap = [(0, 1), (1, 0)]

    def struct(shape, dtype):
        return jax.ShapeDtypeStruct(shape, dtype)

    send, raw = call(
        functools.partial(pack_kernel, slot),
        (struct((regions, 2, blocks * per, hours), BF), struct((32 + outs, reaches), F32)),
        2 * kap * MB * grid * hours * blocks * 2,
        in_specs=vmem(7),
        out_specs=tuple(vmem(2)),
    )(
        jnp.transpose(runoff, (1, 2, 0)),
        send_rows.reshape(1, recv),
        remap_index.T,
        remap_weight.T,
        class_id.T,
        outlets.reshape(1, outs),
        incidence.reshape(outs, reaches),
    )
    received = lax.all_to_all(
        send.reshape(regions * 2, blocks * per, hours), ("region", "core"), 0, 0
    ).reshape(regions, 2, blocks * per, hours)
    other = lax.ppermute(raw, "core", swap)
    table, mix, passing, cls_out, wide_mix, link, cls_target, cls_own = call(
        functools.partial(prep_kernel, slot, columns),
        (
            struct((hours, class_count * padded), BF),
            struct((2, 2, kap, wide), BF),
            struct((2, wide, wide), BF),
            struct((2, 8, wide), F32),
            struct((2, kap, MB * reaches), BF),
            struct((group * outs, group * reaches), BF),
            struct((8, wide), F32),
            struct((8, reaches), F32),
        ),
        10_000_000,
        in_specs=[SCALAR] + vmem(4),
        out_specs=tuple(vmem(8)),
    )(core_arg, raw, other, kernel_rate.reshape(class_count, 1), kernel_shape)

    conv_flops = 2 * hours * class_count * padded * wide
    panel_shape = struct((blocks, hours, wide), BF)
    even, odd, panel, rows_own, rows_send = call(
        functools.partial(head_kernel, class_count),
        (
            struct((blocks, hours, wide), F32),
            struct((blocks, hours, wide), F32),
            panel_shape,
            struct((blocks, kap, hours), BF),
            struct((blocks, kap, hours), BF),
        ),
        3 * blocks * conv_flops,
        in_specs=[SCALAR] + vmem(5),
        out_specs=tuple(vmem(5)),
    )(core_arg, received, table, mix, passing, cls_out)

    inflow = jnp.zeros(panel_shape.shape, BF)
    own = given = None
    for step in range(pairs - 1):
        arrived = lax.ppermute(panel, "pair", [(step, step + 1)])
        inflow = arrived if step == 0 else inflow + arrived
        if step < pairs - 2:
            panel, own, given = call(
                functools.partial(hop_kernel, class_count),
                (panel_shape, panel_shape, panel_shape),
                2 * blocks * conv_flops,
                in_specs=[SCALAR] + vmem(6),
                out_specs=tuple(vmem(3)),
            )(core_arg, inflow, table, passing, cls_out, even, odd)
    if pairs == 1:
        inflow = jnp.zeros(panel_shape.shape, BF)
    rows_other = lax.ppermute(rows_send, "core", swap)

    def base(rows):
        return call(
            functools.partial(base_kernel, class_count),
            struct((blocks, hours, MB * reaches), F32),
            blocks * conv_flops * reaches // outs,
            grid=(blocks,),
            in_specs=[pl.BlockSpec((1, kap, hours), lambda b: (b, 0, 0))] + vmem(3),
            out_specs=pl.BlockSpec((1, hours, MB * reaches), lambda b: (b, 0, 0)),
        )(rows, table, wide_mix, cls_own)

    base_own = base(rows_own)
    base_other = base(rows_other)
    own, given = call(
        functools.partial(last_hop_kernel, class_count),
        (panel_shape, panel_shape),
        blocks * conv_flops,
        in_specs=[SCALAR] + vmem(5),
        out_specs=tuple(vmem(2)),
    )(core_arg, inflow, table, passing, cls_out, even)
    gotten = lax.ppermute(given, "core", swap)

    def final(place, panel_rows, base_flow, before):
        extra = [] if before is None else [before]
        return pl.pallas_call(
            functools.partial(final_kernel, class_count),
            out_shape=struct((hours, members, reaches), BF),
            grid_spec=pltpu.PrefetchScalarGridSpec(
                num_scalar_prefetch=1,
                grid=(1,),
                in_specs=vmem(5) + [pl.BlockSpec(memory_space=pl.ANY)] * len(extra),
                out_specs=pl.BlockSpec((hours, half, reaches), lambda g, place: (0, place[0], 0)),
                scratch_shapes=[pltpu.VMEM((hours * half, reaches), F32)],
            ),
            input_output_aliases={6: 0} if extra else {},
            compiler_params=pltpu.CompilerParams(vmem_limit_bytes=VMEM_LIMIT),
            cost_estimate=pl.CostEstimate(
                flops=2 * blocks * conv_flops, bytes_accessed=6_000_000, transcendentals=0
            ),
        )(place, panel_rows, base_flow, table, link, cls_target, *extra)

    out = final(core_arg, own, base_own, None)
    return final(1 - core_arg, gotten, base_other, out)


def solution(mesh):
    regions, orders = mesh.shape["region"], mesh.shape["order"]
    split_mesh = Mesh(mesh.devices.reshape(regions, orders // 2, 2), ("region", "pair", "core"))
    order = ("pair", "core")
    every = ("region", "pair", "core")
    return jax.shard_map(
        local,
        mesh=split_mesh,
        in_specs=(
            P(None, None, every),
            P("region", order, None),
            P(every, None),
            P(every, None),
            P(every, None),
            P(),
            P(),
            P("region", order, None),
            P("region", order, None, None),
        ),
        out_specs=P(None, None, every),
        check_vma=False,
    )
```

```python
import functools
import jax
import jax.numpy as jnp
from jax import lax
from jax.experimental import pallas as pl
from jax.experimental.pallas import tpu as pltpu
from jax.sharding import Mesh, PartitionSpec as P

BF = jnp.bfloat16
F32 = jnp.float32
MB = 8
LANES = 128
VMEM_LIMIT = 20 * 1024 * 1024
WHOLE_VMEM = 56 * 1024 * 1024


def iota(shape, dim):
    return lax.broadcasted_iota(jnp.int32, shape, dim)


def mm(a, b):
    return jnp.dot(a, b, preferred_element_type=F32)


def tmm(a, b):
    return lax.dot_general(a, b, (((0,), (0,)), ((), ())), preferred_element_type=F32)


def one_hot(condition):
    return jnp.where(condition, 1.0, 0.0).astype(BF)


def split(value):
    high = value.astype(BF)
    return high, (value - high.astype(F32)).astype(BF)


def call(kernel, out_shape, flops, limit=VMEM_LIMIT, **extra):
    nbytes = sum(s.size * s.dtype.itemsize for s in jax.tree.leaves(out_shape))
    return pl.pallas_call(
        kernel,
        out_shape=out_shape,
        compiler_params=pltpu.CompilerParams(vmem_limit_bytes=limit),
        cost_estimate=pl.CostEstimate(flops=flops, bytes_accessed=2 * nbytes, transcendentals=0),
        **extra,
    )


def vmem(count):
    return [pl.BlockSpec(memory_space=pltpu.VMEM)] * count


SCALAR = pl.BlockSpec(memory_space=pltpu.SMEM)


def convolve(table, value, classes, class_count, padded):
    pad = padded - value.shape[0]
    if pad:
        value = jnp.concatenate([value, jnp.zeros((pad, value.shape[1]), BF)], axis=0)
    parts = [value * one_hot(classes == float(k)) for k in range(class_count)]
    return mm(table, jnp.concatenate(parts, axis=0))


def pack_kernel(slot, x_ref, rows_ref, idx_ref, w_ref, cls_ref, outl_ref, inc_ref, send_ref, raw_ref):
    members, grid, hours = x_ref.shape
    regions = send_ref.shape[0]
    per = MB * slot
    count = regions * per
    recv = rows_ref.shape[1]
    row = iota((count, recv), 0)
    wanted = (row // per) * slot + row % slot
    rows = rows_ref[...].astype(F32)
    chosen = jnp.sum(jnp.where(iota((count, recv), 1) == wanted, rows, 0.0), axis=1, keepdims=True)
    lane = iota((count, MB * grid), 1)
    member = (iota((count, MB * grid), 0) // slot) % MB
    select = one_hot((lane // grid == member) & ((lane % grid).astype(F32) == chosen))
    half = members // 2
    for block in range(members // MB):
        x = x_ref[block * MB : (block + 1) * MB].reshape(MB * grid, hours).astype(BF)
        y = mm(select, x).astype(BF).reshape(regions, per, hours)
        core, inner = divmod(block, half // MB)
        send_ref[:, core, inner * per : (inner + 1) * per, :] = y
    raw_ref[...] = jnp.zeros_like(raw_ref)
    raw_ref[0 : idx_ref.shape[0], :] = idx_ref[...].astype(F32)
    raw_ref[8 : 8 + w_ref.shape[0], :] = w_ref[...]
    raw_ref[16:17, :] = cls_ref[...].astype(F32)
    raw_ref[24:25, 0 : outl_ref.shape[1]] = outl_ref[...].astype(F32)
    raw_ref[32:, :] = inc_ref[...].astype(F32)


def prep_kernel(
    slot, columns, core_ref, own_ref, other_ref, rate_ref, shape_ref,
    table_ref, mix_ref, pass_ref, cls_out_ref, wide_ref, link_ref, cls_target_ref, cls_own_ref,
):
    core = core_ref[0]
    class_count, hours = shape_ref.shape
    padded = table_ref.shape[1] // class_count
    kap = mix_ref.shape[2]
    recv = kap // MB
    per = MB * slot
    outs = own_ref.shape[0] - 32
    reaches = own_ref.shape[1]
    wide = MB * outs

    lag = iota((class_count, hours), 1).astype(F32)
    rate = jnp.where(iota((class_count, class_count), 0) == iota((class_count, class_count), 1), rate_ref[...], 0.0)
    rate = jnp.sum(rate, axis=1, keepdims=True)
    hydro = (rate * shape_ref[...] * jnp.exp(-rate * lag)).astype(BF)
    reverse = one_hot((iota((hours, padded), 0) + iota((hours, padded), 1)) % padded == 0)
    turned = mm(hydro, reverse)
    early = iota((padded, padded), 0)
    late = iota((padded, padded), 1)
    for k in range(class_count):
        rolled = pltpu.roll(
            jnp.broadcast_to(turned[k : k + 1, :], (padded, padded)), 0, 1, stride=1, stride_axis=0
        )
        rolled = jnp.where(late <= early, rolled, 0.0)
        table_ref[:, k * padded : (k + 1) * padded] = rolled[:hours].astype(BF)

    row_p = iota((kap, recv), 0)
    expand = one_hot((row_p // per) * slot + row_p % slot == iota((kap, recv), 1))
    tile = one_hot(iota((reaches, wide), 0) == iota((reaches, wide), 1) % outs)
    member = (iota((kap, wide), 0) // slot) % MB
    lane_member = iota((kap, wide), 1) // outs

    def weights(raw):
        total = jnp.zeros((recv, reaches), F32)
        for j in range(columns):
            hit = iota((recv, reaches), 0).astype(F32) == raw[j : j + 1, :]
            total = total + jnp.where(hit, raw[8 + j : 9 + j, :], 0.0)
        return split(total)

    for level in range(2):
        mine = core == level
        raw = jnp.where(mine, own_ref[...], other_ref[...])
        outlet_lanes = mm(raw[24:32, :].astype(BF), tile)[0:1, :]
        pick = one_hot(iota((reaches, wide), 0).astype(F32) == outlet_lanes)
        for part, weight in enumerate(weights(raw)):
            spread = mm(expand, mm(weight, pick).astype(BF))
            mix_ref[level, part] = jnp.where(member == lane_member, spread, 0.0).astype(BF)
        moved = mm(raw[32:, :].astype(BF), pick)
        moved = jnp.concatenate([moved] * MB, axis=0)
        here = iota((wide, wide), 0) // outs == iota((wide, wide), 1) // outs
        pass_ref[level] = jnp.where(here, moved, 0.0).astype(BF)
        cls_out_ref[level] = mm(raw[16:24, :].astype(BF), pick)

    own = own_ref[...]
    for part, weight in enumerate(weights(own)):
        spread = mm(expand, weight)
        owner = (iota((kap, reaches), 0) // slot) % MB
        for m in range(MB):
            wide_ref[part, :, m * reaches : (m + 1) * reaches] = jnp.where(owner == m, spread, 0.0).astype(BF)
    links = own[32:, :].astype(BF)
    cls_own_ref[...] = own[16:24, :]
    target = lax.dot_general(
        own[16:24, :].astype(BF),
        jnp.concatenate([links] * MB, axis=0),
        (((1,), (1,)), ((), ())),
        preferred_element_type=F32,
    )
    cls_target_ref[...] = target
    group = link_ref.shape[0] // outs
    stacked = jnp.concatenate([own[32:, :]] * group, axis=0)
    owner = iota((group * outs, reaches), 0) // outs
    for m in range(group):
        link_ref[:, m * reaches : (m + 1) * reaches] = jnp.where(owner == m, stacked, 0.0).astype(BF)


def head_kernel(
    class_count, core_ref, rows_ref, table_ref, mix_ref, pass_ref, cls_ref,
    even_ref, odd_ref, panel_ref, own_ref, send_ref,
):
    core = core_ref[0]
    padded = table_ref.shape[1] // class_count
    regions, _, total, hours = rows_ref.shape
    blocks = even_ref.shape[0]
    per = total // blocks
    for block in range(blocks):
        rows = []
        lateral = []
        for level in range(2):
            one = rows_ref[:, level, block * per : (block + 1) * per, :].reshape(regions * per, hours)
            rows.append(one)
            lateral.append((tmm(one, mix_ref[level, 0]) + tmm(one, mix_ref[level, 1])).astype(BF))
        first = core == 0
        own_ref[block] = jnp.where(first, rows[0], rows[1])
        send_ref[block] = jnp.where(first, rows[1], rows[0])
        even = convolve(table_ref[...], lateral[0], cls_ref[0, 0:1, :], class_count, padded)
        odd = convolve(table_ref[...], lateral[1], cls_ref[1, 0:1, :], class_count, padded)
        even_ref[block] = even
        odd_ref[block] = odd
        inflow = mm(even.astype(BF), pass_ref[1]).astype(BF)
        panel = odd + convolve(table_ref[...], inflow, cls_ref[1, 0:1, :], class_count, padded)
        panel_ref[block] = panel.astype(BF)


def hop_kernel(
    class_count, core_ref, inflow_ref, table_ref, pass_ref, cls_ref, even_ref, odd_ref,
    panel_ref, own_ref, send_ref,
):
    core = core_ref[0]
    padded = table_ref.shape[1] // class_count
    for block in range(even_ref.shape[0]):
        arrived = inflow_ref[block]
        moved = mm(arrived, pass_ref[0]).astype(BF)
        even = even_ref[block] + convolve(table_ref[...], moved, cls_ref[0, 0:1, :], class_count, padded)
        even = even.astype(BF)
        first = core == 0
        own_ref[block] = jnp.where(first, arrived, even)
        send_ref[block] = jnp.where(first, even, arrived)
        if panel_ref is not None:
            moved = mm(even, pass_ref[1]).astype(BF)
            odd = odd_ref[block] + convolve(
                table_ref[...], moved, cls_ref[1, 0:1, :], class_count, padded
            )
            panel_ref[block] = odd.astype(BF)


def last_hop_kernel(
    class_count, core_ref, inflow_ref, table_ref, pass_ref, cls_ref, even_ref, own_ref, send_ref
):
    hop_kernel(
        class_count, core_ref, inflow_ref, table_ref, pass_ref, cls_ref, even_ref, None,
        None, own_ref, send_ref,
    )


def base_kernel(class_count, rows_ref, table_ref, wide_ref, cls_ref, base_ref):
    padded = table_ref.shape[1] // class_count
    reaches = cls_ref.shape[1]
    rows = rows_ref[0]
    classes = cls_ref[0:1, :]
    pair = max(1, 256 // reaches)
    width = pair * reaches
    classes = jnp.concatenate([classes] * pair, axis=1)
    for start in range(0, base_ref.shape[2], width):
        lateral = tmm(rows, wide_ref[0, :, start : start + width])
        lateral = lateral + tmm(rows, wide_ref[1, :, start : start + width])
        base_ref[0, :, start : start + width] = convolve(
            table_ref[...], lateral.astype(BF), classes, class_count, padded
        )


def final_kernel(class_count, place_ref, inflow_ref, base_ref, table_ref, link_ref, cls_ref, *rest):
    out_ref, scratch = rest[-2:]
    padded = table_ref.shape[1] // class_count
    blocks, hours, _ = inflow_ref.shape
    members = out_ref.shape[1]
    reaches = out_ref.shape[2]
    lanes, width = link_ref.shape
    links = jnp.concatenate([link_ref[...]] * 2, axis=0)
    for block in range(blocks):
        routed = convolve(table_ref[...], inflow_ref[block], cls_ref[0:1, :], class_count, padded)
        high, low = split(routed)
        for part in range(routed.shape[1] // lanes):
            cut = slice(part * lanes, (part + 1) * lanes)
            spread = mm(jnp.concatenate([high[:, cut], low[:, cut]], axis=1), links)
            total = spread + base_ref[block, :, part * width : (part + 1) * width]
            for j in range(width // reaches):
                member = block * MB + part * (width // reaches) + j
                scratch[pl.ds(member, hours, stride=members), :] = total[
                    :, j * reaches : (j + 1) * reaches
                ]
    out_ref[...] = scratch[...].reshape(hours, members, reaches).astype(BF)


def local(
    runoff, send_rows, remap_index, remap_weight, class_id, kernel_shape, kernel_rate, outlets, incidence
):
    hours, members, grid = runoff.shape
    regions = lax.axis_size("region")
    pairs = lax.axis_size("pair")
    class_count = kernel_shape.shape[0]
    reaches, columns = remap_index.shape
    recv = send_rows.size
    slot = recv // regions
    outs = outlets.size
    half = members // 2
    blocks = half // MB
    padded = -(-hours // LANES) * LANES
    per = MB * slot
    kap = regions * per
    wide = MB * outs
    group = max(1, LANES // outs)
    core = lax.axis_index("core").astype(jnp.int32)
    core_arg = core.reshape(1)
    swap = [(0, 1), (1, 0)]

    def struct(shape, dtype):
        return jax.ShapeDtypeStruct(shape, dtype)

    send, raw = call(
        functools.partial(pack_kernel, slot),
        (struct((regions, 2, blocks * per, hours), BF), struct((32 + outs, reaches), F32)),
        2 * kap * MB * grid * hours * blocks * 2,
        limit=WHOLE_VMEM,
        in_specs=vmem(7),
        out_specs=tuple(vmem(2)),
    )(
        jnp.transpose(runoff, (1, 2, 0)),
        send_rows.reshape(1, recv),
        remap_index.T,
        remap_weight.T,
        class_id.T,
        outlets.reshape(1, outs),
        incidence.reshape(outs, reaches),
    )
    received = lax.all_to_all(
        send.reshape(regions * 2, blocks * per, hours), ("region", "core"), 0, 0
    ).reshape(regions, 2, blocks * per, hours)
    other = lax.ppermute(raw, "core", swap)
    table, mix, passing, cls_out, wide_mix, link, cls_target, cls_own = call(
        functools.partial(prep_kernel, slot, columns),
        (
            struct((hours, class_count * padded), BF),
            struct((2, 2, kap, wide), BF),
            struct((2, wide, wide), BF),
            struct((2, 8, wide), F32),
            struct((2, kap, MB * reaches), BF),
            struct((group * outs, group * reaches), BF),
            struct((8, wide), F32),
            struct((8, reaches), F32),
        ),
        10_000_000,
        in_specs=[SCALAR] + vmem(4),
        out_specs=tuple(vmem(8)),
    )(core_arg, raw, other, kernel_rate.reshape(1, class_count), kernel_shape)

    conv_flops = 2 * hours * class_count * padded * wide
    panel_shape = struct((blocks, hours, wide), BF)
    even, odd, panel, rows_own, rows_send = call(
        functools.partial(head_kernel, class_count),
        (
            struct((blocks, hours, wide), F32),
            struct((blocks, hours, wide), F32),
            panel_shape,
            struct((blocks, kap, hours), BF),
            struct((blocks, kap, hours), BF),
        ),
        3 * blocks * conv_flops,
        in_specs=[SCALAR] + vmem(5),
        out_specs=tuple(vmem(5)),
    )(core_arg, received, table, mix, passing, cls_out)

    inflow = jnp.zeros(panel_shape.shape, BF)
    own = given = None
    for step in range(pairs - 1):
        arrived = lax.ppermute(panel, "pair", [(step, step + 1)])
        inflow = arrived if step == 0 else inflow + arrived
        if step < pairs - 2:
            panel, own, given = call(
                functools.partial(hop_kernel, class_count),
                (panel_shape, panel_shape, panel_shape),
                2 * blocks * conv_flops,
                in_specs=[SCALAR] + vmem(6),
                out_specs=tuple(vmem(3)),
            )(core_arg, inflow, table, passing, cls_out, even, odd)
    if pairs == 1:
        inflow = jnp.zeros(panel_shape.shape, BF)
    rows_other = lax.ppermute(rows_send, "core", swap)

    def base(rows):
        return call(
            functools.partial(base_kernel, class_count),
            struct((blocks, hours, MB * reaches), F32),
            blocks * conv_flops * reaches // outs,
            grid=(blocks,),
            in_specs=[pl.BlockSpec((1, kap, hours), lambda b: (b, 0, 0))] + vmem(3),
            out_specs=pl.BlockSpec((1, hours, MB * reaches), lambda b: (b, 0, 0)),
        )(rows, table, wide_mix, cls_own)

    base_own = base(rows_own)
    base_other = base(rows_other)
    own, given = call(
        functools.partial(last_hop_kernel, class_count),
        (panel_shape, panel_shape),
        blocks * conv_flops,
        in_specs=[SCALAR] + vmem(5),
        out_specs=tuple(vmem(2)),
    )(core_arg, inflow, table, passing, cls_out, even)
    gotten = lax.ppermute(given, "core", swap)

    def final(place, panel_rows, base_flow, before):
        extra = [] if before is None else [before]
        return pl.pallas_call(
            functools.partial(final_kernel, class_count),
            out_shape=struct((hours, members, reaches), BF),
            grid_spec=pltpu.PrefetchScalarGridSpec(
                num_scalar_prefetch=1,
                grid=(1,),
                in_specs=vmem(5) + [pl.BlockSpec(memory_space=pl.ANY)] * len(extra),
                out_specs=pl.BlockSpec((hours, half, reaches), lambda g, place: (0, place[0], 0)),
                scratch_shapes=[pltpu.VMEM((hours * half, reaches), F32)],
            ),
            input_output_aliases={6: 0} if extra else {},
            compiler_params=pltpu.CompilerParams(vmem_limit_bytes=VMEM_LIMIT),
            cost_estimate=pl.CostEstimate(
                flops=2 * blocks * conv_flops, bytes_accessed=6_000_000, transcendentals=0
            ),
        )(place, panel_rows, base_flow, table, link, cls_target, *extra)

    out = final(core_arg, own, base_own, None)
    return final(1 - core_arg, gotten, base_other, out)


def solution(mesh):
    regions, orders = mesh.shape["region"], mesh.shape["order"]
    split_mesh = Mesh(mesh.devices.reshape(regions, orders // 2, 2), ("region", "pair", "core"))
    order = ("pair", "core")
    every = ("region", "pair", "core")
    return jax.shard_map(
        local,
        mesh=split_mesh,
        in_specs=(
            P(None, None, every),
            P("region", order, None),
            P(every, None),
            P(every, None),
            P(every, None),
            P(),
            P(),
            P("region", order, None),
            P("region", order, None, None),
        ),
        out_specs=P(None, None, every),
        check_vma=False,
    )
```

```python
import functools
import jax
import jax.numpy as jnp
from jax import lax
from jax.experimental import pallas as pl
from jax.experimental.pallas import tpu as pltpu
from jax.sharding import Mesh, PartitionSpec as P

BF = jnp.bfloat16
F32 = jnp.float32
MB = 8
SUB = 4
LANES = 128
VMEM_LIMIT = 20 * 1024 * 1024
SEND_VMEM = 53760 * 1024


def iota(shape, dim):
    return lax.broadcasted_iota(jnp.int32, shape, dim)


def mm(a, b):
    return jnp.dot(a, b, preferred_element_type=F32)


def tmm(a, b):
    return lax.dot_general(a, b, (((0,), (0,)), ((), ())), preferred_element_type=F32)


def one_hot(condition):
    return jnp.where(condition, 1.0, 0.0).astype(BF)


def split(value):
    high = value.astype(BF)
    return high, (value - high.astype(F32)).astype(BF)


def call(kernel, out_shape, flops, limit=VMEM_LIMIT, **extra):
    nbytes = sum(s.size * s.dtype.itemsize for s in jax.tree.leaves(out_shape))
    return pl.pallas_call(
        kernel,
        out_shape=out_shape,
        compiler_params=pltpu.CompilerParams(vmem_limit_bytes=limit),
        cost_estimate=pl.CostEstimate(flops=flops, bytes_accessed=2 * nbytes, transcendentals=0),
        **extra,
    )


def vmem(count):
    return [pl.BlockSpec(memory_space=pltpu.VMEM)] * count


SCALAR = pl.BlockSpec(memory_space=pltpu.SMEM)


def convolve(table, value, classes, class_count):
    hours = table.shape[0]
    masks = [one_hot(classes == float(k)) for k in range(class_count)]
    total = None
    for start in range(0, hours, LANES):
        block = value[start : start + LANES]
        short = LANES - block.shape[0]
        if short:
            block = jnp.concatenate([block, jnp.zeros((short, block.shape[1]), BF)], axis=0)
        parts = jnp.concatenate([block * mask for mask in masks], axis=0)
        added = mm(table[: hours - start], parts)
        if start == 0:
            total = added
        else:
            total = jnp.concatenate([total[:start], total[start:] + added], axis=0)
    return total


def pack_kernel(slot, x_ref, rows_ref, send_ref):
    members, grid, hours = x_ref.shape
    blocks = members // MB
    regions = send_ref.shape[0]
    per = MB * slot
    count = regions * per
    recv = rows_ref.shape[1]
    row = iota((count, recv), 0)
    wanted = (row // per) * slot + row % slot
    rows = rows_ref[...].astype(F32)
    chosen = jnp.sum(jnp.where(iota((count, recv), 1) == wanted, rows, 0.0), axis=1, keepdims=True)
    lane = iota((count, MB * grid), 1)
    member = (iota((count, MB * grid), 0) // slot) % MB
    select = one_hot((lane // grid == member) & ((lane % grid).astype(F32) == chosen))
    for block in range(blocks):
        x = x_ref[block * MB : (block + 1) * MB].reshape(MB * grid, hours).astype(BF)
        y = mm(select, x).astype(BF).reshape(regions, per, hours)
        core, inner = divmod(block, blocks // 2)
        send_ref[:, core, inner * per : (inner + 1) * per, :] = y


def raw_kernel(idx_ref, w_ref, cls_ref, outl_ref, inc_ref, raw_ref):
    raw_ref[...] = jnp.zeros_like(raw_ref)
    raw_ref[0 : idx_ref.shape[0], :] = idx_ref[...].astype(F32)
    raw_ref[8 : 8 + w_ref.shape[0], :] = w_ref[...]
    raw_ref[16:17, :] = cls_ref[...].astype(F32)
    raw_ref[24:25, 0 : outl_ref.shape[1]] = outl_ref[...].astype(F32)
    raw_ref[32:, :] = inc_ref[...].astype(F32)


def prep_kernel(
    slot, columns, core_ref, own_ref, other_ref, rate_ref, shape_ref,
    table_ref, mix_ref, pass_ref, cls_out_ref, wide_ref, link_ref, cls_target_ref, cls_own_ref,
):
    core = core_ref[0]
    class_count, hours = shape_ref.shape
    padded = -(-hours // LANES) * LANES
    kap = mix_ref.shape[1] // 2
    recv = kap // SUB
    per = SUB * slot
    outs = own_ref.shape[0] - 32
    reaches = own_ref.shape[1]
    wide = MB * outs
    narrow = SUB * outs

    lag = iota((class_count, hours), 1).astype(F32)
    square = (class_count, class_count)
    rate = jnp.where(iota(square, 0) == iota(square, 1), rate_ref[...], 0.0)
    rate = jnp.sum(rate, axis=1, keepdims=True)
    hydro = (rate * shape_ref[...] * jnp.exp(-rate * lag)).astype(BF)
    reverse = one_hot((iota((hours, padded), 0) + iota((hours, padded), 1)) % padded == 0)
    turned = mm(hydro, reverse)
    later = iota((padded, LANES), 1) <= iota((padded, LANES), 0)
    for k in range(class_count):
        rolled = pltpu.roll(
            jnp.broadcast_to(turned[k : k + 1, :], (padded, padded)), 0, 1, stride=1, stride_axis=0
        )
        rolled = jnp.where(later, rolled[:, :LANES], 0.0)
        table_ref[:, k * LANES : (k + 1) * LANES] = rolled[:hours].astype(BF)

    row_p = iota((kap, recv), 0)
    expand = one_hot((row_p // per) * slot + row_p % slot == iota((kap, recv), 1))

    def owner(width):
        return (iota((kap, width), 0) // slot) % SUB

    def tile(width):
        return one_hot(iota((outs, width), 0) == iota((outs, width), 1) % outs)

    def weights(raw):
        total = jnp.zeros((recv, reaches), F32)
        for j in range(columns):
            hit = iota((recv, reaches), 0).astype(F32) == raw[j : j + 1, :]
            total = total + jnp.where(hit, raw[8 + j : 9 + j, :], 0.0)
        return split(total)

    own = own_ref[...]
    for level in range(2):
        raw = jnp.where(core == level, own, other_ref[...])
        lanes = mm(raw[24:32, :outs].astype(BF), tile(wide))[0:1, :]
        pick = one_hot(iota((reaches, wide), 0).astype(F32) == lanes)
        for part, weight in enumerate(weights(raw)):
            spread = mm(expand, mm(weight, pick[:, :narrow]).astype(BF))
            spread = jnp.where(owner(narrow) == iota((kap, narrow), 1) // outs, spread, 0.0)
            mix_ref[level, part * kap : (part + 1) * kap] = spread.astype(BF)
        moved = jnp.concatenate([mm(raw[32:, :].astype(BF), pick)] * MB, axis=0)
        here = iota((wide, wide), 0) // outs == iota((wide, wide), 1) // outs
        pass_ref[level] = jnp.where(here, moved, 0.0).astype(BF)
        cls_out_ref[level] = mm(raw[16:24, :].astype(BF), pick)

    for part, weight in enumerate(weights(own)):
        spread = mm(expand, weight)
        for m in range(SUB):
            piece = jnp.where(owner(reaches) == m, spread, 0.0).astype(BF)
            wide_ref[part * kap : (part + 1) * kap, m * reaches : (m + 1) * reaches] = piece
    cls_own_ref[...] = own[16:24, :]
    cls_target_ref[...] = lax.dot_general(
        own[16:24, :].astype(BF),
        jnp.concatenate([own[32:, :]] * MB, axis=0).astype(BF),
        (((1,), (1,)), ((), ())),
        preferred_element_type=F32,
    )
    stacked = jnp.concatenate([own[32:, :]] * SUB, axis=0)
    who = iota((narrow, reaches), 0) // outs
    for m in range(SUB):
        piece = jnp.where(who == m, stacked, 0.0).astype(BF)
        for part in range(2):
            link_ref[part * narrow : (part + 1) * narrow, m * reaches : (m + 1) * reaches] = piece


def twice(rows_ref, sub, size):
    rows = rows_ref[:, sub * size : (sub + 1) * size, :]
    rows = rows.reshape(rows.shape[0] * size, rows.shape[2])
    return jnp.concatenate([rows, rows], axis=0)


def pass_on(panel, pass_matrix):
    width = pass_matrix.shape[0]
    parts = [
        mm(panel[:, start : start + width], pass_matrix).astype(BF)
        for start in range(0, panel.shape[1], width)
    ]
    return jnp.concatenate(parts, axis=1)


def tiled(classes, width):
    return jnp.concatenate([classes] * (width // classes.shape[1]), axis=1)


def head_kernel(
    class_count, core_ref, rows_ref, table_ref, mix_ref, pass_ref, cls_ref,
    even_ref, odd_ref, panel_ref, own_ref, send_ref,
):
    first = core_ref[0] == 0
    rows = [rows_ref[:, level] for level in range(2)]
    own_ref[...] = jnp.where(first, rows[0], rows[1])
    send_ref[...] = jnp.where(first, rows[1], rows[0])
    regions, _, total, _ = rows_ref.shape
    size = mix_ref.shape[1] // 2 // regions
    wide = even_ref.shape[1]
    lateral = [
        jnp.concatenate(
            [
                tmm(twice(rows_ref.at[:, level], sub, size), mix_ref[level])
                for sub in range(total // size)
            ],
            axis=1,
        )
        for level in range(2)
    ]
    classes = [tiled(cls_ref[level, 0:1, :], wide) for level in range(2)]
    even = convolve(table_ref[...], lateral[0].astype(BF), classes[0], class_count)
    even_ref[...] = even
    odd_ref[...] = lateral[1]
    inflow = lateral[1] + pass_on(even.astype(BF), pass_ref[1]).astype(F32)
    panel_ref[...] = convolve(table_ref[...], inflow.astype(BF), classes[1], class_count).astype(BF)


def hop_kernel(class_count, inflow_ref, table_ref, pass_ref, cls_ref, even_ref, odd_ref, panel_ref):
    classes = [tiled(cls_ref[level, 0:1, :], even_ref.shape[1]) for level in range(2)]
    moved = pass_on(inflow_ref[...], pass_ref[0])
    even = even_ref[...] + convolve(table_ref[...], moved, classes[0], class_count)
    moved = odd_ref[...] + pass_on(even.astype(BF), pass_ref[1]).astype(F32)
    panel_ref[...] = convolve(table_ref[...], moved.astype(BF), classes[1], class_count).astype(BF)


def last_hop_kernel(class_count, core_ref, inflow_ref, table_ref, pass_ref, cls_ref, even_ref, *rest):
    own_ref, send_ref = rest[-2:]
    arrived = inflow_ref[...]
    classes = tiled(cls_ref[0, 0:1, :], even_ref.shape[1])
    moved = pass_on(arrived, pass_ref[0])
    even = even_ref[...] + convolve(table_ref[...], moved, classes, class_count)
    even = even.astype(BF)
    first = core_ref[0] == 0
    own_ref[...] = jnp.where(first, arrived, even)
    send_ref[...] = jnp.where(first, even, arrived)


def base_kernel(class_count, rows_ref, table_ref, wide_ref, cls_ref, base_ref):
    regions, total, _ = rows_ref.shape
    size = wide_ref.shape[0] // 2 // regions
    width = wide_ref.shape[1]
    classes = tiled(cls_ref[0:1, :], width)
    for sub in range(total // size):
        lateral = tmm(twice(rows_ref, sub, size), wide_ref[...]).astype(BF)
        base_ref[:, sub * width : (sub + 1) * width] = convolve(
            table_ref[...], lateral, classes, class_count
        )


def final_kernel(class_count, place_ref, inflow_ref, base_ref, table_ref, link_ref, cls_ref, *rest):
    out_ref, scratch = rest[-2:]
    hours, members, reaches = out_ref.shape
    lanes, width = link_ref.shape[0] // 2, link_ref.shape[1]
    classes = tiled(cls_ref[0:1, :], inflow_ref.shape[1])
    routed = convolve(table_ref[...], inflow_ref[...], classes, class_count)
    high, low = split(routed)
    for part in range(routed.shape[1] // lanes):
        cut = slice(part * lanes, (part + 1) * lanes)
        spread = mm(jnp.concatenate([high[:, cut], low[:, cut]], axis=1), link_ref[...])
        total = spread + base_ref[:, part * width : (part + 1) * width]
        for j in range(width // reaches):
            member = part * (width // reaches) + j
            scratch[pl.ds(member, hours, stride=members), :] = total[
                :, j * reaches : (j + 1) * reaches
            ]
    out_ref[...] = scratch[...].reshape(hours, members, reaches).astype(BF)


def local(
    runoff, send_rows, remap_index, remap_weight, class_id, kernel_shape, kernel_rate, outlets, incidence
):
    hours, members, grid = runoff.shape
    regions = lax.axis_size("region")
    pairs = lax.axis_size("pair")
    class_count = kernel_shape.shape[0]
    reaches, columns = remap_index.shape
    recv = send_rows.size
    slot = recv // regions
    outs = outlets.size
    half = members // 2
    kap = recv * SUB
    wide = half * outs
    core = lax.axis_index("core").astype(jnp.int32)
    core_arg = core.reshape(1)
    swap = [(0, 1), (1, 0)]
    anywhere = pl.BlockSpec(memory_space=pl.ANY)
    conv_flops = 2 * hours * class_count * hours * wide

    def struct(shape, dtype):
        return jax.ShapeDtypeStruct(shape, dtype)

    send = call(
        functools.partial(pack_kernel, slot),
        struct((regions, 2, half * slot, hours), BF),
        2 * recv * MB * grid * hours * members,
        limit=SEND_VMEM,
        in_specs=vmem(2),
        out_specs=vmem(1)[0],
    )(jnp.transpose(runoff, (1, 2, 0)), send_rows.reshape(1, recv))
    received = lax.all_to_all(
        send.reshape(regions * 2, half * slot, hours), ("region", "core"), 0, 0
    ).reshape(regions, 2, half * slot, hours)
    raw = call(
        raw_kernel,
        struct((32 + outs, reaches), F32),
        1000,
        limit=SEND_VMEM,
        in_specs=vmem(5),
        out_specs=vmem(1)[0],
    )(
        remap_index.T,
        remap_weight.T,
        class_id.T,
        outlets.reshape(1, outs),
        incidence.reshape(outs, reaches),
    )
    other = lax.ppermute(raw, "core", swap)
    table, mix, passing, cls_out, wide_mix, link, cls_target, cls_own = call(
        functools.partial(prep_kernel, slot, columns),
        (
            struct((hours, class_count * LANES), BF),
            struct((2, 2 * kap, SUB * outs), BF),
            struct((2, MB * outs, MB * outs), BF),
            struct((2, 8, MB * outs), F32),
            struct((2 * kap, SUB * reaches), BF),
            struct((2 * SUB * outs, SUB * reaches), BF),
            struct((8, MB * outs), F32),
            struct((8, reaches), F32),
        ),
        10_000_000,
        in_specs=[SCALAR] + vmem(4),
        out_specs=tuple(vmem(8)),
    )(core_arg, raw, other, kernel_rate.reshape(1, class_count), kernel_shape)

    panel_shape = struct((hours, wide), BF)
    rows_shape = struct((regions, half * slot, hours), BF)
    even, odd, panel, rows_own, rows_send = call(
        functools.partial(head_kernel, class_count),
        (struct((hours, wide), F32), struct((hours, wide), F32), panel_shape, rows_shape, rows_shape),
        2 * conv_flops,
        in_specs=[SCALAR] + vmem(5),
        out_specs=tuple(vmem(5)),
    )(core_arg, received, table, mix, passing, cls_out)

    inflow = jnp.zeros(panel_shape.shape, BF)
    for step in range(pairs - 1):
        arrived = lax.ppermute(panel, "pair", [(step, step + 1)])
        inflow = arrived if step == 0 else inflow + arrived
        if step < pairs - 2:
            panel = call(
                functools.partial(hop_kernel, class_count),
                panel_shape,
                2 * conv_flops,
                in_specs=vmem(6),
                out_specs=vmem(1)[0],
            )(inflow, table, passing, cls_out, even, odd)
    rows_other = lax.ppermute(rows_send, "core", swap)

    def base(rows):
        return call(
            functools.partial(base_kernel, class_count),
            struct((hours, half * reaches), F32),
            conv_flops * reaches // outs,
            in_specs=vmem(4),
            out_specs=vmem(1)[0],
        )(rows, table, wide_mix, cls_own)

    base_own = base(rows_own)
    base_other = base(rows_other)
    own, given = call(
        functools.partial(last_hop_kernel, class_count),
        (panel_shape, panel_shape),
        conv_flops,
        in_specs=[SCALAR] + vmem(5) + [anywhere] * 2,
        out_specs=tuple(vmem(2)),
    )(core_arg, inflow, table, passing, cls_out, even, base_own, base_other)
    gotten = lax.ppermute(given, "core", swap)

    def final(place, panel_rows, base_flow, before):
        extra = [] if before is None else [before]
        return call(
            functools.partial(final_kernel, class_count),
            struct((hours, members, reaches), BF),
            2 * conv_flops,
            grid_spec=pltpu.PrefetchScalarGridSpec(
                num_scalar_prefetch=1,
                grid=(1,),
                in_specs=vmem(5) + [anywhere] * len(extra),
                out_specs=pl.BlockSpec((hours, half, reaches), lambda g, place: (0, place[0], 0)),
                scratch_shapes=[pltpu.VMEM((hours * half, reaches), F32)],
            ),
            input_output_aliases={6: 0} if extra else {},
        )(place, panel_rows, base_flow, table, link, cls_target, *extra)

    out = final(core_arg, own, base_own, None)
    return final(1 - core_arg, gotten, base_other, out)


def solution(mesh):
    regions, orders = mesh.shape["region"], mesh.shape["order"]
    split_mesh = Mesh(mesh.devices.reshape(regions, orders // 2, 2), ("region", "pair", "core"))
    order = ("pair", "core")
    every = ("region", "pair", "core")
    return jax.shard_map(
        local,
        mesh=split_mesh,
        in_specs=(
            P(None, None, every),
            P("region", order, None),
            P(every, None),
            P(every, None),
            P(every, None),
            P(),
            P(),
            P("region", order, None),
            P("region", order, None, None),
        ),
        out_specs=P(None, None, every),
        check_vma=False,
    )
```

```python
import functools
import jax
import jax.numpy as jnp
from jax import lax
from jax.experimental import pallas as pl
from jax.experimental.pallas import tpu as pltpu
from jax.sharding import Mesh, PartitionSpec as P

BF = jnp.bfloat16
F32 = jnp.float32
MB = 8
SUB = 4
LANES = 128
VMEM_LIMIT = 20 * 1024 * 1024
FULL_VMEM = 56 * 1024 * 1024


def iota(shape, dim):
    return lax.broadcasted_iota(jnp.int32, shape, dim)


def mm(a, b):
    return jnp.dot(a, b, preferred_element_type=F32)


def tmm(a, b):
    return lax.dot_general(a, b, (((0,), (0,)), ((), ())), preferred_element_type=F32)


def one_hot(condition):
    return jnp.where(condition, 1.0, 0.0).astype(BF)


def split(value):
    high = value.astype(BF)
    return high, (value - high.astype(F32)).astype(BF)


def call(kernel, out_shape, flops, limit=VMEM_LIMIT, **extra):
    nbytes = sum(s.size * s.dtype.itemsize for s in jax.tree.leaves(out_shape))
    return pl.pallas_call(
        kernel,
        out_shape=out_shape,
        compiler_params=pltpu.CompilerParams(vmem_limit_bytes=limit),
        cost_estimate=pl.CostEstimate(flops=flops, bytes_accessed=2 * nbytes, transcendentals=0),
        **extra,
    )


def vmem(count):
    return [pl.BlockSpec(memory_space=pltpu.VMEM)] * count


SCALAR = pl.BlockSpec(memory_space=pltpu.SMEM)


def convolve(table, value, classes, class_count):
    hours = table.shape[0]
    masks = [one_hot(classes == float(k)) for k in range(class_count)]
    total = None
    for start in range(0, hours, LANES):
        block = value[start : start + LANES]
        short = LANES - block.shape[0]
        if short:
            block = jnp.concatenate([block, jnp.zeros((short, block.shape[1]), BF)], axis=0)
        parts = jnp.concatenate([block * mask for mask in masks], axis=0)
        added = mm(table[: hours - start], parts)
        if start == 0:
            total = added
        else:
            total = jnp.concatenate([total[:start], total[start:] + added], axis=0)
    return total


def pack_kernel(slot, x_ref, rows_ref, send_ref, held, rows_held, ready, arrived, sent):
    members, grid, hours = x_ref.shape
    blocks = members // MB
    regions = send_ref.shape[0]
    per = MB * slot

    half = members // 2

    def fetch(core):
        place = pl.ds(core * half, half)
        return pltpu.make_async_copy(x_ref.at[place], held.at[place], arrived.at[core])

    def deliver(core):
        return pltpu.make_async_copy(ready.at[:, core], send_ref.at[:, core], sent.at[core])

    first = pltpu.make_async_copy(rows_ref, rows_held, arrived.at[2])
    first.start()
    for core in range(2):
        fetch(core).start()
    first.wait()
    count = regions * per
    recv = rows_ref.shape[1]
    row = iota((count, recv), 0)
    wanted = (row // per) * slot + row % slot
    rows = rows_held[...].astype(F32)
    chosen = jnp.sum(jnp.where(iota((count, recv), 1) == wanted, rows, 0.0), axis=1, keepdims=True)
    lane = iota((count, MB * grid), 1)
    member = (iota((count, MB * grid), 0) // slot) % MB
    select = one_hot((lane // grid == member) & ((lane % grid).astype(F32) == chosen))
    for core in range(2):
        fetch(core).wait()
        for inner in range(blocks // 2):
            begin = core * half + inner * MB
            x = held[begin : begin + MB].reshape(MB * grid, hours).astype(BF)
            y = mm(select, x).astype(BF).reshape(regions, per, hours)
            ready[:, core, inner * per : (inner + 1) * per, :] = y
        deliver(core).start()
    for core in range(2):
        deliver(core).wait()


def raw_kernel(idx_ref, w_ref, cls_ref, outl_ref, inc_ref, raw_ref):
    raw_ref[...] = jnp.zeros_like(raw_ref)
    raw_ref[0 : idx_ref.shape[0], :] = idx_ref[...].astype(F32)
    raw_ref[8 : 8 + w_ref.shape[0], :] = w_ref[...]
    raw_ref[16:17, :] = cls_ref[...].astype(F32)
    raw_ref[24:25, 0 : outl_ref.shape[1]] = outl_ref[...].astype(F32)
    raw_ref[32:, :] = inc_ref[...].astype(F32)


def prep_kernel(
    slot, columns, core_ref, own_ref, other_ref, rate_ref, shape_ref,
    table_ref, mix_ref, pass_ref, cls_out_ref, wide_ref, link_ref, cls_target_ref, cls_own_ref,
):
    core = core_ref[0]
    class_count, hours = shape_ref.shape
    padded = -(-hours // LANES) * LANES
    kap = mix_ref.shape[1] // 2
    recv = kap // SUB
    per = SUB * slot
    outs = own_ref.shape[0] - 32
    reaches = own_ref.shape[1]
    wide = MB * outs
    narrow = SUB * outs

    lag = iota((class_count, hours), 1).astype(F32)
    square = (class_count, class_count)
    rate = jnp.where(iota(square, 0) == iota(square, 1), rate_ref[...], 0.0)
    rate = jnp.sum(rate, axis=1, keepdims=True)
    hydro = (rate * shape_ref[...] * jnp.exp(-rate * lag)).astype(BF)
    reverse = one_hot((iota((hours, padded), 0) + iota((hours, padded), 1)) % padded == 0)
    turned = mm(hydro, reverse)
    later = iota((padded, LANES), 1) <= iota((padded, LANES), 0)
    for k in range(class_count):
        rolled = pltpu.roll(
            jnp.broadcast_to(turned[k : k + 1, :], (padded, padded)), 0, 1, stride=1, stride_axis=0
        )
        rolled = jnp.where(later, rolled[:, :LANES], 0.0)
        table_ref[:, k * LANES : (k + 1) * LANES] = rolled[:hours].astype(BF)

    row_p = iota((kap, recv), 0)
    expand = one_hot((row_p // per) * slot + row_p % slot == iota((kap, recv), 1))

    def owner(width):
        return (iota((kap, width), 0) // slot) % SUB

    def tile(width):
        return one_hot(iota((outs, width), 0) == iota((outs, width), 1) % outs)

    def weights(raw):
        total = jnp.zeros((recv, reaches), F32)
        for j in range(columns):
            hit = iota((recv, reaches), 0).astype(F32) == raw[j : j + 1, :]
            total = total + jnp.where(hit, raw[8 + j : 9 + j, :], 0.0)
        return split(total)

    own = own_ref[...]
    for level in range(2):
        raw = jnp.where(core == level, own, other_ref[...])
        lanes = mm(raw[24:32, :outs].astype(BF), tile(wide))[0:1, :]
        pick = one_hot(iota((reaches, wide), 0).astype(F32) == lanes)
        for part, weight in enumerate(weights(raw)):
            spread = mm(expand, mm(weight, pick[:, :narrow]).astype(BF))
            spread = jnp.where(owner(narrow) == iota((kap, narrow), 1) // outs, spread, 0.0)
            mix_ref[level, part * kap : (part + 1) * kap] = spread.astype(BF)
        moved = jnp.concatenate([mm(raw[32:, :].astype(BF), pick)] * MB, axis=0)
        here = iota((wide, wide), 0) // outs == iota((wide, wide), 1) // outs
        pass_ref[level] = jnp.where(here, moved, 0.0).astype(BF)
        cls_out_ref[level] = mm(raw[16:24, :].astype(BF), pick)

    for part, weight in enumerate(weights(own)):
        spread = mm(expand, weight)
        for m in range(SUB):
            piece = jnp.where(owner(reaches) == m, spread, 0.0).astype(BF)
            wide_ref[part * kap : (part + 1) * kap, m * reaches : (m + 1) * reaches] = piece
    cls_own_ref[...] = own[16:24, :]
    cls_target_ref[...] = lax.dot_general(
        own[16:24, :].astype(BF),
        jnp.concatenate([own[32:, :]] * MB, axis=0).astype(BF),
        (((1,), (1,)), ((), ())),
        preferred_element_type=F32,
    )
    stacked = jnp.concatenate([own[32:, :]] * SUB, axis=0)
    who = iota((narrow, reaches), 0) // outs
    for m in range(SUB):
        piece = jnp.where(who == m, stacked, 0.0).astype(BF)
        for part in range(2):
            link_ref[part * narrow : (part + 1) * narrow, m * reaches : (m + 1) * reaches] = piece


def twice(rows_ref, sub, size):
    rows = rows_ref[:, sub * size : (sub + 1) * size, :]
    rows = rows.reshape(rows.shape[0] * size, rows.shape[2])
    return jnp.concatenate([rows, rows], axis=0)


def pass_on(panel, pass_matrix):
    width = pass_matrix.shape[0]
    parts = [
        mm(panel[:, start : start + width], pass_matrix).astype(BF)
        for start in range(0, panel.shape[1], width)
    ]
    return jnp.concatenate(parts, axis=1)


def tiled(classes, width):
    return jnp.concatenate([classes] * (width // classes.shape[1]), axis=1)


def head_kernel(
    class_count, core_ref, rows_ref, table_ref, mix_ref, pass_ref, cls_ref,
    even_ref, odd_ref, panel_ref, own_ref, send_ref,
):
    first = core_ref[0] == 0
    rows = [rows_ref[:, level] for level in range(2)]
    own_ref[...] = jnp.where(first, rows[0], rows[1])
    send_ref[...] = jnp.where(first, rows[1], rows[0])
    regions, _, total, _ = rows_ref.shape
    size = mix_ref.shape[1] // 2 // regions
    wide = even_ref.shape[1]
    lateral = [
        jnp.concatenate(
            [
                tmm(twice(rows_ref.at[:, level], sub, size), mix_ref[level])
                for sub in range(total // size)
            ],
            axis=1,
        )
        for level in range(2)
    ]
    classes = [tiled(cls_ref[level, 0:1, :], wide) for level in range(2)]
    even = convolve(table_ref[...], lateral[0].astype(BF), classes[0], class_count)
    even_ref[...] = even
    odd_ref[...] = lateral[1]
    inflow = lateral[1] + pass_on(even.astype(BF), pass_ref[1]).astype(F32)
    panel_ref[...] = convolve(table_ref[...], inflow.astype(BF), classes[1], class_count).astype(BF)


def hop_kernel(class_count, inflow_ref, table_ref, pass_ref, cls_ref, even_ref, odd_ref, panel_ref):
    classes = [tiled(cls_ref[level, 0:1, :], even_ref.shape[1]) for level in range(2)]
    moved = pass_on(inflow_ref[...], pass_ref[0])
    even = even_ref[...] + convolve(table_ref[...], moved, classes[0], class_count)
    moved = odd_ref[...] + pass_on(even.astype(BF), pass_ref[1]).astype(F32)
    panel_ref[...] = convolve(table_ref[...], moved.astype(BF), classes[1], class_count).astype(BF)


def last_hop_kernel(class_count, core_ref, valid_ref, inflow_ref, table_ref, pass_ref, cls_ref, even_ref, *rest):
    own_ref, send_ref = rest[-2:]
    arrived = jnp.where(valid_ref[0] == 1, inflow_ref[...], jnp.zeros((), BF))
    classes = tiled(cls_ref[0, 0:1, :], even_ref.shape[1])
    moved = pass_on(arrived, pass_ref[0])
    even = even_ref[...] + convolve(table_ref[...], moved, classes, class_count)
    even = even.astype(BF)
    first = core_ref[0] == 0
    own_ref[...] = jnp.where(first, arrived, even)
    send_ref[...] = jnp.where(first, even, arrived)


def base_kernel(class_count, rows_ref, table_ref, wide_ref, cls_ref, base_ref):
    regions, total, _ = rows_ref.shape
    size = wide_ref.shape[0] // 2 // regions
    width = wide_ref.shape[1]
    classes = tiled(cls_ref[0:1, :], width)
    for sub in range(total // size):
        lateral = tmm(twice(rows_ref, sub, size), wide_ref[...]).astype(BF)
        base_ref[:, sub * width : (sub + 1) * width] = convolve(
            table_ref[...], lateral, classes, class_count
        )


def routed_parts(class_count, inflow_ref, table_ref, cls_ref):
    classes = tiled(cls_ref[0:1, :], inflow_ref.shape[1])
    return split(convolve(table_ref[...], inflow_ref[...], classes, class_count))


def assemble(hours, high, low, base_ref, link_ref, scratch, members, reaches):
    lanes, width = link_ref.shape[0] // 2, link_ref.shape[1]
    count = hours.stop - hours.start
    for part in range(high.shape[1] // lanes):
        cut = slice(part * lanes, (part + 1) * lanes)
        both = jnp.concatenate([high[hours, cut], low[hours, cut]], axis=1)
        total = mm(both, link_ref[...]) + base_ref[hours, part * width : (part + 1) * width]
        for j in range(width // reaches):
            member = part * (width // reaches) + j
            scratch[pl.ds(hours.start * members + member, count, stride=members), :] = total[
                :, j * reaches : (j + 1) * reaches
            ]
    flow = scratch[hours.start * members : hours.stop * members, :]
    return flow.reshape(count, members, reaches).astype(BF)


def early_kernel(class_count, inflow_ref, base_ref, table_ref, link_ref, cls_ref, out_ref, scratch):
    hours, members, reaches = out_ref.shape
    high, low = routed_parts(class_count, inflow_ref, table_ref, cls_ref)
    out_ref[...] = assemble(
        slice(0, hours), high, low, base_ref, link_ref, scratch, members, reaches
    )


def late_kernel(
    class_count, core_ref, done_ref, inflow_ref, base_ref, table_ref, link_ref, cls_ref,
    out_ref, scratch, ready, sems,
):
    hours, members, reaches = done_ref.shape
    core = core_ref[0]

    def place(which):
        return pl.ds(pl.multiple_of(which * members, members), members)

    copies = [pltpu.make_async_copy(done_ref, out_ref.at[:, place(core)], sems.at[0])]
    copies[0].start()
    high, low = routed_parts(class_count, inflow_ref, table_ref, cls_ref)
    for start in range(0, hours, LANES):
        part = slice(start, min(start + LANES, hours))
        ready[part] = assemble(part, high, low, base_ref, link_ref, scratch, members, reaches)
        span = pl.ds(start, part.stop - start)
        copies.append(
            pltpu.make_async_copy(
                ready.at[span], out_ref.at[span, place(1 - core)], sems.at[len(copies)]
            )
        )
        copies[-1].start()
    for copy in copies:
        copy.wait()


def local(
    runoff, send_rows, remap_index, remap_weight, class_id, kernel_shape, kernel_rate, outlets, incidence
):
    hours, members, grid = runoff.shape
    regions = lax.axis_size("region")
    pairs = lax.axis_size("pair")
    class_count = kernel_shape.shape[0]
    reaches, columns = remap_index.shape
    recv = send_rows.size
    slot = recv // regions
    outs = outlets.size
    half = members // 2
    kap = recv * SUB
    wide = half * outs
    core = lax.axis_index("core").astype(jnp.int32)
    core_arg = core.reshape(1)
    pair = lax.axis_index("pair")
    valid = (pair > 0).astype(jnp.int32).reshape(1)
    swap = [(0, 1), (1, 0)]
    anywhere = pl.BlockSpec(memory_space=pl.ANY)
    conv_flops = 2 * hours * class_count * hours * wide

    def struct(shape, dtype):
        return jax.ShapeDtypeStruct(shape, dtype)

    send = call(
        functools.partial(pack_kernel, slot),
        struct((regions, 2, half * slot, hours), BF),
        2 * recv * MB * grid * hours * members,
        limit=FULL_VMEM,
        in_specs=[anywhere] * 2,
        out_specs=anywhere,
        scratch_shapes=[
            pltpu.VMEM((members, grid, hours), F32),
            pltpu.VMEM((1, recv), jnp.int32),
            pltpu.VMEM((regions, 2, half * slot, hours), BF),
            pltpu.SemaphoreType.DMA((3,)),
            pltpu.SemaphoreType.DMA((2,)),
        ],
    )(jnp.transpose(runoff, (1, 2, 0)), send_rows.reshape(1, recv))
    received = lax.all_to_all(
        send.reshape(regions * 2, half * slot, hours), ("region", "core"), 0, 0
    ).reshape(regions, 2, half * slot, hours)
    raw = call(
        raw_kernel,
        struct((32 + outs, reaches), F32),
        1000,
        in_specs=vmem(5),
        out_specs=vmem(1)[0],
    )(
        remap_index.T,
        remap_weight.T,
        class_id.T,
        outlets.reshape(1, outs),
        incidence.reshape(outs, reaches),
    )
    other = lax.ppermute(raw, "core", swap)
    table, mix, passing, cls_out, wide_mix, link, cls_target, cls_own = call(
        functools.partial(prep_kernel, slot, columns),
        (
            struct((hours, class_count * LANES), BF),
            struct((2, 2 * kap, SUB * outs), BF),
            struct((2, MB * outs, MB * outs), BF),
            struct((2, 8, MB * outs), F32),
            struct((2 * kap, SUB * reaches), BF),
            struct((2 * SUB * outs, SUB * reaches), BF),
            struct((8, MB * outs), F32),
            struct((8, reaches), F32),
        ),
        10_000_000,
        in_specs=[SCALAR] + vmem(4),
        out_specs=tuple(vmem(8)),
    )(core_arg, raw, other, kernel_rate.reshape(1, class_count), kernel_shape)

    panel_shape = struct((hours, wide), BF)
    rows_shape = struct((regions, half * slot, hours), BF)
    even, odd, panel, rows_own, rows_send = call(
        functools.partial(head_kernel, class_count),
        (struct((hours, wide), F32), struct((hours, wide), F32), panel_shape, rows_shape, rows_shape),
        2 * conv_flops,
        in_specs=[SCALAR] + vmem(5),
        out_specs=tuple(vmem(5)),
    )(core_arg, received, table, mix, passing, cls_out)

    inflow = jnp.zeros(panel_shape.shape, BF)
    for step in range(pairs - 1):
        arrived = lax.ppermute(panel, "pair", [(step, step + 1), (step + 1, step)])
        if pairs == 2:
            inflow = arrived
        else:
            inflow = jnp.where(pair == step + 1, arrived, inflow)
        if step < pairs - 2:
            panel = call(
                functools.partial(hop_kernel, class_count),
                panel_shape,
                2 * conv_flops,
                in_specs=vmem(6),
                out_specs=vmem(1)[0],
            )(inflow, table, passing, cls_out, even, odd)
    rows_other = lax.ppermute(rows_send, "core", swap)

    def base(rows):
        return call(
            functools.partial(base_kernel, class_count),
            struct((hours, half * reaches), F32),
            conv_flops * reaches // outs,
            in_specs=vmem(4),
            out_specs=vmem(1)[0],
        )(rows, table, wide_mix, cls_own)

    base_own = base(rows_own)
    base_other = base(rows_other)
    own, given = call(
        functools.partial(last_hop_kernel, class_count),
        (panel_shape, panel_shape),
        conv_flops,
        in_specs=[SCALAR] * 2 + vmem(5) + [anywhere] * 2,
        out_specs=tuple(vmem(2)),
    )(core_arg, valid, inflow, table, passing, cls_out, even, base_own, base_other)
    gotten = lax.ppermute(given, "core", swap)

    flow_shape = struct((hours, half, reaches), BF)
    flat = pltpu.VMEM((hours * half, reaches), F32)
    done = call(
        functools.partial(early_kernel, class_count),
        flow_shape,
        2 * conv_flops,
        in_specs=vmem(5),
        out_specs=vmem(1)[0],
        scratch_shapes=[flat],
    )(own, base_own, table, link, cls_target)
    return call(
        functools.partial(late_kernel, class_count),
        struct((hours, members, reaches), BF),
        2 * conv_flops,
        in_specs=[SCALAR] + vmem(6),
        out_specs=anywhere,
        scratch_shapes=[
            flat,
            pltpu.VMEM((hours, half, reaches), BF),
            pltpu.SemaphoreType.DMA((1 + -(-hours // LANES),)),
        ],
    )(core_arg, done, gotten, base_other, table, link, cls_target)


def solution(mesh):
    regions, orders = mesh.shape["region"], mesh.shape["order"]
    split_mesh = Mesh(mesh.devices.reshape(regions, orders // 2, 2), ("region", "pair", "core"))
    order = ("pair", "core")
    every = ("region", "pair", "core")
    return jax.shard_map(
        local,
        mesh=split_mesh,
        in_specs=(
            P(None, None, every),
            P("region", order, None),
            P(every, None),
            P(every, None),
            P(every, None),
            P(),
            P(),
            P("region", order, None),
            P("region", order, None, None),
        ),
        out_specs=P(None, None, every),
        check_vma=False,
    )
```

```python
import functools
import jax
import jax.numpy as jnp
from jax import lax
from jax.experimental import pallas as pl
from jax.experimental.pallas import tpu as pltpu
from jax.sharding import Mesh, PartitionSpec as P

BF = jnp.bfloat16
F32 = jnp.float32
MB = 8
SUB = 4
LANES = 128
BLOCK = 64
CHUNK = 256
VMEM_LIMIT = 20 * 1024 * 1024
FULL_VMEM = 56 * 1024 * 1024


def iota(shape, dim):
    return lax.broadcasted_iota(jnp.int32, shape, dim)


def mm(a, b):
    return jnp.dot(a, b, preferred_element_type=F32)


def tmm(a, b):
    return lax.dot_general(a, b, (((0,), (0,)), ((), ())), preferred_element_type=F32)


def one_hot(condition):
    return jnp.where(condition, 1.0, 0.0).astype(BF)


def split(value):
    high = value.astype(BF)
    return high, (value - high.astype(F32)).astype(BF)


def call(kernel, out_shape, limit=VMEM_LIMIT, **extra):
    return pl.pallas_call(
        kernel,
        out_shape=out_shape,
        compiler_params=pltpu.CompilerParams(vmem_limit_bytes=limit),
        cost_estimate=pl.CostEstimate(flops=1, bytes_accessed=1, transcendentals=0),
        **extra,
    )


def vmem(count):
    return [pl.BlockSpec(memory_space=pltpu.VMEM)] * count


SCALAR = pl.BlockSpec(memory_space=pltpu.SMEM)


def convolve(table, value, classes, class_count):
    hours, width = value.shape
    columns = []
    for begin in range(0, width, CHUNK):
        cut = slice(begin, min(begin + CHUNK, width))
        masks = [one_hot(classes[:, cut] == float(k)) for k in range(class_count)]
        total = None
        for start in range(0, hours, BLOCK):
            block = value[start : start + BLOCK, cut]
            short = BLOCK - block.shape[0]
            if short:
                block = jnp.concatenate([block, jnp.zeros((short, block.shape[1]), BF)], axis=0)
            parts = jnp.concatenate([block * mask for mask in masks], axis=0)
            added = mm(table[: hours - start], parts)
            if start == 0:
                total = added
            else:
                total = jnp.concatenate([total[:start], total[start:] + added], axis=0)
        columns.append(total)
    return jnp.concatenate(columns, axis=1)


def pack_kernel(slot, x_ref, rows_ref, send_ref, held, rows_held, ready, arrived, sent):
    members, grid, hours = x_ref.shape
    blocks = members // MB
    regions = send_ref.shape[0]
    per = MB * slot

    half = members // 2

    def fetch(core):
        place = pl.ds(core * half, half)
        return pltpu.make_async_copy(x_ref.at[place], held.at[place], arrived.at[core])

    def deliver(core):
        return pltpu.make_async_copy(ready.at[:, core], send_ref.at[:, core], sent.at[core])

    first = pltpu.make_async_copy(rows_ref, rows_held, arrived.at[2])
    first.start()
    for core in range(2):
        fetch(core).start()
    first.wait()
    count = regions * per
    recv = rows_ref.shape[1]
    row = iota((count, recv), 0)
    wanted = (row // per) * slot + row % slot
    rows = rows_held[...].astype(F32)
    chosen = jnp.sum(jnp.where(iota((count, recv), 1) == wanted, rows, 0.0), axis=1, keepdims=True)
    lane = iota((count, MB * grid), 1)
    member = (iota((count, MB * grid), 0) // slot) % MB
    select = one_hot((lane // grid == member) & ((lane % grid).astype(F32) == chosen))
    for core in range(2):
        fetch(core).wait()
        for inner in range(blocks // 2):
            begin = core * half + inner * MB
            x = held[begin : begin + MB].reshape(MB * grid, hours).astype(BF)
            y = mm(select, x).astype(BF).reshape(regions, per, hours)
            ready[:, core, inner * per : (inner + 1) * per, :] = y
        deliver(core).start()
    for core in range(2):
        deliver(core).wait()


def raw_kernel(idx_ref, w_ref, cls_ref, outl_ref, inc_ref, raw_ref):
    raw_ref[...] = jnp.zeros_like(raw_ref)
    raw_ref[0 : idx_ref.shape[0], :] = idx_ref[...].astype(F32)
    raw_ref[8 : 8 + w_ref.shape[0], :] = w_ref[...]
    raw_ref[16:17, :] = cls_ref[...].astype(F32)
    raw_ref[24:25, 0 : outl_ref.shape[1]] = outl_ref[...].astype(F32)
    raw_ref[32:, :] = inc_ref[...].astype(F32)


def prep_kernel(
    slot, columns, core_ref, own_ref, other_ref, rate_ref, shape_ref,
    table_ref, mix_ref, pass_ref, cls_out_ref, wide_ref, link_ref, cls_target_ref, cls_own_ref,
):
    core = core_ref[0]
    class_count, hours = shape_ref.shape
    padded = -(-hours // LANES) * LANES
    kap = mix_ref.shape[1] // 2
    recv = kap // SUB
    per = SUB * slot
    outs = own_ref.shape[0] - 32
    reaches = own_ref.shape[1]
    wide = MB * outs
    narrow = SUB * outs

    lag = iota((class_count, hours), 1).astype(F32)
    square = (class_count, class_count)
    rate = jnp.where(iota(square, 0) == iota(square, 1), rate_ref[...], 0.0)
    rate = jnp.sum(rate, axis=1, keepdims=True)
    hydro = (rate * shape_ref[...] * jnp.exp(-rate * lag)).astype(BF)
    reverse = one_hot((iota((hours, padded), 0) + iota((hours, padded), 1)) % padded == 0)
    turned = mm(hydro, reverse)
    later = iota((padded, BLOCK), 1) <= iota((padded, BLOCK), 0)
    for k in range(class_count):
        rolled = pltpu.roll(
            jnp.broadcast_to(turned[k : k + 1, :], (padded, padded)), 0, 1, stride=1, stride_axis=0
        )
        rolled = jnp.where(later, rolled[:, :BLOCK], 0.0)
        table_ref[:, k * BLOCK : (k + 1) * BLOCK] = rolled[:hours].astype(BF)

    row_p = iota((kap, recv), 0)
    expand = one_hot((row_p // per) * slot + row_p % slot == iota((kap, recv), 1))

    def owner(width):
        return (iota((kap, width), 0) // slot) % SUB

    def tile(width):
        return one_hot(iota((outs, width), 0) == iota((outs, width), 1) % outs)

    def weights(raw):
        total = jnp.zeros((recv, reaches), F32)
        for j in range(columns):
            hit = iota((recv, reaches), 0).astype(F32) == raw[j : j + 1, :]
            total = total + jnp.where(hit, raw[8 + j : 9 + j, :], 0.0)
        return split(total)

    own = own_ref[...]
    for level in range(2):
        raw = jnp.where(core == level, own, other_ref[...])
        lanes = mm(raw[24:32, :outs].astype(BF), tile(wide))[0:1, :]
        pick = one_hot(iota((reaches, wide), 0).astype(F32) == lanes)
        for part, weight in enumerate(weights(raw)):
            spread = mm(expand, mm(weight, pick[:, :narrow]).astype(BF))
            spread = jnp.where(owner(narrow) == iota((kap, narrow), 1) // outs, spread, 0.0)
            mix_ref[level, part * kap : (part + 1) * kap] = spread.astype(BF)
        moved = jnp.concatenate([mm(raw[32:, :].astype(BF), pick)] * MB, axis=0)
        here = iota((wide, wide), 0) // outs == iota((wide, wide), 1) // outs
        pass_ref[level] = jnp.where(here, moved, 0.0).astype(BF)
        cls_out_ref[level] = mm(raw[16:24, :].astype(BF), pick)

    for part, weight in enumerate(weights(own)):
        spread = mm(expand, weight)
        for m in range(SUB):
            piece = jnp.where(owner(reaches) == m, spread, 0.0).astype(BF)
            wide_ref[part * kap : (part + 1) * kap, m * reaches : (m + 1) * reaches] = piece
    cls_own_ref[...] = own[16:24, :]
    cls_target_ref[...] = lax.dot_general(
        own[16:24, :].astype(BF),
        jnp.concatenate([own[32:, :]] * MB, axis=0).astype(BF),
        (((1,), (1,)), ((), ())),
        preferred_element_type=F32,
    )
    stacked = jnp.concatenate([own[32:, :]] * SUB, axis=0)
    who = iota((narrow, reaches), 0) // outs
    for m in range(SUB):
        piece = jnp.where(who == m, stacked, 0.0).astype(BF)
        for part in range(2):
            link_ref[part * narrow : (part + 1) * narrow, m * reaches : (m + 1) * reaches] = piece


def twice(rows_ref, sub, size):
    rows = rows_ref[:, sub * size : (sub + 1) * size, :]
    rows = rows.reshape(rows.shape[0] * size, rows.shape[2])
    return jnp.concatenate([rows, rows], axis=0)


def pass_on(panel, pass_matrix):
    width = pass_matrix.shape[0]
    parts = [
        mm(panel[:, start : start + width], pass_matrix).astype(BF)
        for start in range(0, panel.shape[1], width)
    ]
    return jnp.concatenate(parts, axis=1)


def tiled(classes, width):
    return jnp.concatenate([classes] * (width // classes.shape[1]), axis=1)


def head_kernel(class_count, core_ref, rows_ref, table_ref, mix_ref, pass_ref, cls_ref, *outs):
    panel_ref, even_ref, first_ref, send_ref = outs[:4]
    regions, _, total, _ = rows_ref.shape
    size = mix_ref.shape[1] // 2 // regions
    wide = panel_ref.shape[1]
    classes = [tiled(cls_ref[level, 0:1, :], wide) for level in range(2)]
    lateral = [
        jnp.concatenate(
            [
                tmm(twice(rows_ref.at[:, level], sub, size), mix_ref[level])
                for sub in range(total // size)
            ],
            axis=1,
        )
        for level in range(2)
    ]
    even = convolve(table_ref[...], lateral[0].astype(BF), classes[0], class_count)
    even_ref[...] = even
    first = even.astype(BF)
    first_ref[...] = first
    inflow = lateral[1] + pass_on(first, pass_ref[1]).astype(F32)
    panel_ref[...] = convolve(table_ref[...], inflow.astype(BF), classes[1], class_count).astype(BF)
    send_ref[...] = jnp.where(core_ref[0] == 0, rows_ref[:, 1], rows_ref[:, 0])
    if len(outs) > 4:
        outs[4][...] = lateral[1]


def hop_kernel(class_count, inflow_ref, table_ref, pass_ref, cls_ref, even_ref, odd_ref, panel_ref):
    classes = [tiled(cls_ref[level, 0:1, :], even_ref.shape[1]) for level in range(2)]
    moved = pass_on(inflow_ref[...], pass_ref[0])
    even = even_ref[...] + convolve(table_ref[...], moved, classes[0], class_count)
    moved = odd_ref[...] + pass_on(even.astype(BF), pass_ref[1]).astype(F32)
    panel_ref[...] = convolve(table_ref[...], moved.astype(BF), classes[1], class_count).astype(BF)


def last_hop_kernel(class_count, core_ref, pair_ref, inflow_ref, table_ref, pass_ref, cls_ref, even_ref, *rest):
    own_ref, send_ref = rest[-2:]

    @pl.when(pair_ref[0] > 0)
    def _():
        arrived = inflow_ref[...]
        classes = tiled(cls_ref[0, 0:1, :], even_ref.shape[1])
        moved = pass_on(arrived, pass_ref[0])
        even = even_ref[...] + convolve(table_ref[...], moved, classes, class_count)
        even = even.astype(BF)
        first = core_ref[0] == 0
        own_ref[...] = jnp.where(first, arrived, even)
        send_ref[...] = jnp.where(first, even, arrived)


def base_kernel(class_count, core_ref, rows_ref, table_ref, wide_ref, cls_ref, base_ref):
    if len(rows_ref.shape) == 4:
        rows_ref = rows_ref.at[:, core_ref[0]]
    regions, total, _ = rows_ref.shape
    size = wide_ref.shape[0] // 2 // regions
    width = wide_ref.shape[1]
    step = max(cls_ref.shape[1], 256)
    classes = tiled(cls_ref[0:1, :], step)
    for sub in range(total // size):
        rows = twice(rows_ref, sub, size)
        for start in range(0, width, step):
            lateral = tmm(rows, wide_ref[:, start : start + step]).astype(BF)
            place = sub * width + start
            base_ref[:, place : place + step] = convolve(
                table_ref[...], lateral, classes, class_count
            )


def routed_parts(class_count, top, core_ref, inflow_ref, table_ref, cls_ref):
    inflow = inflow_ref[...]
    if top:
        inflow = jnp.where(core_ref[0] == 0, jnp.zeros((), BF), inflow)
    classes = tiled(cls_ref[0:1, :], inflow.shape[1])
    return split(convolve(table_ref[...], inflow, classes, class_count))


def mine(top, pair_ref):
    return pl.when((pair_ref[0] == 0) == top)


def assemble(hours, high, low, base_ref, link_ref, scratch, members, reaches):
    lanes, width = link_ref.shape[0] // 2, link_ref.shape[1]
    count = hours.stop - hours.start
    for part in range(high.shape[1] // lanes):
        cut = slice(part * lanes, (part + 1) * lanes)
        both = jnp.concatenate([high[hours, cut], low[hours, cut]], axis=1)
        total = mm(both, link_ref[...]) + base_ref[hours, part * width : (part + 1) * width]
        for j in range(width // reaches):
            member = part * (width // reaches) + j
            scratch[pl.ds(hours.start * members + member, count, stride=members), :] = total[
                :, j * reaches : (j + 1) * reaches
            ]
    flow = scratch[hours.start * members : hours.stop * members, :]
    return flow.reshape(count, members, reaches).astype(BF)


def early_kernel(
    class_count, top, core_ref, pair_ref, inflow_ref, base_ref, table_ref, link_ref, cls_ref,
    out_ref, scratch,
):
    hours, members, reaches = out_ref.shape

    @mine(top, pair_ref)
    def _():
        high, low = routed_parts(class_count, top, core_ref, inflow_ref, table_ref, cls_ref)
        out_ref[...] = assemble(
            slice(0, hours), high, low, base_ref, link_ref, scratch, members, reaches
        )


def late_kernel(
    class_count, top, core_ref, pair_ref, done_ref, inflow_ref, base_ref, table_ref, link_ref,
    cls_ref, *rest,
):
    out_ref, scratch, ready, sems = rest[-4:]
    hours, members, reaches = done_ref.shape

    @mine(top, pair_ref)
    def _():
        core = core_ref[0]

        def place(which):
            return pl.ds(pl.multiple_of(which * members, members), members)

        copies = [pltpu.make_async_copy(done_ref, out_ref.at[:, place(core)], sems.at[0])]
        copies[0].start()
        high, low = routed_parts(class_count, top, core_ref, inflow_ref, table_ref, cls_ref)
        for start in range(0, hours, LANES):
            part = slice(start, min(start + LANES, hours))
            ready[part] = assemble(part, high, low, base_ref, link_ref, scratch, members, reaches)
            span = pl.ds(start, part.stop - start)
            copies.append(
                pltpu.make_async_copy(
                    ready.at[span], out_ref.at[span, place(1 - core)], sems.at[len(copies)]
                )
            )
            copies[-1].start()
        for copy in copies:
            copy.wait()


def local(
    runoff, send_rows, remap_index, remap_weight, class_id, kernel_shape, kernel_rate, outlets, incidence
):
    hours, members, grid = runoff.shape
    regions = lax.axis_size("region")
    pairs = lax.axis_size("pair")
    class_count = kernel_shape.shape[0]
    reaches, columns = remap_index.shape
    recv = send_rows.size
    slot = recv // regions
    outs = outlets.size
    half = members // 2
    kap = recv * SUB
    wide = half * outs
    core = lax.axis_index("core").astype(jnp.int32)
    core_arg = core.reshape(1)
    pair = lax.axis_index("pair")
    pair_arg = pair.astype(jnp.int32).reshape(1)
    swap = [(0, 1), (1, 0)]
    anywhere = pl.BlockSpec(memory_space=pl.ANY)

    def struct(shape, dtype):
        return jax.ShapeDtypeStruct(shape, dtype)

    send = call(
        functools.partial(pack_kernel, slot),
        struct((regions, 2, half * slot, hours), BF),
        limit=FULL_VMEM,
        in_specs=[anywhere] * 2,
        out_specs=anywhere,
        scratch_shapes=[
            pltpu.VMEM((members, grid, hours), F32),
            pltpu.VMEM((1, recv), jnp.int32),
            pltpu.VMEM((regions, 2, half * slot, hours), BF),
            pltpu.SemaphoreType.DMA((3,)),
            pltpu.SemaphoreType.DMA((2,)),
        ],
    )(jnp.transpose(runoff, (1, 2, 0)), send_rows.reshape(1, recv))
    received = lax.all_to_all(
        send.reshape(regions * 2, half * slot, hours), ("region", "core"), 0, 0
    ).reshape(regions, 2, half * slot, hours)
    raw = call(
        raw_kernel,
        struct((32 + outs, reaches), F32),
        in_specs=vmem(5),
        out_specs=vmem(1)[0],
    )(
        remap_index.T,
        remap_weight.T,
        class_id.T,
        outlets.reshape(1, outs),
        incidence.reshape(outs, reaches),
    )
    other = lax.ppermute(raw, "core", swap)
    table, mix, passing, cls_out, wide_mix, link, cls_target, cls_own = call(
        functools.partial(prep_kernel, slot, columns),
        (
            struct((hours, class_count * BLOCK), BF),
            struct((2, 2 * kap, SUB * outs), BF),
            struct((2, MB * outs, MB * outs), BF),
            struct((2, 8, MB * outs), F32),
            struct((2 * kap, SUB * reaches), BF),
            struct((2 * SUB * outs, SUB * reaches), BF),
            struct((8, MB * outs), F32),
            struct((8, reaches), F32),
        ),
        in_specs=[SCALAR] + vmem(4),
        out_specs=tuple(vmem(8)),
    )(core_arg, raw, other, kernel_rate.reshape(1, class_count), kernel_shape)

    panel_shape = struct((hours, wide), BF)
    float_shape = struct((hours, wide), F32)
    shapes = [panel_shape, float_shape, panel_shape, struct((regions, half * slot, hours), BF)]
    if pairs > 2:
        shapes.append(float_shape)
    heads = call(
        functools.partial(head_kernel, class_count),
        tuple(shapes),
        in_specs=[SCALAR] + vmem(5),
        out_specs=tuple(vmem(len(shapes))),
    )(core_arg, received, table, mix, passing, cls_out)
    panel, even, first, rows_send = heads[:4]

    inflow = jnp.zeros(panel_shape.shape, BF)
    for step in range(pairs - 1):
        arrived = lax.ppermute(panel, "pair", [(step, step + 1), (step + 1, step)])
        inflow = arrived if pairs == 2 else jnp.where(pair == step + 1, arrived, inflow)
        if step < pairs - 2:
            panel = call(
                functools.partial(hop_kernel, class_count),
                panel_shape,
                in_specs=vmem(6),
                out_specs=vmem(1)[0],
            )(inflow, table, passing, cls_out, even, heads[4])

    def base(rows):
        return call(
            functools.partial(base_kernel, class_count),
            struct((hours, half * reaches), F32),
            in_specs=[SCALAR] + vmem(4),
            out_specs=vmem(1)[0],
        )(core_arg, rows, table, wide_mix, cls_own)

    flat = pltpu.VMEM((hours * half, reaches), F32)
    rows_other = lax.ppermute(rows_send, "core", swap)
    first_other = lax.ppermute(first, "core", swap)
    base_own = base(received)
    base_other = base(rows_other)

    def early(top, own):
        return call(
            functools.partial(early_kernel, class_count, top),
            struct((hours, half, reaches), BF),
            in_specs=[SCALAR] * 2 + vmem(5),
            out_specs=vmem(1)[0],
            scratch_shapes=[flat],
        )(core_arg, pair_arg, own, base_own, table, link, cls_target)

    def late(top, done, gotten, before):
        return call(
            functools.partial(late_kernel, class_count, top),
            struct((hours, members, reaches), BF),
            in_specs=[SCALAR] * 2 + vmem(6) + [anywhere] * len(before),
            out_specs=anywhere,
            scratch_shapes=[
                flat,
                pltpu.VMEM((hours, half, reaches), BF),
                pltpu.SemaphoreType.DMA((1 + -(-hours // LANES),)),
            ],
            input_output_aliases={8: 0} if before else {},
        )(core_arg, pair_arg, done, gotten, base_other, table, link, cls_target, *before)

    done_first = early(True, first)
    own, given = call(
        functools.partial(last_hop_kernel, class_count),
        (panel_shape, panel_shape),
        in_specs=[SCALAR] * 2 + vmem(5) + [anywhere] * 2,
        out_specs=tuple(vmem(2)),
    )(core_arg, pair_arg, inflow, table, passing, cls_out, even, done_first, base_other)
    gotten = lax.ppermute(given, "core", swap)
    out = late(True, done_first, first_other, [])
    return late(False, early(False, own), gotten, [out])


def solution(mesh):
    regions, orders = mesh.shape["region"], mesh.shape["order"]
    split_mesh = Mesh(mesh.devices.reshape(regions, orders // 2, 2), ("region", "pair", "core"))
    order = ("pair", "core")
    every = ("region", "pair", "core")
    return jax.shard_map(
        local,
        mesh=split_mesh,
        in_specs=(
            P(None, None, every),
            P("region", order, None),
            P(every, None),
            P(every, None),
            P(every, None),
            P(),
            P(),
            P("region", order, None),
            P("region", order, None, None),
        ),
        out_specs=P(None, None, every),
        check_vma=False,
    )
```

```python
import functools
import jax
import jax.numpy as jnp
from jax import lax
from jax.experimental import pallas as pl
from jax.experimental.pallas import tpu as pltpu
from jax.sharding import Mesh, PartitionSpec as P

BF = jnp.bfloat16
F32 = jnp.float32
MB = 8
SUB = 4
LANES = 128
BLOCK = 32
CHUNK = 256
VMEM_LIMIT = 20 * 1024 * 1024
FULL_VMEM = 56 * 1024 * 1024


def iota(shape, dim):
    return lax.broadcasted_iota(jnp.int32, shape, dim)


def mm(a, b):
    return jnp.dot(a, b, preferred_element_type=F32)


def tmm(a, b):
    return lax.dot_general(a, b, (((0,), (0,)), ((), ())), preferred_element_type=F32)


def one_hot(condition):
    return jnp.where(condition, 1.0, 0.0).astype(BF)


def split(value):
    high = value.astype(BF)
    return high, (value - high.astype(F32)).astype(BF)


def call(kernel, out_shape, limit=VMEM_LIMIT, **extra):
    return pl.pallas_call(
        kernel,
        out_shape=out_shape,
        compiler_params=pltpu.CompilerParams(vmem_limit_bytes=limit),
        cost_estimate=pl.CostEstimate(flops=1, bytes_accessed=1, transcendentals=0),
        **extra,
    )


def vmem(count):
    return [pl.BlockSpec(memory_space=pltpu.VMEM)] * count


SCALAR = pl.BlockSpec(memory_space=pltpu.SMEM)


def convolve(table, value, classes, class_count):
    hours, width = value.shape
    columns = []
    for begin in range(0, width, CHUNK):
        cut = slice(begin, min(begin + CHUNK, width))
        masks = [one_hot(classes[:, cut] == float(k)) for k in range(class_count)]
        total = None
        for start in range(0, hours, BLOCK):
            block = value[start : start + BLOCK, cut]
            short = BLOCK - block.shape[0]
            if short:
                block = jnp.concatenate([block, jnp.zeros((short, block.shape[1]), BF)], axis=0)
            parts = jnp.concatenate([block * mask for mask in masks], axis=0)
            added = mm(table[: hours - start], parts)
            if start == 0:
                total = added
            else:
                total = jnp.concatenate([total[:start], total[start:] + added], axis=0)
        columns.append(total)
    return jnp.concatenate(columns, axis=1)


def pack_kernel(slot, x_ref, rows_ref, send_ref, held, rows_held, ready, arrived, sent):
    members, grid, hours = x_ref.shape
    blocks = members // MB
    regions = send_ref.shape[0]
    per = MB * slot

    half = members // 2

    def fetch(core):
        place = pl.ds(core * half, half)
        return pltpu.make_async_copy(x_ref.at[place], held.at[place], arrived.at[core])

    def deliver(core):
        return pltpu.make_async_copy(ready.at[:, core], send_ref.at[:, core], sent.at[core])

    first = pltpu.make_async_copy(rows_ref, rows_held, arrived.at[2])
    first.start()
    for core in range(2):
        fetch(core).start()
    first.wait()
    count = regions * per
    recv = rows_ref.shape[1]
    row = iota((count, recv), 0)
    wanted = (row // per) * slot + row % slot
    rows = rows_held[...].astype(F32)
    chosen = jnp.sum(jnp.where(iota((count, recv), 1) == wanted, rows, 0.0), axis=1, keepdims=True)
    lane = iota((count, MB * grid), 1)
    member = (iota((count, MB * grid), 0) // slot) % MB
    select = one_hot((lane // grid == member) & ((lane % grid).astype(F32) == chosen))
    for core in range(2):
        fetch(core).wait()
        for inner in range(blocks // 2):
            begin = core * half + inner * MB
            x = held[begin : begin + MB].reshape(MB * grid, hours).astype(BF)
            y = mm(select, x).astype(BF).reshape(regions, per, hours)
            ready[:, core, inner * per : (inner + 1) * per, :] = y
        deliver(core).start()
    for core in range(2):
        deliver(core).wait()


def raw_kernel(idx_ref, w_ref, cls_ref, outl_ref, inc_ref, raw_ref):
    raw_ref[...] = jnp.zeros_like(raw_ref)
    raw_ref[0 : idx_ref.shape[0], :] = idx_ref[...].astype(F32)
    raw_ref[8 : 8 + w_ref.shape[0], :] = w_ref[...]
    raw_ref[16:17, :] = cls_ref[...].astype(F32)
    raw_ref[24:25, 0 : outl_ref.shape[1]] = outl_ref[...].astype(F32)
    raw_ref[32:, :] = inc_ref[...].astype(F32)


def prep_kernel(
    slot, columns, core_ref, own_ref, other_ref, rate_ref, shape_ref,
    table_ref, mix_ref, pass_ref, cls_out_ref, wide_ref, link_ref, cls_target_ref, cls_own_ref,
):
    core = core_ref[0]
    class_count, hours = shape_ref.shape
    padded = -(-hours // LANES) * LANES
    kap = mix_ref.shape[1] // 2
    recv = kap // SUB
    per = SUB * slot
    outs = own_ref.shape[0] - 32
    reaches = own_ref.shape[1]
    wide = MB * outs
    narrow = SUB * outs

    lag = iota((class_count, hours), 1).astype(F32)
    square = (class_count, class_count)
    rate = jnp.where(iota(square, 0) == iota(square, 1), rate_ref[...], 0.0)
    rate = jnp.sum(rate, axis=1, keepdims=True)
    hydro = (rate * shape_ref[...] * jnp.exp(-rate * lag)).astype(BF)
    reverse = one_hot((iota((hours, padded), 0) + iota((hours, padded), 1)) % padded == 0)
    turned = mm(hydro, reverse)
    later = iota((padded, BLOCK), 1) <= iota((padded, BLOCK), 0)
    for k in range(class_count):
        rolled = pltpu.roll(
            jnp.broadcast_to(turned[k : k + 1, :], (padded, padded)), 0, 1, stride=1, stride_axis=0
        )
        rolled = jnp.where(later, rolled[:, :BLOCK], 0.0)
        table_ref[:, k * BLOCK : (k + 1) * BLOCK] = rolled[:hours].astype(BF)

    row_p = iota((kap, recv), 0)
    expand = one_hot((row_p // per) * slot + row_p % slot == iota((kap, recv), 1))

    def owner(width):
        return (iota((kap, width), 0) // slot) % SUB

    def tile(width):
        return one_hot(iota((outs, width), 0) == iota((outs, width), 1) % outs)

    def weights(raw):
        total = jnp.zeros((recv, reaches), F32)
        for j in range(columns):
            hit = iota((recv, reaches), 0).astype(F32) == raw[j : j + 1, :]
            total = total + jnp.where(hit, raw[8 + j : 9 + j, :], 0.0)
        return split(total)

    own = own_ref[...]
    for level in range(2):
        raw = jnp.where(core == level, own, other_ref[...])
        lanes = mm(raw[24:32, :outs].astype(BF), tile(wide))[0:1, :]
        pick = one_hot(iota((reaches, wide), 0).astype(F32) == lanes)
        for part, weight in enumerate(weights(raw)):
            spread = mm(expand, mm(weight, pick[:, :narrow]).astype(BF))
            spread = jnp.where(owner(narrow) == iota((kap, narrow), 1) // outs, spread, 0.0)
            mix_ref[level, part * kap : (part + 1) * kap] = spread.astype(BF)
        moved = jnp.concatenate([mm(raw[32:, :].astype(BF), pick)] * MB, axis=0)
        here = iota((wide, wide), 0) // outs == iota((wide, wide), 1) // outs
        pass_ref[level] = jnp.where(here, moved, 0.0).astype(BF)
        cls_out_ref[level] = mm(raw[16:24, :].astype(BF), pick)

    for part, weight in enumerate(weights(own)):
        spread = mm(expand, weight)
        for m in range(SUB):
            piece = jnp.where(owner(reaches) == m, spread, 0.0).astype(BF)
            wide_ref[part * kap : (part + 1) * kap, m * reaches : (m + 1) * reaches] = piece
    cls_own_ref[...] = own[16:24, :]
    cls_target_ref[...] = lax.dot_general(
        own[16:24, :].astype(BF),
        jnp.concatenate([own[32:, :]] * MB, axis=0).astype(BF),
        (((1,), (1,)), ((), ())),
        preferred_element_type=F32,
    )
    stacked = jnp.concatenate([own[32:, :]] * SUB, axis=0)
    who = iota((narrow, reaches), 0) // outs
    for m in range(SUB):
        piece = jnp.where(who == m, stacked, 0.0).astype(BF)
        for part in range(2):
            link_ref[part * narrow : (part + 1) * narrow, m * reaches : (m + 1) * reaches] = piece


def twice(rows_ref, sub, size):
    rows = rows_ref[:, sub * size : (sub + 1) * size, :]
    rows = rows.reshape(rows.shape[0] * size, rows.shape[2])
    return jnp.concatenate([rows, rows], axis=0)


def pass_on(panel, pass_matrix):
    width = pass_matrix.shape[0]
    parts = [
        mm(panel[:, start : start + width], pass_matrix).astype(BF)
        for start in range(0, panel.shape[1], width)
    ]
    return jnp.concatenate(parts, axis=1)


def tiled(classes, width):
    return jnp.concatenate([classes] * (width // classes.shape[1]), axis=1)


def head_kernel(class_count, core_ref, rows_ref, table_ref, mix_ref, pass_ref, cls_ref, *outs):
    panel_ref, even_ref, first_ref, send_ref = outs[:4]
    regions, _, total, _ = rows_ref.shape
    size = mix_ref.shape[1] // 2 // regions
    wide = panel_ref.shape[1]
    classes = [tiled(cls_ref[level, 0:1, :], wide) for level in range(2)]
    lateral = [
        jnp.concatenate(
            [
                tmm(twice(rows_ref.at[:, level], sub, size), mix_ref[level])
                for sub in range(total // size)
            ],
            axis=1,
        )
        for level in range(2)
    ]
    even = convolve(table_ref[...], lateral[0].astype(BF), classes[0], class_count)
    even_ref[...] = even
    first = even.astype(BF)
    first_ref[...] = first
    inflow = lateral[1] + pass_on(first, pass_ref[1]).astype(F32)
    panel_ref[...] = convolve(table_ref[...], inflow.astype(BF), classes[1], class_count).astype(BF)
    send_ref[...] = jnp.where(core_ref[0] == 0, rows_ref[:, 1], rows_ref[:, 0])
    if len(outs) > 4:
        outs[4][...] = lateral[1]


def hop_kernel(class_count, inflow_ref, table_ref, pass_ref, cls_ref, even_ref, odd_ref, panel_ref):
    classes = [tiled(cls_ref[level, 0:1, :], even_ref.shape[1]) for level in range(2)]
    moved = pass_on(inflow_ref[...], pass_ref[0])
    even = even_ref[...] + convolve(table_ref[...], moved, classes[0], class_count)
    moved = odd_ref[...] + pass_on(even.astype(BF), pass_ref[1]).astype(F32)
    panel_ref[...] = convolve(table_ref[...], moved.astype(BF), classes[1], class_count).astype(BF)


def last_hop_kernel(class_count, core_ref, pair_ref, inflow_ref, table_ref, pass_ref, cls_ref, even_ref, *rest):
    own_ref, send_ref = rest[-2:]

    @pl.when(pair_ref[0] > 0)
    def _():
        arrived = inflow_ref[...]
        classes = tiled(cls_ref[0, 0:1, :], even_ref.shape[1])
        moved = pass_on(arrived, pass_ref[0])
        even = even_ref[...] + convolve(table_ref[...], moved, classes, class_count)
        even = even.astype(BF)
        first = core_ref[0] == 0
        own_ref[...] = jnp.where(first, arrived, even)
        send_ref[...] = jnp.where(first, even, arrived)


def base_kernel(class_count, core_ref, rows_ref, table_ref, wide_ref, cls_ref, base_ref):
    if len(rows_ref.shape) == 4:
        rows_ref = rows_ref.at[:, core_ref[0]]
    regions, total, _ = rows_ref.shape
    size = wide_ref.shape[0] // 2 // regions
    width = wide_ref.shape[1]
    step = max(cls_ref.shape[1], 256)
    classes = tiled(cls_ref[0:1, :], step)
    for sub in range(total // size):
        rows = twice(rows_ref, sub, size)
        for start in range(0, width, step):
            lateral = tmm(rows, wide_ref[:, start : start + step]).astype(BF)
            place = sub * width + start
            base_ref[:, place : place + step] = convolve(
                table_ref[...], lateral, classes, class_count
            )


def routed_parts(class_count, top, core_ref, inflow_ref, table_ref, cls_ref):
    inflow = inflow_ref[...]
    if top:
        inflow = jnp.where(core_ref[0] == 0, jnp.zeros((), BF), inflow)
    classes = tiled(cls_ref[0:1, :], inflow.shape[1])
    return split(convolve(table_ref[...], inflow, classes, class_count))


def mine(top, pair_ref):
    return pl.when((pair_ref[0] == 0) == top)


def assemble(hours, high, low, base_ref, link_ref, members, reaches):
    lanes, width = link_ref.shape[0] // 2, link_ref.shape[1]
    flows = []
    for part in range(high.shape[1] // lanes):
        cut = slice(part * lanes, (part + 1) * lanes)
        both = jnp.concatenate([high[hours, cut], low[hours, cut]], axis=1)
        total = mm(both, link_ref[...]) + base_ref[hours, part * width : (part + 1) * width]
        flows.append(total.astype(BF))
    return jnp.concatenate(flows, axis=1).reshape(hours.stop - hours.start, members, reaches)


def early_kernel(
    class_count, top, core_ref, pair_ref, inflow_ref, base_ref, table_ref, link_ref, cls_ref,
    out_ref,
):
    hours, members, reaches = out_ref.shape

    @mine(top, pair_ref)
    def _():
        high, low = routed_parts(class_count, top, core_ref, inflow_ref, table_ref, cls_ref)
        out_ref[...] = assemble(slice(0, hours), high, low, base_ref, link_ref, members, reaches)


def late_kernel(
    class_count, top, core_ref, pair_ref, done_ref, inflow_ref, base_ref, table_ref, link_ref,
    cls_ref, *rest,
):
    out_ref, ready, sems = rest[-3:]
    hours, members, reaches = done_ref.shape

    @mine(top, pair_ref)
    def _():
        core = core_ref[0]

        def place(which):
            return pl.ds(pl.multiple_of(which * members, members), members)

        copies = [pltpu.make_async_copy(done_ref, out_ref.at[:, place(core)], sems.at[0])]
        copies[0].start()
        high, low = routed_parts(class_count, top, core_ref, inflow_ref, table_ref, cls_ref)
        for start in range(0, hours, LANES):
            part = slice(start, min(start + LANES, hours))
            ready[part] = assemble(part, high, low, base_ref, link_ref, members, reaches)
            span = pl.ds(start, part.stop - start)
            copies.append(
                pltpu.make_async_copy(
                    ready.at[span], out_ref.at[span, place(1 - core)], sems.at[len(copies)]
                )
            )
            copies[-1].start()
        for copy in copies:
            copy.wait()


def local(
    runoff, send_rows, remap_index, remap_weight, class_id, kernel_shape, kernel_rate, outlets, incidence
):
    hours, members, grid = runoff.shape
    regions = lax.axis_size("region")
    pairs = lax.axis_size("pair")
    class_count = kernel_shape.shape[0]
    reaches, columns = remap_index.shape
    recv = send_rows.size
    slot = recv // regions
    outs = outlets.size
    half = members // 2
    kap = recv * SUB
    wide = half * outs
    core = lax.axis_index("core").astype(jnp.int32)
    core_arg = core.reshape(1)
    pair = lax.axis_index("pair")
    pair_arg = pair.astype(jnp.int32).reshape(1)
    swap = [(0, 1), (1, 0)]
    anywhere = pl.BlockSpec(memory_space=pl.ANY)

    def struct(shape, dtype):
        return jax.ShapeDtypeStruct(shape, dtype)

    send = call(
        functools.partial(pack_kernel, slot),
        struct((regions, 2, half * slot, hours), BF),
        limit=FULL_VMEM,
        in_specs=[anywhere] * 2,
        out_specs=anywhere,
        scratch_shapes=[
            pltpu.VMEM((members, grid, hours), F32),
            pltpu.VMEM((1, recv), jnp.int32),
            pltpu.VMEM((regions, 2, half * slot, hours), BF),
            pltpu.SemaphoreType.DMA((3,)),
            pltpu.SemaphoreType.DMA((2,)),
        ],
    )(jnp.transpose(runoff, (1, 2, 0)), send_rows.reshape(1, recv))
    received = lax.all_to_all(
        send.reshape(regions * 2, half * slot, hours), ("region", "core"), 0, 0
    ).reshape(regions, 2, half * slot, hours)
    raw = call(
        raw_kernel,
        struct((32 + outs, reaches), F32),
        in_specs=vmem(5),
        out_specs=vmem(1)[0],
    )(
        remap_index.T,
        remap_weight.T,
        class_id.T,
        outlets.reshape(1, outs),
        incidence.reshape(outs, reaches),
    )
    other = lax.ppermute(raw, "core", swap)
    table, mix, passing, cls_out, wide_mix, link, cls_target, cls_own = call(
        functools.partial(prep_kernel, slot, columns),
        (
            struct((hours, class_count * BLOCK), BF),
            struct((2, 2 * kap, SUB * outs), BF),
            struct((2, MB * outs, MB * outs), BF),
            struct((2, 8, MB * outs), F32),
            struct((2 * kap, SUB * reaches), BF),
            struct((2 * SUB * outs, SUB * reaches), BF),
            struct((8, MB * outs), F32),
            struct((8, reaches), F32),
        ),
        in_specs=[SCALAR] + vmem(4),
        out_specs=tuple(vmem(8)),
    )(core_arg, raw, other, kernel_rate.reshape(1, class_count), kernel_shape)

    panel_shape = struct((hours, wide), BF)
    float_shape = struct((hours, wide), F32)
    shapes = [panel_shape, float_shape, panel_shape, struct((regions, half * slot, hours), BF)]
    if pairs > 2:
        shapes.append(float_shape)
    heads = call(
        functools.partial(head_kernel, class_count),
        tuple(shapes),
        in_specs=[SCALAR] + vmem(5),
        out_specs=tuple(vmem(len(shapes))),
    )(core_arg, received, table, mix, passing, cls_out)
    panel, even, first, rows_send = heads[:4]

    inflow = jnp.zeros(panel_shape.shape, BF)
    for step in range(pairs - 1):
        arrived = lax.ppermute(panel, "pair", [(step, step + 1), (step + 1, step)])
        inflow = arrived if pairs == 2 else jnp.where(pair == step + 1, arrived, inflow)
        if step < pairs - 2:
            panel = call(
                functools.partial(hop_kernel, class_count),
                panel_shape,
                in_specs=vmem(6),
                out_specs=vmem(1)[0],
            )(inflow, table, passing, cls_out, even, heads[4])

    def base(rows):
        return call(
            functools.partial(base_kernel, class_count),
            struct((hours, half * reaches), F32),
            in_specs=[SCALAR] + vmem(4),
            out_specs=vmem(1)[0],
        )(core_arg, rows, table, wide_mix, cls_own)

    rows_other = lax.ppermute(rows_send, "core", swap)
    first_other = lax.ppermute(first, "core", swap)
    base_own = base(received)
    base_other = base(rows_other)

    def early(top, own):
        return call(
            functools.partial(early_kernel, class_count, top),
            struct((hours, half, reaches), BF),
            in_specs=[SCALAR] * 2 + vmem(5),
            out_specs=vmem(1)[0],
        )(core_arg, pair_arg, own, base_own, table, link, cls_target)

    def late(top, done, gotten, before):
        return call(
            functools.partial(late_kernel, class_count, top),
            struct((hours, members, reaches), BF),
            in_specs=[SCALAR] * 2 + vmem(6) + [anywhere] * len(before),
            out_specs=anywhere,
            scratch_shapes=[
                pltpu.VMEM((hours, half, reaches), BF),
                pltpu.SemaphoreType.DMA((1 + -(-hours // LANES),)),
            ],
            input_output_aliases={8: 0} if before else {},
        )(core_arg, pair_arg, done, gotten, base_other, table, link, cls_target, *before)

    done_first = early(True, first)
    own, given = call(
        functools.partial(last_hop_kernel, class_count),
        (panel_shape, panel_shape),
        in_specs=[SCALAR] * 2 + vmem(5) + [anywhere] * 2,
        out_specs=tuple(vmem(2)),
    )(core_arg, pair_arg, inflow, table, passing, cls_out, even, done_first, base_other)
    gotten = lax.ppermute(given, "core", swap)
    out = late(True, done_first, first_other, [])
    return late(False, early(False, own), gotten, [out])


def solution(mesh):
    regions, orders = mesh.shape["region"], mesh.shape["order"]
    split_mesh = Mesh(mesh.devices.reshape(regions, orders // 2, 2), ("region", "pair", "core"))
    order = ("pair", "core")
    every = ("region", "pair", "core")
    return jax.shard_map(
        local,
        mesh=split_mesh,
        in_specs=(
            P(None, None, every),
            P("region", order, None),
            P(every, None),
            P(every, None),
            P(every, None),
            P(),
            P(),
            P("region", order, None),
            P("region", order, None, None),
        ),
        out_specs=P(None, None, every),
        check_vma=False,
    )
```

```python
import functools
import jax
import jax.numpy as jnp
from jax import lax
from jax.experimental import pallas as pl
from jax.experimental.pallas import tpu as pltpu
from jax.sharding import Mesh, PartitionSpec as P

BF = jnp.bfloat16
F32 = jnp.float32
MB = 8
SUB = 4
LANES = 128
BLOCK = 32
CHUNK = 256
VMEM_LIMIT = 20 * 1024 * 1024
FULL_VMEM = 56 * 1024 * 1024


def iota(shape, dim):
    return lax.broadcasted_iota(jnp.int32, shape, dim)


def mm(a, b):
    return jnp.dot(a, b, preferred_element_type=F32)


def one_hot(condition):
    return jnp.where(condition, 1.0, 0.0).astype(BF)


def split(value):
    high = value.astype(BF)
    return high, (value - high.astype(F32)).astype(BF)


def call(kernel, out_shape, limit=VMEM_LIMIT, **extra):
    return pl.pallas_call(
        kernel,
        out_shape=out_shape,
        compiler_params=pltpu.CompilerParams(vmem_limit_bytes=limit),
        cost_estimate=pl.CostEstimate(flops=1, bytes_accessed=1, transcendentals=0),
        **extra,
    )


def vmem(count):
    return [pl.BlockSpec(memory_space=pltpu.VMEM)] * count


SCALAR = pl.BlockSpec(memory_space=pltpu.SMEM)


def convolve(table, value, classes, class_count):
    hours, width = value.shape
    columns = []
    for begin in range(0, width, CHUNK):
        cut = slice(begin, min(begin + CHUNK, width))
        masks = [one_hot(classes[:, cut] == float(k)) for k in range(class_count)]
        total = None
        for start in range(0, hours, BLOCK):
            block = value[start : start + BLOCK, cut]
            short = BLOCK - block.shape[0]
            if short:
                block = jnp.concatenate([block, jnp.zeros((short, block.shape[1]), BF)], axis=0)
            parts = jnp.concatenate([block * mask for mask in masks], axis=0)
            added = mm(table[: hours - start], parts)
            if start == 0:
                total = added
            else:
                total = jnp.concatenate([total[:start], total[start:] + added], axis=0)
        columns.append(total)
    return jnp.concatenate(columns, axis=1)


def pack_kernel(slot, x_ref, rows_ref, send_ref, held, rows_held, ready, arrived, sent):
    members, grid, hours = x_ref.shape
    blocks = members // MB
    regions = send_ref.shape[0]
    per = MB * slot

    half = members // 2

    def fetch(core):
        place = pl.ds(core * half, half)
        return pltpu.make_async_copy(x_ref.at[place], held.at[place], arrived.at[core])

    def deliver(core):
        return pltpu.make_async_copy(ready.at[:, core], send_ref.at[:, core], sent.at[core])

    first = pltpu.make_async_copy(rows_ref, rows_held, arrived.at[2])
    first.start()
    for core in range(2):
        fetch(core).start()
    first.wait()
    count = regions * per
    recv = rows_ref.shape[1]
    row = iota((count, recv), 0)
    wanted = (row // per) * slot + row % slot
    rows = rows_held[...].astype(F32)
    chosen = jnp.sum(jnp.where(iota((count, recv), 1) == wanted, rows, 0.0), axis=1, keepdims=True)
    lane = iota((count, MB * grid), 1)
    member = (iota((count, MB * grid), 0) // slot) % MB
    select = one_hot((lane // grid == member) & ((lane % grid).astype(F32) == chosen))
    for core in range(2):
        fetch(core).wait()
        for inner in range(blocks // 2):
            begin = core * half + inner * MB
            x = held[begin : begin + MB].reshape(MB * grid, hours).astype(BF)
            y = mm(select, x).astype(BF).reshape(regions, per, hours)
            ready[:, core, inner * per : (inner + 1) * per, :] = y
        deliver(core).start()
    for core in range(2):
        deliver(core).wait()


def raw_kernel(idx_ref, w_ref, cls_ref, outl_ref, inc_ref, raw_ref):
    raw_ref[...] = jnp.zeros_like(raw_ref)
    raw_ref[0 : idx_ref.shape[0], :] = idx_ref[...].astype(F32)
    raw_ref[8 : 8 + w_ref.shape[0], :] = w_ref[...]
    raw_ref[16:17, :] = cls_ref[...].astype(F32)
    raw_ref[24:25, 0 : outl_ref.shape[1]] = outl_ref[...].astype(F32)
    raw_ref[32:, :] = inc_ref[...].astype(F32)


def prep_kernel(
    slot, columns, core_ref, own_ref, other_ref, rate_ref, shape_ref,
    table_ref, mix_ref, pass_ref, cls_out_ref, wide_ref, link_ref, cls_target_ref, cls_own_ref,
):
    core = core_ref[0]
    class_count, hours = shape_ref.shape
    padded = -(-hours // LANES) * LANES
    kap = mix_ref.shape[1] // 2
    recv = kap // SUB
    per = SUB * slot
    outs = own_ref.shape[0] - 32
    reaches = own_ref.shape[1]
    wide = MB * outs
    narrow = SUB * outs

    lag = iota((class_count, hours), 1).astype(F32)
    square = (class_count, class_count)
    rate = jnp.where(iota(square, 0) == iota(square, 1), rate_ref[...], 0.0)
    rate = jnp.sum(rate, axis=1, keepdims=True)
    hydro = (rate * shape_ref[...] * jnp.exp(-rate * lag)).astype(BF)
    reverse = one_hot((iota((hours, padded), 0) + iota((hours, padded), 1)) % padded == 0)
    turned = mm(hydro, reverse)
    later = iota((padded, BLOCK), 1) <= iota((padded, BLOCK), 0)
    for k in range(class_count):
        rolled = pltpu.roll(
            jnp.broadcast_to(turned[k : k + 1, :], (padded, padded)), 0, 1, stride=1, stride_axis=0
        )
        rolled = jnp.where(later, rolled[:, :BLOCK], 0.0)
        table_ref[:, k * BLOCK : (k + 1) * BLOCK] = rolled[:hours].astype(BF)

    row_p = iota((kap, recv), 0)
    expand = one_hot((row_p // per) * slot + row_p % slot == iota((kap, recv), 1))

    def owner(width):
        return (iota((kap, width), 0) // slot) % SUB

    def tile(width):
        return one_hot(iota((outs, width), 0) == iota((outs, width), 1) % outs)

    def weights(raw):
        total = jnp.zeros((recv, reaches), F32)
        for j in range(columns):
            hit = iota((recv, reaches), 0).astype(F32) == raw[j : j + 1, :]
            total = total + jnp.where(hit, raw[8 + j : 9 + j, :], 0.0)
        return split(total)

    own = own_ref[...]
    for level in range(2):
        raw = jnp.where(core == level, own, other_ref[...])
        lanes = mm(raw[24:32, :outs].astype(BF), tile(wide))[0:1, :]
        pick = one_hot(iota((reaches, wide), 0).astype(F32) == lanes)
        for part, weight in enumerate(weights(raw)):
            spread = mm(expand, mm(weight, pick[:, :narrow]).astype(BF))
            spread = jnp.where(owner(narrow) == iota((kap, narrow), 1) // outs, spread, 0.0)
            mix_ref[level, part * kap : (part + 1) * kap] = spread.astype(BF)
        moved = jnp.concatenate([mm(raw[32:, :].astype(BF), pick)] * MB, axis=0)
        here = iota((wide, wide), 0) // outs == iota((wide, wide), 1) // outs
        pass_ref[level] = jnp.where(here, moved, 0.0).astype(BF)
        cls_out_ref[level] = mm(raw[16:24, :].astype(BF), pick)

    for part, weight in enumerate(weights(own)):
        spread = mm(expand, weight)
        for m in range(SUB):
            piece = jnp.where(owner(reaches) == m, spread, 0.0).astype(BF)
            wide_ref[part * kap : (part + 1) * kap, m * reaches : (m + 1) * reaches] = piece
    cls_own_ref[...] = own[16:24, :]
    cls_target_ref[...] = lax.dot_general(
        own[16:24, :].astype(BF),
        jnp.concatenate([own[32:, :]] * MB, axis=0).astype(BF),
        (((1,), (1,)), ((), ())),
        preferred_element_type=F32,
    )
    stacked = jnp.concatenate([own[32:, :]] * SUB, axis=0)
    who = iota((narrow, reaches), 0) // outs
    for m in range(SUB):
        piece = jnp.where(who == m, stacked, 0.0).astype(BF)
        for part in range(2):
            link_ref[part * narrow : (part + 1) * narrow, m * reaches : (m + 1) * reaches] = piece


def twice(rows_ref, sub, size):
    rows = rows_ref[:, sub * size : (sub + 1) * size, :]
    rows = rows.reshape(rows.shape[0] * size, rows.shape[2]).T
    return jnp.concatenate([rows, rows], axis=1)


def pass_on(panel, pass_matrix):
    width = pass_matrix.shape[0]
    parts = [
        mm(panel[:, start : start + width], pass_matrix).astype(BF)
        for start in range(0, panel.shape[1], width)
    ]
    return jnp.concatenate(parts, axis=1)


def tiled(classes, width):
    return jnp.concatenate([classes] * (width // classes.shape[1]), axis=1)


def outlet_lateral(level, rows_ref, mix_ref):
    regions, _, total, _ = rows_ref.shape
    size = mix_ref.shape[1] // 2 // regions
    rows_ref = rows_ref.at[:, level]
    parts = [mm(twice(rows_ref, sub, size), mix_ref[level]) for sub in range(total // size)]
    return jnp.concatenate(parts, axis=1)


def head_kernel(
    class_count, core_ref, pair_ref, rows_ref, table_ref, mix_ref, pass_ref, cls_ref,
    panel_ref, first_ref, send_ref,
):
    send_ref[...] = jnp.where(core_ref[0] == 0, rows_ref[:, 1], rows_ref[:, 0])

    @pl.when(pair_ref[0] == 0)
    def _():
        wide = panel_ref.shape[1]
        classes = [tiled(cls_ref[level, 0:1, :], wide) for level in range(2)]
        lateral = [outlet_lateral(level, rows_ref, mix_ref) for level in range(2)]
        first = convolve(table_ref[...], lateral[0].astype(BF), classes[0], class_count).astype(BF)
        first_ref[...] = first
        inflow = (lateral[1] + pass_on(first, pass_ref[1]).astype(F32)).astype(BF)
        panel_ref[...] = convolve(table_ref[...], inflow, classes[1], class_count).astype(BF)


def hop_kernel(class_count, inflow_ref, table_ref, pass_ref, cls_ref, even_ref, odd_ref, panel_ref):
    classes = [tiled(cls_ref[level, 0:1, :], even_ref.shape[1]) for level in range(2)]
    moved = pass_on(inflow_ref[...], pass_ref[0])
    even = even_ref[...] + convolve(table_ref[...], moved, classes[0], class_count)
    moved = odd_ref[...] + pass_on(even.astype(BF), pass_ref[1]).astype(F32)
    panel_ref[...] = convolve(table_ref[...], moved.astype(BF), classes[1], class_count).astype(BF)


def last_hop_kernel(class_count, core_ref, pair_ref, inflow_ref, table_ref, pass_ref, cls_ref, even_ref, *rest):
    own_ref, send_ref = rest[-2:]

    @pl.when(pair_ref[0] > 0)
    def _():
        arrived = inflow_ref[...]
        classes = tiled(cls_ref[0, 0:1, :], even_ref.shape[1])
        moved = pass_on(arrived, pass_ref[0])
        even = even_ref[...] + convolve(table_ref[...], moved, classes, class_count)
        even = even.astype(BF)
        first = core_ref[0] == 0
        own_ref[...] = jnp.where(first, arrived, even)
        send_ref[...] = jnp.where(first, even, arrived)


def base_kernel(class_count, core_ref, rows_ref, table_ref, wide_ref, cls_ref, base_ref):
    if len(rows_ref.shape) == 4:
        rows_ref = rows_ref.at[:, core_ref[0]]
    regions, total, _ = rows_ref.shape
    size = wide_ref.shape[0] // 2 // regions
    width = wide_ref.shape[1]
    step = max(cls_ref.shape[1], 256)
    classes = tiled(cls_ref[0:1, :], step)
    for sub in range(total // size):
        rows = twice(rows_ref, sub, size)
        for start in range(0, width, step):
            lateral = mm(rows, wide_ref[:, start : start + step]).astype(BF)
            place = sub * width + start
            base_ref[:, place : place + step] = convolve(
                table_ref[...], lateral, classes, class_count
            )


def base_own_kernel(
    class_count, core_ref, pair_ref, rows_ref, table_ref, wide_ref, cls_ref, mix_ref, cls_out_ref,
    base_ref, even_ref, *odd_ref,
):
    base_kernel(class_count, core_ref, rows_ref, table_ref, wide_ref, cls_ref, base_ref)

    @pl.when(pair_ref[0] > 0)
    def _():
        lateral = outlet_lateral(0, rows_ref, mix_ref).astype(BF)
        classes = tiled(cls_out_ref[0, 0:1, :], even_ref.shape[1])
        even_ref[...] = convolve(table_ref[...], lateral, classes, class_count)
        if odd_ref:
            odd_ref[0][...] = outlet_lateral(1, rows_ref, mix_ref)


def routed_parts(class_count, top, core_ref, inflow_ref, table_ref, cls_ref):
    inflow = inflow_ref[...]
    if top:
        inflow = jnp.where(core_ref[0] == 0, jnp.zeros((), BF), inflow)
    classes = tiled(cls_ref[0:1, :], inflow.shape[1])
    return split(convolve(table_ref[...], inflow, classes, class_count))


def mine(top, pair_ref):
    return pl.when((pair_ref[0] == 0) == top)


def assemble(hours, high, low, base_ref, link_ref, members, reaches):
    lanes, width = link_ref.shape[0] // 2, link_ref.shape[1]
    flows = []
    for part in range(high.shape[1] // lanes):
        cut = slice(part * lanes, (part + 1) * lanes)
        both = jnp.concatenate([high[hours, cut], low[hours, cut]], axis=1)
        total = mm(both, link_ref[...]) + base_ref[hours, part * width : (part + 1) * width]
        flows.append(total.astype(BF))
    return jnp.concatenate(flows, axis=1).reshape(hours.stop - hours.start, members, reaches)


def early_kernel(
    class_count, top, core_ref, pair_ref, inflow_ref, base_ref, table_ref, link_ref, cls_ref,
    out_ref,
):
    hours, members, reaches = out_ref.shape

    @mine(top, pair_ref)
    def _():
        high, low = routed_parts(class_count, top, core_ref, inflow_ref, table_ref, cls_ref)
        out_ref[...] = assemble(slice(0, hours), high, low, base_ref, link_ref, members, reaches)


def late_kernel(
    class_count, top, core_ref, pair_ref, done_ref, inflow_ref, base_ref, table_ref, link_ref,
    cls_ref, *rest,
):
    out_ref, ready, sems = rest[-3:]
    hours, members, reaches = done_ref.shape

    @mine(top, pair_ref)
    def _():
        core = core_ref[0]

        def place(which):
            return pl.ds(pl.multiple_of(which * members, members), members)

        copies = [pltpu.make_async_copy(done_ref, out_ref.at[:, place(core)], sems.at[0])]
        copies[0].start()
        high, low = routed_parts(class_count, top, core_ref, inflow_ref, table_ref, cls_ref)
        for start in range(0, hours, LANES):
            part = slice(start, min(start + LANES, hours))
            ready[part] = assemble(part, high, low, base_ref, link_ref, members, reaches)
            span = pl.ds(start, part.stop - start)
            copies.append(
                pltpu.make_async_copy(
                    ready.at[span], out_ref.at[span, place(1 - core)], sems.at[len(copies)]
                )
            )
            copies[-1].start()
        for copy in copies:
            copy.wait()


def local(
    runoff, send_rows, remap_index, remap_weight, class_id, kernel_shape, kernel_rate, outlets, incidence
):
    hours, members, grid = runoff.shape
    regions = lax.axis_size("region")
    pairs = lax.axis_size("pair")
    class_count = kernel_shape.shape[0]
    reaches, columns = remap_index.shape
    recv = send_rows.size
    slot = recv // regions
    outs = outlets.size
    half = members // 2
    kap = recv * SUB
    wide = half * outs
    core = lax.axis_index("core").astype(jnp.int32)
    core_arg = core.reshape(1)
    pair = lax.axis_index("pair")
    pair_arg = pair.astype(jnp.int32).reshape(1)
    swap = [(0, 1), (1, 0)]
    anywhere = pl.BlockSpec(memory_space=pl.ANY)

    def struct(shape, dtype):
        return jax.ShapeDtypeStruct(shape, dtype)

    send = call(
        functools.partial(pack_kernel, slot),
        struct((regions, 2, half * slot, hours), BF),
        limit=FULL_VMEM,
        in_specs=[anywhere] * 2,
        out_specs=anywhere,
        scratch_shapes=[
            pltpu.VMEM((members, grid, hours), F32),
            pltpu.VMEM((1, recv), jnp.int32),
            pltpu.VMEM((regions, 2, half * slot, hours), BF),
            pltpu.SemaphoreType.DMA((3,)),
            pltpu.SemaphoreType.DMA((2,)),
        ],
    )(jnp.transpose(runoff, (1, 2, 0)), send_rows.reshape(1, recv))
    received = lax.all_to_all(
        send.reshape(regions * 2, half * slot, hours), ("region", "core"), 0, 0
    ).reshape(regions, 2, half * slot, hours)
    raw = call(
        raw_kernel,
        struct((32 + outs, reaches), F32),
        in_specs=vmem(5),
        out_specs=vmem(1)[0],
    )(
        remap_index.T,
        remap_weight.T,
        class_id.T,
        outlets.reshape(1, outs),
        incidence.reshape(outs, reaches),
    )
    other = lax.ppermute(raw, "core", swap)
    table, mix, passing, cls_out, wide_mix, link, cls_target, cls_own = call(
        functools.partial(prep_kernel, slot, columns),
        (
            struct((hours, class_count * BLOCK), BF),
            struct((2, 2 * kap, SUB * outs), BF),
            struct((2, MB * outs, MB * outs), BF),
            struct((2, 8, MB * outs), F32),
            struct((2 * kap, SUB * reaches), BF),
            struct((2 * SUB * outs, SUB * reaches), BF),
            struct((8, MB * outs), F32),
            struct((8, reaches), F32),
        ),
        in_specs=[SCALAR] + vmem(4),
        out_specs=tuple(vmem(8)),
    )(core_arg, raw, other, kernel_rate.reshape(1, class_count), kernel_shape)

    panel_shape = struct((hours, wide), BF)
    float_shape = struct((hours, wide), F32)
    panel, first, rows_send = call(
        functools.partial(head_kernel, class_count),
        (panel_shape, panel_shape, struct((regions, half * slot, hours), BF)),
        in_specs=[SCALAR] * 2 + vmem(5),
        out_specs=tuple(vmem(3)),
    )(core_arg, pair_arg, received, table, mix, passing, cls_out)
    inflow = lax.ppermute(panel, "pair", [(0, 1), (1, 0)]) if pairs > 1 else panel
    rows_other = lax.ppermute(rows_send, "core", swap)
    first_other = lax.ppermute(first, "core", swap)

    base_shape = struct((hours, half * reaches), F32)
    shapes = [base_shape, float_shape] + [float_shape] * (pairs > 2)
    base_own, even, *odd = call(
        functools.partial(base_own_kernel, class_count),
        tuple(shapes),
        in_specs=[SCALAR] * 2 + vmem(6),
        out_specs=tuple(vmem(len(shapes))),
    )(core_arg, pair_arg, received, table, wide_mix, cls_own, mix, cls_out)
    base_other = call(
        functools.partial(base_kernel, class_count),
        base_shape,
        in_specs=[SCALAR] + vmem(4),
        out_specs=vmem(1)[0],
    )(core_arg, rows_other, table, wide_mix, cls_own)


    for step in range(1, pairs - 1):
        panel = call(
            functools.partial(hop_kernel, class_count),
            panel_shape,
            in_specs=vmem(6),
            out_specs=vmem(1)[0],
        )(inflow, table, passing, cls_out, even, odd[0])
        arriving = lax.ppermute(panel, "pair", [(step, step + 1), (step + 1, step)])
        inflow = jnp.where(pair == step + 1, arriving, inflow)

    def early(top, own):
        return call(
            functools.partial(early_kernel, class_count, top),
            struct((hours, half, reaches), BF),
            in_specs=[SCALAR] * 2 + vmem(5),
            out_specs=vmem(1)[0],
        )(core_arg, pair_arg, own, base_own, table, link, cls_target)

    def late(top, done, gotten, before):
        return call(
            functools.partial(late_kernel, class_count, top),
            struct((hours, members, reaches), BF),
            in_specs=[SCALAR] * 2 + vmem(6) + [anywhere] * len(before),
            out_specs=anywhere,
            scratch_shapes=[
                pltpu.VMEM((hours, half, reaches), BF),
                pltpu.SemaphoreType.DMA((1 + -(-hours // LANES),)),
            ],
            input_output_aliases={8: 0} if before else {},
        )(core_arg, pair_arg, done, gotten, base_other, table, link, cls_target, *before)

    done_first = early(True, first)
    own, given = call(
        functools.partial(last_hop_kernel, class_count),
        (panel_shape, panel_shape),
        in_specs=[SCALAR] * 2 + vmem(5) + [anywhere] * 2,
        out_specs=tuple(vmem(2)),
    )(core_arg, pair_arg, inflow, table, passing, cls_out, even, done_first, base_other)
    gotten = lax.ppermute(given, "core", swap)
    out = late(True, done_first, first_other, [])
    return late(False, early(False, own), gotten, [out])


def solution(mesh):
    regions, orders = mesh.shape["region"], mesh.shape["order"]
    split_mesh = Mesh(mesh.devices.reshape(regions, orders // 2, 2), ("region", "pair", "core"))
    order = ("pair", "core")
    every = ("region", "pair", "core")
    return jax.shard_map(
        local,
        mesh=split_mesh,
        in_specs=(
            P(None, None, every),
            P("region", order, None),
            P(every, None),
            P(every, None),
            P(every, None),
            P(),
            P(),
            P("region", order, None),
            P("region", order, None, None),
        ),
        out_specs=P(None, None, every),
        check_vma=False,
    )
```

```python
import functools
import jax
import jax.numpy as jnp
from jax import lax
from jax.experimental import pallas as pl
from jax.experimental.pallas import tpu as pltpu
from jax.sharding import Mesh, PartitionSpec as P

BF = jnp.bfloat16
F32 = jnp.float32
MB = 8
SUB = 4
LANES = 128
BLOCK = 32
CHUNK = 256
VMEM_LIMIT = 20 * 1024 * 1024
FULL_VMEM = 56 * 1024 * 1024


def iota(shape, dim):
    return lax.broadcasted_iota(jnp.int32, shape, dim)


def mm(a, b):
    return jnp.dot(a, b, preferred_element_type=F32)


def one_hot(condition):
    return jnp.where(condition, 1.0, 0.0).astype(BF)


def split(value):
    high = value.astype(BF)
    return high, (value - high.astype(F32)).astype(BF)


def call(kernel, out_shape, limit=VMEM_LIMIT, **extra):
    return pl.pallas_call(
        kernel,
        out_shape=out_shape,
        compiler_params=pltpu.CompilerParams(vmem_limit_bytes=limit),
        cost_estimate=pl.CostEstimate(flops=1, bytes_accessed=1, transcendentals=0),
        **extra,
    )


def vmem(count):
    return [pl.BlockSpec(memory_space=pltpu.VMEM)] * count


SCALAR = pl.BlockSpec(memory_space=pltpu.SMEM)


def convolve(table, value, classes, class_count):
    hours, width = value.shape
    columns = []
    for begin in range(0, width, CHUNK):
        cut = slice(begin, min(begin + CHUNK, width))
        masks = [one_hot(classes[:, cut] == float(k)) for k in range(class_count)]
        total = None
        for start in range(0, hours, BLOCK):
            block = value[start : start + BLOCK, cut]
            short = BLOCK - block.shape[0]
            if short:
                block = jnp.concatenate([block, jnp.zeros((short, block.shape[1]), BF)], axis=0)
            parts = jnp.concatenate([block * mask for mask in masks], axis=0)
            added = mm(table[: hours - start], parts)
            if start == 0:
                total = added
            else:
                total = jnp.concatenate([total[:start], total[start:] + added], axis=0)
        columns.append(total)
    return jnp.concatenate(columns, axis=1)


def pack_kernel(slot, x_ref, rows_ref, send_ref, held, rows_held, ready, arrived, sent):
    members, grid, hours = x_ref.shape
    blocks = members // MB
    regions = send_ref.shape[0]
    per = MB * slot

    half = members // 2

    def fetch(core):
        place = pl.ds(core * half, half)
        return pltpu.make_async_copy(x_ref.at[place], held.at[place], arrived.at[core])

    def deliver(core):
        return pltpu.make_async_copy(ready.at[:, core], send_ref.at[:, core], sent.at[core])

    first = pltpu.make_async_copy(rows_ref, rows_held, arrived.at[2])
    first.start()
    for core in range(2):
        fetch(core).start()
    first.wait()
    count = regions * per
    recv = rows_ref.shape[1]
    row = iota((count, recv), 0)
    wanted = (row // per) * slot + row % slot
    rows = rows_held[...].astype(F32)
    chosen = jnp.sum(jnp.where(iota((count, recv), 1) == wanted, rows, 0.0), axis=1, keepdims=True)
    lane = iota((count, MB * grid), 1)
    member = (iota((count, MB * grid), 0) // slot) % MB
    select = one_hot((lane // grid == member) & ((lane % grid).astype(F32) == chosen))
    for core in range(2):
        fetch(core).wait()
        for inner in range(blocks // 2):
            begin = core * half + inner * MB
            x = held[begin : begin + MB].reshape(MB * grid, hours).astype(BF)
            y = mm(select, x).astype(BF).reshape(regions, per, hours)
            ready[:, core, inner * per : (inner + 1) * per, :] = y
        deliver(core).start()
    for core in range(2):
        deliver(core).wait()


def raw_kernel(idx_ref, w_ref, cls_ref, outl_ref, inc_ref, raw_ref):
    raw_ref[...] = jnp.zeros_like(raw_ref)
    raw_ref[0 : idx_ref.shape[0], :] = idx_ref[...].astype(F32)
    raw_ref[8 : 8 + w_ref.shape[0], :] = w_ref[...]
    raw_ref[16:17, :] = cls_ref[...].astype(F32)
    raw_ref[24:25, 0 : outl_ref.shape[1]] = outl_ref[...].astype(F32)
    raw_ref[32:, :] = inc_ref[...].astype(F32)


def prep_kernel(
    slot, columns, core_ref, own_ref, other_ref, rate_ref, shape_ref,
    table_ref, mix_ref, pass_ref, cls_out_ref, wide_ref, link_ref, cls_target_ref, cls_own_ref,
):
    core = core_ref[0]
    class_count, hours = shape_ref.shape
    padded = -(-hours // LANES) * LANES
    kap = mix_ref.shape[1] // 2
    recv = kap // SUB
    per = SUB * slot
    outs = own_ref.shape[0] - 32
    reaches = own_ref.shape[1]
    wide = MB * outs
    narrow = SUB * outs

    lag = iota((class_count, hours), 1).astype(F32)
    square = (class_count, class_count)
    rate = jnp.where(iota(square, 0) == iota(square, 1), rate_ref[...], 0.0)
    rate = jnp.sum(rate, axis=1, keepdims=True)
    hydro = (rate * shape_ref[...] * jnp.exp(-rate * lag)).astype(BF)
    reverse = one_hot((iota((hours, padded), 0) + iota((hours, padded), 1)) % padded == 0)
    turned = mm(hydro, reverse)
    later = iota((padded, BLOCK), 1) <= iota((padded, BLOCK), 0)
    for k in range(class_count):
        rolled = pltpu.roll(
            jnp.broadcast_to(turned[k : k + 1, :], (padded, padded)), 0, 1, stride=1, stride_axis=0
        )
        rolled = jnp.where(later, rolled[:, :BLOCK], 0.0)
        table_ref[:, k * BLOCK : (k + 1) * BLOCK] = rolled[:hours].astype(BF)

    row_p = iota((kap, recv), 0)
    expand = one_hot((row_p // per) * slot + row_p % slot == iota((kap, recv), 1))

    def owner(width):
        return (iota((kap, width), 0) // slot) % SUB

    def tile(width):
        return one_hot(iota((outs, width), 0) == iota((outs, width), 1) % outs)

    def weights(raw):
        total = jnp.zeros((recv, reaches), F32)
        for j in range(columns):
            hit = iota((recv, reaches), 0).astype(F32) == raw[j : j + 1, :]
            total = total + jnp.where(hit, raw[8 + j : 9 + j, :], 0.0)
        return split(total)

    own = own_ref[...]
    for level in range(2):
        raw = jnp.where(core == level, own, other_ref[...])
        lanes = mm(raw[24:32, :outs].astype(BF), tile(wide))[0:1, :]
        pick = one_hot(iota((reaches, wide), 0).astype(F32) == lanes)
        for part, weight in enumerate(weights(raw)):
            spread = mm(expand, mm(weight, pick[:, :narrow]).astype(BF))
            spread = jnp.where(owner(narrow) == iota((kap, narrow), 1) // outs, spread, 0.0)
            mix_ref[level, part * kap : (part + 1) * kap] = spread.astype(BF)
        moved = jnp.concatenate([mm(raw[32:, :].astype(BF), pick)] * MB, axis=0)
        here = iota((wide, wide), 0) // outs == iota((wide, wide), 1) // outs
        pass_ref[level] = jnp.where(here, moved, 0.0).astype(BF)
        cls_out_ref[level] = mm(raw[16:24, :].astype(BF), pick)

    for part, weight in enumerate(weights(own)):
        spread = mm(expand, weight)
        for m in range(SUB):
            piece = jnp.where(owner(reaches) == m, spread, 0.0).astype(BF)
            wide_ref[part * kap : (part + 1) * kap, m * reaches : (m + 1) * reaches] = piece
    cls_own_ref[...] = own[16:24, :]
    cls_target_ref[...] = lax.dot_general(
        own[16:24, :].astype(BF),
        jnp.concatenate([own[32:, :]] * MB, axis=0).astype(BF),
        (((1,), (1,)), ((), ())),
        preferred_element_type=F32,
    )
    stacked = jnp.concatenate([own[32:, :]] * SUB, axis=0)
    who = iota((narrow, reaches), 0) // outs
    for m in range(SUB):
        piece = jnp.where(who == m, stacked, 0.0).astype(BF)
        for part in range(2):
            link_ref[part * narrow : (part + 1) * narrow, m * reaches : (m + 1) * reaches] = piece


def side_by_side(parts, right):
    product = mm(jnp.concatenate(parts, axis=0), right)
    count = parts[0].shape[0]
    rows = [product[i * count : (i + 1) * count] for i in range(len(parts))]
    return jnp.concatenate(rows, axis=1)


def twice(rows_ref, sub, size):
    rows = rows_ref[:, sub * size : (sub + 1) * size, :]
    rows = rows.reshape(rows.shape[0] * size, rows.shape[2]).T
    return jnp.concatenate([rows, rows], axis=1)


def pass_on(panel, pass_matrix):
    width = pass_matrix.shape[0]
    parts = [
        mm(panel[:, start : start + width], pass_matrix).astype(BF)
        for start in range(0, panel.shape[1], width)
    ]
    return jnp.concatenate(parts, axis=1)


def tiled(classes, width):
    return jnp.concatenate([classes] * (width // classes.shape[1]), axis=1)


def outlet_lateral(level, rows_ref, mix_ref):
    regions, _, total, _ = rows_ref.shape
    size = mix_ref.shape[1] // 2 // regions
    rows_ref = rows_ref.at[:, level]
    parts = [mm(twice(rows_ref, sub, size), mix_ref[level]) for sub in range(total // size)]
    return jnp.concatenate(parts, axis=1)


def head_kernel(
    class_count, core_ref, pair_ref, rows_ref, table_ref, mix_ref, pass_ref, cls_ref,
    panel_ref, first_ref, send_ref,
):
    send_ref[...] = jnp.where(core_ref[0] == 0, rows_ref[:, 1], rows_ref[:, 0])

    @pl.when(pair_ref[0] == 0)
    def _():
        wide = panel_ref.shape[1]
        classes = [tiled(cls_ref[level, 0:1, :], wide) for level in range(2)]
        lateral = [outlet_lateral(level, rows_ref, mix_ref) for level in range(2)]
        first = convolve(table_ref[...], lateral[0].astype(BF), classes[0], class_count).astype(BF)
        first_ref[...] = first
        inflow = (lateral[1] + pass_on(first, pass_ref[1]).astype(F32)).astype(BF)
        panel_ref[...] = convolve(table_ref[...], inflow, classes[1], class_count).astype(BF)


def hop_kernel(class_count, inflow_ref, table_ref, pass_ref, cls_ref, even_ref, odd_ref, panel_ref):
    classes = [tiled(cls_ref[level, 0:1, :], even_ref.shape[1]) for level in range(2)]
    moved = pass_on(inflow_ref[...], pass_ref[0])
    even = even_ref[...] + convolve(table_ref[...], moved, classes[0], class_count)
    moved = odd_ref[...] + pass_on(even.astype(BF), pass_ref[1]).astype(F32)
    panel_ref[...] = convolve(table_ref[...], moved.astype(BF), classes[1], class_count).astype(BF)


def last_hop_kernel(class_count, core_ref, pair_ref, inflow_ref, table_ref, pass_ref, cls_ref, even_ref, *rest):
    own_ref, send_ref = rest[-2:]

    @pl.when(pair_ref[0] > 0)
    def _():
        arrived = inflow_ref[...]
        classes = tiled(cls_ref[0, 0:1, :], even_ref.shape[1])
        moved = pass_on(arrived, pass_ref[0])
        even = even_ref[...] + convolve(table_ref[...], moved, classes, class_count)
        even = even.astype(BF)
        first = core_ref[0] == 0
        own_ref[...] = jnp.where(first, arrived, even)
        send_ref[...] = jnp.where(first, even, arrived)


def base_kernel(class_count, core_ref, rows_ref, table_ref, wide_ref, cls_ref, base_ref):
    if len(rows_ref.shape) == 4:
        rows_ref = rows_ref.at[:, core_ref[0]]
    regions, total, _ = rows_ref.shape
    size = wide_ref.shape[0] // 2 // regions
    width = wide_ref.shape[1]
    parts = [twice(rows_ref, sub, size) for sub in range(total // size)]
    classes = tiled(cls_ref[0:1, :], width)
    lateral = side_by_side(parts, wide_ref[...]).astype(BF)
    for start in range(0, base_ref.shape[1], width):
        base_ref[:, start : start + width] = convolve(
            table_ref[...], lateral[:, start : start + width], classes, class_count
        )


def base_own_kernel(
    class_count, core_ref, pair_ref, rows_ref, table_ref, wide_ref, cls_ref, mix_ref, cls_out_ref,
    base_ref, even_ref, *odd_ref,
):
    base_kernel(class_count, core_ref, rows_ref, table_ref, wide_ref, cls_ref, base_ref)

    @pl.when(pair_ref[0] > 0)
    def _():
        lateral = outlet_lateral(0, rows_ref, mix_ref).astype(BF)
        classes = tiled(cls_out_ref[0, 0:1, :], even_ref.shape[1])
        even_ref[...] = convolve(table_ref[...], lateral, classes, class_count)
        if odd_ref:
            odd_ref[0][...] = outlet_lateral(1, rows_ref, mix_ref)


def routed_parts(class_count, top, core_ref, inflow_ref, table_ref, cls_ref):
    inflow = inflow_ref[...]
    if top:
        inflow = jnp.where(core_ref[0] == 0, jnp.zeros((), BF), inflow)
    classes = tiled(cls_ref[0:1, :], inflow.shape[1])
    return split(convolve(table_ref[...], inflow, classes, class_count))


def mine(top, pair_ref):
    return pl.when((pair_ref[0] == 0) == top)


def assemble(hours, high, low, base_ref, link_ref, members, reaches):
    lanes, width = link_ref.shape[0] // 2, link_ref.shape[1]
    flows = []
    for part in range(high.shape[1] // lanes):
        cut = slice(part * lanes, (part + 1) * lanes)
        both = jnp.concatenate([high[hours, cut], low[hours, cut]], axis=1)
        total = mm(both, link_ref[...]) + base_ref[hours, part * width : (part + 1) * width]
        flows.append(total.astype(BF))
    return jnp.concatenate(flows, axis=1).reshape(hours.stop - hours.start, members, reaches)


def early_kernel(
    class_count, top, core_ref, pair_ref, inflow_ref, base_ref, table_ref, link_ref, cls_ref,
    out_ref,
):
    hours, members, reaches = out_ref.shape

    @mine(top, pair_ref)
    def _():
        high, low = routed_parts(class_count, top, core_ref, inflow_ref, table_ref, cls_ref)
        out_ref[...] = assemble(slice(0, hours), high, low, base_ref, link_ref, members, reaches)


def late_kernel(
    class_count, top, core_ref, pair_ref, done_ref, inflow_ref, base_ref, table_ref, link_ref,
    cls_ref, *rest,
):
    out_ref, ready, sems = rest[-3:]
    hours, members, reaches = done_ref.shape

    @mine(top, pair_ref)
    def _():
        core = core_ref[0]

        def place(which):
            return pl.ds(pl.multiple_of(which * members, members), members)

        copies = [pltpu.make_async_copy(done_ref, out_ref.at[:, place(core)], sems.at[0])]
        copies[0].start()
        high, low = routed_parts(class_count, top, core_ref, inflow_ref, table_ref, cls_ref)
        for start in range(0, hours, LANES):
            part = slice(start, min(start + LANES, hours))
            ready[part] = assemble(part, high, low, base_ref, link_ref, members, reaches)
            span = pl.ds(start, part.stop - start)
            copies.append(
                pltpu.make_async_copy(
                    ready.at[span], out_ref.at[span, place(1 - core)], sems.at[len(copies)]
                )
            )
            copies[-1].start()
        for copy in copies:
            copy.wait()


def local(
    runoff, send_rows, remap_index, remap_weight, class_id, kernel_shape, kernel_rate, outlets, incidence
):
    hours, members, grid = runoff.shape
    regions = lax.axis_size("region")
    pairs = lax.axis_size("pair")
    class_count = kernel_shape.shape[0]
    reaches, columns = remap_index.shape
    recv = send_rows.size
    slot = recv // regions
    outs = outlets.size
    half = members // 2
    kap = recv * SUB
    wide = half * outs
    core = lax.axis_index("core").astype(jnp.int32)
    core_arg = core.reshape(1)
    pair = lax.axis_index("pair")
    pair_arg = pair.astype(jnp.int32).reshape(1)
    swap = [(0, 1), (1, 0)]
    anywhere = pl.BlockSpec(memory_space=pl.ANY)

    def struct(shape, dtype):
        return jax.ShapeDtypeStruct(shape, dtype)

    send = call(
        functools.partial(pack_kernel, slot),
        struct((regions, 2, half * slot, hours), BF),
        limit=FULL_VMEM,
        in_specs=[anywhere] * 2,
        out_specs=anywhere,
        scratch_shapes=[
            pltpu.VMEM((members, grid, hours), F32),
            pltpu.VMEM((1, recv), jnp.int32),
            pltpu.VMEM((regions, 2, half * slot, hours), BF),
            pltpu.SemaphoreType.DMA((3,)),
            pltpu.SemaphoreType.DMA((2,)),
        ],
    )(jnp.transpose(runoff, (1, 2, 0)), send_rows.reshape(1, recv))
    received = lax.all_to_all(
        send.reshape(regions * 2, half * slot, hours), ("region", "core"), 0, 0
    ).reshape(regions, 2, half * slot, hours)
    raw = call(
        raw_kernel,
        struct((32 + outs, reaches), F32),
        in_specs=vmem(5),
        out_specs=vmem(1)[0],
    )(
        remap_index.T,
        remap_weight.T,
        class_id.T,
        outlets.reshape(1, outs),
        incidence.reshape(outs, reaches),
    )
    other = lax.ppermute(raw, "core", swap)
    table, mix, passing, cls_out, wide_mix, link, cls_target, cls_own = call(
        functools.partial(prep_kernel, slot, columns),
        (
            struct((hours, class_count * BLOCK), BF),
            struct((2, 2 * kap, SUB * outs), BF),
            struct((2, MB * outs, MB * outs), BF),
            struct((2, 8, MB * outs), F32),
            struct((2 * kap, SUB * reaches), BF),
            struct((2 * SUB * outs, SUB * reaches), BF),
            struct((8, MB * outs), F32),
            struct((8, reaches), F32),
        ),
        in_specs=[SCALAR] + vmem(4),
        out_specs=tuple(vmem(8)),
    )(core_arg, raw, other, kernel_rate.reshape(1, class_count), kernel_shape)

    panel_shape = struct((hours, wide), BF)
    float_shape = struct((hours, wide), F32)
    panel, first, rows_send = call(
        functools.partial(head_kernel, class_count),
        (panel_shape, panel_shape, struct((regions, half * slot, hours), BF)),
        in_specs=[SCALAR] * 2 + vmem(5),
        out_specs=tuple(vmem(3)),
    )(core_arg, pair_arg, received, table, mix, passing, cls_out)
    inflow = lax.ppermute(panel, "pair", [(0, 1), (1, 0)]) if pairs > 1 else panel
    rows_other = lax.ppermute(rows_send, "core", swap)
    first_other = lax.ppermute(first, "core", swap)

    base_shape = struct((hours, half * reaches), F32)
    shapes = [base_shape, float_shape] + [float_shape] * (pairs > 2)
    base_own, even, *odd = call(
        functools.partial(base_own_kernel, class_count),
        tuple(shapes),
        in_specs=[SCALAR] * 2 + vmem(6),
        out_specs=tuple(vmem(len(shapes))),
    )(core_arg, pair_arg, received, table, wide_mix, cls_own, mix, cls_out)
    base_other = call(
        functools.partial(base_kernel, class_count),
        base_shape,
        in_specs=[SCALAR] + vmem(4),
        out_specs=vmem(1)[0],
    )(core_arg, rows_other, table, wide_mix, cls_own)


    for step in range(1, pairs - 1):
        panel = call(
            functools.partial(hop_kernel, class_count),
            panel_shape,
            in_specs=vmem(6),
            out_specs=vmem(1)[0],
        )(inflow, table, passing, cls_out, even, odd[0])
        arriving = lax.ppermute(panel, "pair", [(step, step + 1), (step + 1, step)])
        inflow = jnp.where(pair == step + 1, arriving, inflow)

    def early(top, own):
        return call(
            functools.partial(early_kernel, class_count, top),
            struct((hours, half, reaches), BF),
            in_specs=[SCALAR] * 2 + vmem(5),
            out_specs=vmem(1)[0],
        )(core_arg, pair_arg, own, base_own, table, link, cls_target)

    def late(top, done, gotten, before):
        return call(
            functools.partial(late_kernel, class_count, top),
            struct((hours, members, reaches), BF),
            in_specs=[SCALAR] * 2 + vmem(6) + [anywhere] * len(before),
            out_specs=anywhere,
            scratch_shapes=[
                pltpu.VMEM((hours, half, reaches), BF),
                pltpu.SemaphoreType.DMA((1 + -(-hours // LANES),)),
            ],
            input_output_aliases={8: 0} if before else {},
        )(core_arg, pair_arg, done, gotten, base_other, table, link, cls_target, *before)

    done_first = early(True, first)
    own, given = call(
        functools.partial(last_hop_kernel, class_count),
        (panel_shape, panel_shape),
        in_specs=[SCALAR] * 2 + vmem(5) + [anywhere] * 2,
        out_specs=tuple(vmem(2)),
    )(core_arg, pair_arg, inflow, table, passing, cls_out, even, done_first, base_other)
    gotten = lax.ppermute(given, "core", swap)
    out = late(True, done_first, first_other, [])
    return late(False, early(False, own), gotten, [out])


def solution(mesh):
    regions, orders = mesh.shape["region"], mesh.shape["order"]
    split_mesh = Mesh(mesh.devices.reshape(regions, orders // 2, 2), ("region", "pair", "core"))
    order = ("pair", "core")
    every = ("region", "pair", "core")
    return jax.shard_map(
        local,
        mesh=split_mesh,
        in_specs=(
            P(None, None, every),
            P("region", order, None),
            P(every, None),
            P(every, None),
            P(every, None),
            P(),
            P(),
            P("region", order, None),
            P("region", order, None, None),
        ),
        out_specs=P(None, None, every),
        check_vma=False,
    )
```

```python
import functools
import jax
import jax.numpy as jnp
from jax import lax
from jax.experimental import pallas as pl
from jax.experimental.pallas import tpu as pltpu
from jax.sharding import Mesh, PartitionSpec as P

BF = jnp.bfloat16
F32 = jnp.float32
MB = 8
SUB = 4
LANES = 128
SIDE = 2
BLOCK = 32
CHUNK = 256
VMEM_LIMIT = 20 * 1024 * 1024
FULL_VMEM = 56 * 1024 * 1024


def iota(shape, dim):
    return lax.broadcasted_iota(jnp.int32, shape, dim)


def mm(a, b):
    return jnp.dot(a, b, preferred_element_type=F32)


def one_hot(condition):
    return jnp.where(condition, 1.0, 0.0).astype(BF)


def split(value):
    high = value.astype(BF)
    return high, (value - high.astype(F32)).astype(BF)


def call(kernel, out_shape, limit=VMEM_LIMIT, **extra):
    return pl.pallas_call(
        kernel,
        out_shape=out_shape,
        compiler_params=pltpu.CompilerParams(vmem_limit_bytes=limit),
        cost_estimate=pl.CostEstimate(flops=1, bytes_accessed=1, transcendentals=0),
        **extra,
    )


def vmem(count):
    return [pl.BlockSpec(memory_space=pltpu.VMEM)] * count


SCALAR = pl.BlockSpec(memory_space=pltpu.SMEM)


def region_at(place, regions):
    rows = regions // SIDE
    return (place % rows) * SIDE + place // rows


def convolve(table, value, classes, class_count):
    hours, width = value.shape
    columns = []
    for begin in range(0, width, CHUNK):
        cut = slice(begin, min(begin + CHUNK, width))
        masks = [one_hot(classes[:, cut] == float(k)) for k in range(class_count)]
        total = None
        for start in range(0, hours, BLOCK):
            block = value[start : start + BLOCK, cut]
            short = BLOCK - block.shape[0]
            if short:
                block = jnp.concatenate([block, jnp.zeros((short, block.shape[1]), BF)], axis=0)
            parts = jnp.concatenate([block * mask for mask in masks], axis=0)
            added = mm(table[: hours - start], parts)
            if start == 0:
                total = added
            else:
                total = jnp.concatenate([total[:start], total[start:] + added], axis=0)
        columns.append(total)
    return jnp.concatenate(columns, axis=1)


def pack_kernel(slot, x_ref, rows_ref, send_ref, held, rows_held, ready, arrived, sent):
    members, grid, hours = x_ref.shape
    blocks = members // MB
    regions = send_ref.shape[0]
    per = MB * slot

    half = members // 2

    def fetch(core):
        place = pl.ds(core * half, half)
        return pltpu.make_async_copy(x_ref.at[place], held.at[place], arrived.at[core])

    def deliver(core):
        return pltpu.make_async_copy(ready.at[:, core], send_ref.at[:, core], sent.at[core])

    first = pltpu.make_async_copy(rows_ref, rows_held, arrived.at[2])
    first.start()
    for core in range(2):
        fetch(core).start()
    first.wait()
    count = regions * per
    recv = rows_ref.shape[1]
    row = iota((count, recv), 0)
    wanted = region_at(row // per, regions) * slot + row % slot
    rows = rows_held[...].astype(F32)
    chosen = jnp.sum(jnp.where(iota((count, recv), 1) == wanted, rows, 0.0), axis=1, keepdims=True)
    lane = iota((count, MB * grid), 1)
    member = (iota((count, MB * grid), 0) // slot) % MB
    select = one_hot((lane // grid == member) & ((lane % grid).astype(F32) == chosen))
    for core in range(2):
        fetch(core).wait()
        for inner in range(blocks // 2):
            begin = core * half + inner * MB
            x = held[begin : begin + MB].reshape(MB * grid, hours).astype(BF)
            y = mm(select, x).astype(BF).reshape(regions, per, hours)
            ready[:, core, inner * per : (inner + 1) * per, :] = y
        deliver(core).start()
    for core in range(2):
        deliver(core).wait()


def raw_kernel(idx_ref, w_ref, cls_ref, outl_ref, inc_ref, raw_ref):
    raw_ref[...] = jnp.zeros_like(raw_ref)
    raw_ref[0 : idx_ref.shape[0], :] = idx_ref[...].astype(F32)
    raw_ref[8 : 8 + w_ref.shape[0], :] = w_ref[...]
    raw_ref[16:17, :] = cls_ref[...].astype(F32)
    raw_ref[24:25, 0 : outl_ref.shape[1]] = outl_ref[...].astype(F32)
    raw_ref[32:, :] = inc_ref[...].astype(F32)


def prep_kernel(
    slot, columns, core_ref, own_ref, other_ref, rate_ref, shape_ref,
    table_ref, mix_ref, pass_ref, cls_out_ref, wide_ref, link_ref, cls_target_ref, cls_own_ref,
):
    core = core_ref[0]
    class_count, hours = shape_ref.shape
    padded = -(-hours // LANES) * LANES
    kap = mix_ref.shape[1] // 2
    recv = kap // SUB
    per = SUB * slot
    outs = own_ref.shape[0] - 32
    reaches = own_ref.shape[1]
    wide = MB * outs
    narrow = SUB * outs

    lag = iota((class_count, hours), 1).astype(F32)
    square = (class_count, class_count)
    rate = jnp.where(iota(square, 0) == iota(square, 1), rate_ref[...], 0.0)
    rate = jnp.sum(rate, axis=1, keepdims=True)
    hydro = (rate * shape_ref[...] * jnp.exp(-rate * lag)).astype(BF)
    reverse = one_hot((iota((hours, padded), 0) + iota((hours, padded), 1)) % padded == 0)
    turned = mm(hydro, reverse)
    later = iota((padded, BLOCK), 1) <= iota((padded, BLOCK), 0)
    for k in range(class_count):
        rolled = pltpu.roll(
            jnp.broadcast_to(turned[k : k + 1, :], (padded, padded)), 0, 1, stride=1, stride_axis=0
        )
        rolled = jnp.where(later, rolled[:, :BLOCK], 0.0)
        table_ref[:, k * BLOCK : (k + 1) * BLOCK] = rolled[:hours].astype(BF)

    row_p = iota((kap, recv), 0)
    spot = region_at(row_p // per, recv // slot) * slot + row_p % slot
    expand = one_hot(spot == iota((kap, recv), 1))

    def owner(width):
        return (iota((kap, width), 0) // slot) % SUB

    def tile(width):
        return one_hot(iota((outs, width), 0) == iota((outs, width), 1) % outs)

    def weights(raw):
        total = jnp.zeros((recv, reaches), F32)
        for j in range(columns):
            hit = iota((recv, reaches), 0).astype(F32) == raw[j : j + 1, :]
            total = total + jnp.where(hit, raw[8 + j : 9 + j, :], 0.0)
        return split(total)

    own = own_ref[...]
    for level in range(2):
        raw = jnp.where(core == level, own, other_ref[...])
        lanes = mm(raw[24:32, :outs].astype(BF), tile(wide))[0:1, :]
        pick = one_hot(iota((reaches, wide), 0).astype(F32) == lanes)
        for part, weight in enumerate(weights(raw)):
            spread = mm(expand, mm(weight, pick[:, :narrow]).astype(BF))
            spread = jnp.where(owner(narrow) == iota((kap, narrow), 1) // outs, spread, 0.0)
            mix_ref[level, part * kap : (part + 1) * kap] = spread.astype(BF)
        moved = jnp.concatenate([mm(raw[32:, :].astype(BF), pick)] * MB, axis=0)
        here = iota((wide, wide), 0) // outs == iota((wide, wide), 1) // outs
        pass_ref[level] = jnp.where(here, moved, 0.0).astype(BF)
        cls_out_ref[level] = mm(raw[16:24, :].astype(BF), pick)

    for part, weight in enumerate(weights(own)):
        spread = mm(expand, weight)
        for m in range(SUB):
            piece = jnp.where(owner(reaches) == m, spread, 0.0).astype(BF)
            wide_ref[part * kap : (part + 1) * kap, m * reaches : (m + 1) * reaches] = piece
    cls_own_ref[...] = own[16:24, :]
    cls_target_ref[...] = lax.dot_general(
        own[16:24, :].astype(BF),
        jnp.concatenate([own[32:, :]] * MB, axis=0).astype(BF),
        (((1,), (1,)), ((), ())),
        preferred_element_type=F32,
    )
    stacked = jnp.concatenate([own[32:, :]] * SUB, axis=0)
    who = iota((narrow, reaches), 0) // outs
    for m in range(SUB):
        piece = jnp.where(who == m, stacked, 0.0).astype(BF)
        for part in range(2):
            link_ref[part * narrow : (part + 1) * narrow, m * reaches : (m + 1) * reaches] = piece


def side_by_side(parts, right):
    product = mm(jnp.concatenate(parts, axis=0), right)
    count = parts[0].shape[0]
    rows = [product[i * count : (i + 1) * count] for i in range(len(parts))]
    return jnp.concatenate(rows, axis=1)


def twice(rows_ref, sub, size):
    rows = rows_ref[:, sub * size : (sub + 1) * size, :]
    rows = rows.reshape(rows.shape[0] * size, rows.shape[2]).T
    return jnp.concatenate([rows, rows], axis=1)


def pass_on(panel, pass_matrix):
    width = pass_matrix.shape[0]
    parts = [
        mm(panel[:, start : start + width], pass_matrix).astype(BF)
        for start in range(0, panel.shape[1], width)
    ]
    return jnp.concatenate(parts, axis=1)


def tiled(classes, width):
    return jnp.concatenate([classes] * (width // classes.shape[1]), axis=1)


def outlet_lateral(level, rows_ref, mix_ref):
    regions, _, total, _ = rows_ref.shape
    size = mix_ref.shape[1] // 2 // regions
    rows_ref = rows_ref.at[:, level]
    parts = [mm(twice(rows_ref, sub, size), mix_ref[level]) for sub in range(total // size)]
    return jnp.concatenate(parts, axis=1)


def head_kernel(
    class_count, core_ref, pair_ref, rows_ref, table_ref, mix_ref, pass_ref, cls_ref,
    panel_ref, first_ref, send_ref,
):
    send_ref[...] = jnp.where(core_ref[0] == 0, rows_ref[:, 1], rows_ref[:, 0])

    @pl.when(pair_ref[0] == 0)
    def _():
        wide = panel_ref.shape[1]
        classes = [tiled(cls_ref[level, 0:1, :], wide) for level in range(2)]
        lateral = [outlet_lateral(level, rows_ref, mix_ref) for level in range(2)]
        first = convolve(table_ref[...], lateral[0].astype(BF), classes[0], class_count).astype(BF)
        first_ref[...] = first
        inflow = (lateral[1] + pass_on(first, pass_ref[1]).astype(F32)).astype(BF)
        panel_ref[...] = convolve(table_ref[...], inflow, classes[1], class_count).astype(BF)


def hop_kernel(class_count, inflow_ref, table_ref, pass_ref, cls_ref, even_ref, odd_ref, panel_ref):
    classes = [tiled(cls_ref[level, 0:1, :], even_ref.shape[1]) for level in range(2)]
    moved = pass_on(inflow_ref[...], pass_ref[0])
    even = even_ref[...] + convolve(table_ref[...], moved, classes[0], class_count)
    moved = odd_ref[...] + pass_on(even.astype(BF), pass_ref[1]).astype(F32)
    panel_ref[...] = convolve(table_ref[...], moved.astype(BF), classes[1], class_count).astype(BF)


def last_hop_kernel(class_count, core_ref, pair_ref, inflow_ref, table_ref, pass_ref, cls_ref, even_ref, *rest):
    own_ref, send_ref = rest[-2:]

    @pl.when(pair_ref[0] > 0)
    def _():
        arrived = inflow_ref[...]
        classes = tiled(cls_ref[0, 0:1, :], even_ref.shape[1])
        moved = pass_on(arrived, pass_ref[0])
        even = even_ref[...] + convolve(table_ref[...], moved, classes, class_count)
        even = even.astype(BF)
        first = core_ref[0] == 0
        own_ref[...] = jnp.where(first, arrived, even)
        send_ref[...] = jnp.where(first, even, arrived)


def base_kernel(class_count, core_ref, rows_ref, table_ref, wide_ref, cls_ref, base_ref):
    if len(rows_ref.shape) == 4:
        rows_ref = rows_ref.at[:, core_ref[0]]
    regions, total, _ = rows_ref.shape
    size = wide_ref.shape[0] // 2 // regions
    width = wide_ref.shape[1]
    parts = [twice(rows_ref, sub, size) for sub in range(total // size)]
    classes = tiled(cls_ref[0:1, :], width)
    lateral = side_by_side(parts, wide_ref[...]).astype(BF)
    for start in range(0, base_ref.shape[1], width):
        base_ref[:, start : start + width] = convolve(
            table_ref[...], lateral[:, start : start + width], classes, class_count
        )


def base_own_kernel(
    class_count, core_ref, pair_ref, rows_ref, table_ref, wide_ref, cls_ref, mix_ref, cls_out_ref,
    base_ref, even_ref, *odd_ref,
):
    base_kernel(class_count, core_ref, rows_ref, table_ref, wide_ref, cls_ref, base_ref)

    @pl.when(pair_ref[0] > 0)
    def _():
        lateral = outlet_lateral(0, rows_ref, mix_ref).astype(BF)
        classes = tiled(cls_out_ref[0, 0:1, :], even_ref.shape[1])
        even_ref[...] = convolve(table_ref[...], lateral, classes, class_count)
        if odd_ref:
            odd_ref[0][...] = outlet_lateral(1, rows_ref, mix_ref)


def routed_parts(class_count, top, core_ref, inflow_ref, table_ref, cls_ref):
    inflow = inflow_ref[...]
    if top:
        inflow = jnp.where(core_ref[0] == 0, jnp.zeros((), BF), inflow)
    classes = tiled(cls_ref[0:1, :], inflow.shape[1])
    return split(convolve(table_ref[...], inflow, classes, class_count))


def mine(top, pair_ref):
    return pl.when((pair_ref[0] == 0) == top)


def assemble(hours, high, low, base_ref, link_ref, members, reaches):
    lanes, width = link_ref.shape[0] // 2, link_ref.shape[1]
    flows = []
    for part in range(high.shape[1] // lanes):
        cut = slice(part * lanes, (part + 1) * lanes)
        both = jnp.concatenate([high[hours, cut], low[hours, cut]], axis=1)
        total = mm(both, link_ref[...]) + base_ref[hours, part * width : (part + 1) * width]
        flows.append(total.astype(BF))
    return jnp.concatenate(flows, axis=1).reshape(hours.stop - hours.start, members, reaches)


def early_kernel(
    class_count, top, core_ref, pair_ref, inflow_ref, base_ref, table_ref, link_ref, cls_ref,
    out_ref,
):
    hours, members, reaches = out_ref.shape

    @mine(top, pair_ref)
    def _():
        high, low = routed_parts(class_count, top, core_ref, inflow_ref, table_ref, cls_ref)
        out_ref[...] = assemble(slice(0, hours), high, low, base_ref, link_ref, members, reaches)


def late_kernel(
    class_count, top, core_ref, pair_ref, done_ref, inflow_ref, base_ref, table_ref, link_ref,
    cls_ref, *rest,
):
    out_ref, ready, sems = rest[-3:]
    hours, members, reaches = done_ref.shape

    @mine(top, pair_ref)
    def _():
        core = core_ref[0]

        def place(which):
            return pl.ds(pl.multiple_of(which * members, members), members)

        copies = [pltpu.make_async_copy(done_ref, out_ref.at[:, place(core)], sems.at[0])]
        copies[0].start()
        high, low = routed_parts(class_count, top, core_ref, inflow_ref, table_ref, cls_ref)
        for start in range(0, hours, LANES):
            part = slice(start, min(start + LANES, hours))
            ready[part] = assemble(part, high, low, base_ref, link_ref, members, reaches)
            span = pl.ds(start, part.stop - start)
            copies.append(
                pltpu.make_async_copy(
                    ready.at[span], out_ref.at[span, place(1 - core)], sems.at[len(copies)]
                )
            )
            copies[-1].start()
        for copy in copies:
            copy.wait()


def local(
    runoff, send_rows, remap_index, remap_weight, class_id, kernel_shape, kernel_rate, outlets, incidence
):
    hours, members, grid = runoff.shape
    regions = lax.axis_size("row") * lax.axis_size("side")
    pairs = lax.axis_size("pair")
    class_count = kernel_shape.shape[0]
    reaches, columns = remap_index.shape
    recv = send_rows.size
    slot = recv // regions
    outs = outlets.size
    half = members // 2
    kap = recv * SUB
    wide = half * outs
    core = lax.axis_index("core").astype(jnp.int32)
    core_arg = core.reshape(1)
    pair = lax.axis_index("pair")
    pair_arg = pair.astype(jnp.int32).reshape(1)
    swap = [(0, 1), (1, 0)]
    anywhere = pl.BlockSpec(memory_space=pl.ANY)

    def struct(shape, dtype):
        return jax.ShapeDtypeStruct(shape, dtype)

    send = call(
        functools.partial(pack_kernel, slot),
        struct((regions, 2, half * slot, hours), BF),
        limit=FULL_VMEM,
        in_specs=[anywhere] * 2,
        out_specs=anywhere,
        scratch_shapes=[
            pltpu.VMEM((members, grid, hours), F32),
            pltpu.VMEM((1, recv), jnp.int32),
            pltpu.VMEM((regions, 2, half * slot, hours), BF),
            pltpu.SemaphoreType.DMA((3,)),
            pltpu.SemaphoreType.DMA((2,)),
        ],
    )(jnp.transpose(runoff, (1, 2, 0)), send_rows.reshape(1, recv))
    received = lax.all_to_all(
        send.reshape(regions * 2, half * slot, hours), ("side", "row", "core"), 0, 0
    ).reshape(regions, 2, half * slot, hours)
    raw = call(
        raw_kernel,
        struct((32 + outs, reaches), F32),
        in_specs=vmem(5),
        out_specs=vmem(1)[0],
    )(
        remap_index.T,
        remap_weight.T,
        class_id.T,
        outlets.reshape(1, outs),
        incidence.reshape(outs, reaches),
    )
    other = lax.ppermute(raw, "core", swap)
    table, mix, passing, cls_out, wide_mix, link, cls_target, cls_own = call(
        functools.partial(prep_kernel, slot, columns),
        (
            struct((hours, class_count * BLOCK), BF),
            struct((2, 2 * kap, SUB * outs), BF),
            struct((2, MB * outs, MB * outs), BF),
            struct((2, 8, MB * outs), F32),
            struct((2 * kap, SUB * reaches), BF),
            struct((2 * SUB * outs, SUB * reaches), BF),
            struct((8, MB * outs), F32),
            struct((8, reaches), F32),
        ),
        in_specs=[SCALAR] + vmem(4),
        out_specs=tuple(vmem(8)),
    )(core_arg, raw, other, kernel_rate.reshape(1, class_count), kernel_shape)

    panel_shape = struct((hours, wide), BF)
    float_shape = struct((hours, wide), F32)
    panel, first, rows_send = call(
        functools.partial(head_kernel, class_count),
        (panel_shape, panel_shape, struct((regions, half * slot, hours), BF)),
        in_specs=[SCALAR] * 2 + vmem(5),
        out_specs=tuple(vmem(3)),
    )(core_arg, pair_arg, received, table, mix, passing, cls_out)
    inflow = lax.ppermute(panel, "pair", [(0, 1), (1, 0)]) if pairs > 1 else panel
    rows_other = lax.ppermute(rows_send, "core", swap)
    first_other = lax.ppermute(first, "core", swap)

    base_shape = struct((hours, half * reaches), F32)
    shapes = [base_shape, float_shape] + [float_shape] * (pairs > 2)
    base_own, even, *odd = call(
        functools.partial(base_own_kernel, class_count),
        tuple(shapes),
        in_specs=[SCALAR] * 2 + vmem(6),
        out_specs=tuple(vmem(len(shapes))),
    )(core_arg, pair_arg, received, table, wide_mix, cls_own, mix, cls_out)
    base_other = call(
        functools.partial(base_kernel, class_count),
        base_shape,
        in_specs=[SCALAR] + vmem(4),
        out_specs=vmem(1)[0],
    )(core_arg, rows_other, table, wide_mix, cls_own)


    for step in range(1, pairs - 1):
        panel = call(
            functools.partial(hop_kernel, class_count),
            panel_shape,
            in_specs=vmem(6),
            out_specs=vmem(1)[0],
        )(inflow, table, passing, cls_out, even, odd[0])
        arriving = lax.ppermute(panel, "pair", [(step, step + 1), (step + 1, step)])
        inflow = jnp.where(pair == step + 1, arriving, inflow)

    def early(top, own):
        return call(
            functools.partial(early_kernel, class_count, top),
            struct((hours, half, reaches), BF),
            in_specs=[SCALAR] * 2 + vmem(5),
            out_specs=vmem(1)[0],
        )(core_arg, pair_arg, own, base_own, table, link, cls_target)

    def late(top, done, gotten, before):
        return call(
            functools.partial(late_kernel, class_count, top),
            struct((hours, members, reaches), BF),
            in_specs=[SCALAR] * 2 + vmem(6) + [anywhere] * len(before),
            out_specs=anywhere,
            scratch_shapes=[
                pltpu.VMEM((hours, half, reaches), BF),
                pltpu.SemaphoreType.DMA((1 + -(-hours // LANES),)),
            ],
            input_output_aliases={8: 0} if before else {},
        )(core_arg, pair_arg, done, gotten, base_other, table, link, cls_target, *before)

    done_first = early(True, first)
    own, given = call(
        functools.partial(last_hop_kernel, class_count),
        (panel_shape, panel_shape),
        in_specs=[SCALAR] * 2 + vmem(5) + [anywhere] * 2,
        out_specs=tuple(vmem(2)),
    )(core_arg, pair_arg, inflow, table, passing, cls_out, even, done_first, base_other)
    gotten = lax.ppermute(given, "core", swap)
    out = late(True, done_first, first_other, [])
    return late(False, early(False, own), gotten, [out])


def solution(mesh):
    regions, orders = mesh.shape["region"], mesh.shape["order"]
    split_mesh = Mesh(
        mesh.devices.reshape(regions // SIDE, SIDE, orders // 2, 2), ("row", "side", "pair", "core")
    )
    region = ("row", "side")
    order = ("pair", "core")
    every = region + order
    return jax.shard_map(
        local,
        mesh=split_mesh,
        in_specs=(
            P(None, None, every),
            P(region, order, None),
            P(every, None),
            P(every, None),
            P(every, None),
            P(),
            P(),
            P(region, order, None),
            P(region, order, None, None),
        ),
        out_specs=P(None, None, every),
        check_vma=False,
    )
```

```python
import functools
import jax
import jax.numpy as jnp
from jax import lax
from jax.experimental import pallas as pl
from jax.experimental.pallas import tpu as pltpu
from jax.sharding import Mesh, PartitionSpec as P

BF = jnp.bfloat16
F32 = jnp.float32
MB = 8
SUB = 4
LANES = 128
SIDE = 2
BLOCK = 32
CHUNK = 256
VMEM_LIMIT = 20 * 1024 * 1024
FULL_VMEM = 56 * 1024 * 1024


def iota(shape, dim):
    return lax.broadcasted_iota(jnp.int32, shape, dim)


def mm(a, b):
    return jnp.dot(a, b, preferred_element_type=F32)


def one_hot(condition):
    return jnp.where(condition, 1.0, 0.0).astype(BF)


def split(value):
    high = value.astype(BF)
    return high, (value - high.astype(F32)).astype(BF)


def call(kernel, out_shape, limit=VMEM_LIMIT, **extra):
    return pl.pallas_call(
        kernel,
        out_shape=out_shape,
        compiler_params=pltpu.CompilerParams(vmem_limit_bytes=limit),
        cost_estimate=pl.CostEstimate(flops=1, bytes_accessed=1, transcendentals=0),
        **extra,
    )


def vmem(count):
    return [pl.BlockSpec(memory_space=pltpu.VMEM)] * count


SCALAR = pl.BlockSpec(memory_space=pltpu.SMEM)


def region_at(place, regions):
    rows = regions // SIDE
    return (place % rows) * SIDE + place // rows


def convolve(table, value, classes, class_count):
    hours, width = value.shape
    columns = []
    for begin in range(0, width, CHUNK):
        cut = slice(begin, min(begin + CHUNK, width))
        masks = [one_hot(classes[:, cut] == float(k)) for k in range(class_count)]
        total = None
        for start in range(0, hours, BLOCK):
            block = value[start : start + BLOCK, cut]
            short = BLOCK - block.shape[0]
            if short:
                block = jnp.concatenate([block, jnp.zeros((short, block.shape[1]), BF)], axis=0)
            parts = jnp.concatenate([block * mask for mask in masks], axis=0)
            added = mm(table[: hours - start], parts)
            if start == 0:
                total = added
            else:
                total = jnp.concatenate([total[:start], total[start:] + added], axis=0)
        columns.append(total)
    return jnp.concatenate(columns, axis=1)


def pack_kernel(slot, x_ref, rows_ref, send_ref, held, rows_held, ready, arrived, sent):
    members, grid, hours = x_ref.shape
    blocks = members // MB
    regions = send_ref.shape[0]
    per = MB * slot

    half = members // 2

    def fetch(core):
        place = pl.ds(core * half, half)
        return pltpu.make_async_copy(x_ref.at[place], held.at[place], arrived.at[core])

    def deliver(core):
        return pltpu.make_async_copy(ready.at[:, core], send_ref.at[:, core], sent.at[core])

    first = pltpu.make_async_copy(rows_ref, rows_held, arrived.at[2])
    first.start()
    for core in range(2):
        fetch(core).start()
    first.wait()
    count = regions * per
    recv = rows_ref.shape[1]
    row = iota((count, recv), 0)
    wanted = region_at(row // per, regions) * slot + row % slot
    rows = rows_held[...].astype(F32)
    chosen = jnp.sum(jnp.where(iota((count, recv), 1) == wanted, rows, 0.0), axis=1, keepdims=True)
    lane = iota((count, MB * grid), 1)
    member = (iota((count, MB * grid), 0) // slot) % MB
    select = one_hot((lane // grid == member) & ((lane % grid).astype(F32) == chosen))
    for core in range(2):
        fetch(core).wait()
        for inner in range(blocks // 2):
            begin = core * half + inner * MB
            x = held[begin : begin + MB].reshape(MB * grid, hours).astype(BF)
            y = mm(select, x).astype(BF).reshape(regions, per, hours)
            ready[:, core, inner * per : (inner + 1) * per, :] = y
        deliver(core).start()
    for core in range(2):
        deliver(core).wait()


def raw_kernel(idx_ref, w_ref, cls_ref, outl_ref, inc_ref, raw_ref):
    raw_ref[...] = jnp.zeros_like(raw_ref)
    raw_ref[0 : idx_ref.shape[0], :] = idx_ref[...].astype(F32)
    raw_ref[8 : 8 + w_ref.shape[0], :] = w_ref[...]
    raw_ref[16:17, :] = cls_ref[...].astype(F32)
    raw_ref[24:25, 0 : outl_ref.shape[1]] = outl_ref[...].astype(F32)
    raw_ref[32:, :] = inc_ref[...].astype(F32)


def prep_kernel(
    slot, columns, core_ref, own_ref, other_ref, rate_ref, shape_ref,
    table_ref, mix_ref, pass_ref, cls_out_ref, wide_ref, link_ref, cls_target_ref, cls_own_ref,
):
    core = core_ref[0]
    class_count, hours = shape_ref.shape
    padded = -(-hours // LANES) * LANES
    kap = mix_ref.shape[1] // 2
    recv = kap // SUB
    per = SUB * slot
    outs = own_ref.shape[0] - 32
    reaches = own_ref.shape[1]
    wide = MB * outs
    narrow = SUB * outs

    lag = iota((class_count, hours), 1).astype(F32)
    square = (class_count, class_count)
    rate = jnp.where(iota(square, 0) == iota(square, 1), rate_ref[...], 0.0)
    rate = jnp.sum(rate, axis=1, keepdims=True)
    hydro = (rate * shape_ref[...] * jnp.exp(-rate * lag)).astype(BF)
    reverse = one_hot((iota((hours, padded), 0) + iota((hours, padded), 1)) % padded == 0)
    turned = mm(hydro, reverse)
    later = iota((padded, BLOCK), 1) <= iota((padded, BLOCK), 0)
    for k in range(class_count):
        rolled = pltpu.roll(
            jnp.broadcast_to(turned[k : k + 1, :], (padded, padded)), 0, 1, stride=1, stride_axis=0
        )
        rolled = jnp.where(later, rolled[:, :BLOCK], 0.0)
        table_ref[:, k * BLOCK : (k + 1) * BLOCK] = rolled[:hours].astype(BF)

    row_p = iota((kap, recv), 0)
    spot = region_at(row_p // per, recv // slot) * slot + row_p % slot
    expand = one_hot(spot == iota((kap, recv), 1))

    def owner(width):
        return (iota((kap, width), 0) // slot) % SUB

    def tile(width):
        return one_hot(iota((outs, width), 0) == iota((outs, width), 1) % outs)

    def weights(raw):
        total = jnp.zeros((recv, reaches), F32)
        for j in range(columns):
            hit = iota((recv, reaches), 0).astype(F32) == raw[j : j + 1, :]
            total = total + jnp.where(hit, raw[8 + j : 9 + j, :], 0.0)
        return split(total)

    own = own_ref[...]
    for level in range(2):
        raw = jnp.where(core == level, own, other_ref[...])
        lanes = mm(raw[24:32, :outs].astype(BF), tile(wide))[0:1, :]
        pick = one_hot(iota((reaches, wide), 0).astype(F32) == lanes)
        for part, weight in enumerate(weights(raw)):
            spread = mm(expand, mm(weight, pick[:, :narrow]).astype(BF))
            spread = jnp.where(owner(narrow) == iota((kap, narrow), 1) // outs, spread, 0.0)
            mix_ref[level, part * kap : (part + 1) * kap] = spread.astype(BF)
        moved = jnp.concatenate([mm(raw[32:, :].astype(BF), pick)] * MB, axis=0)
        here = iota((wide, wide), 0) // outs == iota((wide, wide), 1) // outs
        pass_ref[level] = jnp.where(here, moved, 0.0).astype(BF)
        cls_out_ref[level] = mm(raw[16:24, :].astype(BF), pick)

    for part, weight in enumerate(weights(own)):
        spread = mm(expand, weight)
        for m in range(SUB):
            piece = jnp.where(owner(reaches) == m, spread, 0.0).astype(BF)
            wide_ref[part * kap : (part + 1) * kap, m * reaches : (m + 1) * reaches] = piece
    cls_own_ref[...] = own[16:24, :]
    cls_target_ref[...] = lax.dot_general(
        own[16:24, :].astype(BF),
        jnp.concatenate([own[32:, :]] * MB, axis=0).astype(BF),
        (((1,), (1,)), ((), ())),
        preferred_element_type=F32,
    )
    stacked = jnp.concatenate([own[32:, :]] * SUB, axis=0)
    who = iota((narrow, reaches), 0) // outs
    for m in range(SUB):
        piece = jnp.where(who == m, stacked, 0.0).astype(BF)
        for part in range(2):
            link_ref[part * narrow : (part + 1) * narrow, m * reaches : (m + 1) * reaches] = piece


def side_by_side(parts, right):
    product = mm(jnp.concatenate(parts, axis=0), right)
    count = parts[0].shape[0]
    rows = [product[i * count : (i + 1) * count] for i in range(len(parts))]
    return jnp.concatenate(rows, axis=1)


def twice(rows_ref, sub, size):
    rows = rows_ref[:, sub * size : (sub + 1) * size, :]
    rows = rows.reshape(rows.shape[0] * size, rows.shape[2]).T
    return jnp.concatenate([rows, rows], axis=1)


def pass_on(panel, pass_matrix):
    width = pass_matrix.shape[0]
    parts = [
        mm(panel[:, start : start + width], pass_matrix).astype(BF)
        for start in range(0, panel.shape[1], width)
    ]
    return jnp.concatenate(parts, axis=1)


def tiled(classes, width):
    return jnp.concatenate([classes] * (width // classes.shape[1]), axis=1)


def outlet_lateral(level, rows_ref, mix_ref):
    regions, _, total, _ = rows_ref.shape
    size = mix_ref.shape[1] // 2 // regions
    rows_ref = rows_ref.at[:, level]
    parts = [mm(twice(rows_ref, sub, size), mix_ref[level]) for sub in range(total // size)]
    return jnp.concatenate(parts, axis=1)


def head_kernel(
    class_count, core_ref, pair_ref, rows_ref, table_ref, mix_ref, pass_ref, cls_ref,
    panel_ref, first_ref, send_ref,
):
    send_ref[...] = jnp.where(core_ref[0] == 0, rows_ref[:, 1], rows_ref[:, 0])

    @pl.when(pair_ref[0] == 0)
    def _():
        wide = panel_ref.shape[1]
        classes = [tiled(cls_ref[level, 0:1, :], wide) for level in range(2)]
        lateral = [outlet_lateral(level, rows_ref, mix_ref) for level in range(2)]
        first = convolve(table_ref[...], lateral[0].astype(BF), classes[0], class_count).astype(BF)
        first_ref[...] = first
        inflow = (lateral[1] + pass_on(first, pass_ref[1]).astype(F32)).astype(BF)
        panel_ref[...] = convolve(table_ref[...], inflow, classes[1], class_count).astype(BF)


def hop_kernel(class_count, inflow_ref, table_ref, pass_ref, cls_ref, even_ref, odd_ref, panel_ref):
    classes = [tiled(cls_ref[level, 0:1, :], even_ref.shape[1]) for level in range(2)]
    moved = pass_on(inflow_ref[...], pass_ref[0])
    even = even_ref[...] + convolve(table_ref[...], moved, classes[0], class_count)
    moved = odd_ref[...] + pass_on(even.astype(BF), pass_ref[1]).astype(F32)
    panel_ref[...] = convolve(table_ref[...], moved.astype(BF), classes[1], class_count).astype(BF)


def last_hop_kernel(class_count, core_ref, pair_ref, inflow_ref, table_ref, pass_ref, cls_ref, even_ref, *rest):
    own_ref, send_ref = rest[-2:]

    @pl.when(pair_ref[0] > 0)
    def _():
        arrived = inflow_ref[...]
        classes = tiled(cls_ref[0, 0:1, :], even_ref.shape[1])
        moved = pass_on(arrived, pass_ref[0])
        even = even_ref[...] + convolve(table_ref[...], moved, classes, class_count)
        even = even.astype(BF)
        first = core_ref[0] == 0
        own_ref[...] = jnp.where(first, arrived, even)
        send_ref[...] = jnp.where(first, even, arrived)


def base_kernel(class_count, core_ref, rows_ref, table_ref, wide_ref, cls_ref, base_ref):
    if len(rows_ref.shape) == 4:
        rows_ref = rows_ref.at[:, core_ref[0]]
    regions, total, _ = rows_ref.shape
    size = wide_ref.shape[0] // 2 // regions
    width = wide_ref.shape[1]
    parts = [twice(rows_ref, sub, size) for sub in range(total // size)]
    classes = tiled(cls_ref[0:1, :], width)
    lateral = side_by_side(parts, wide_ref[...]).astype(BF)
    for start in range(0, base_ref.shape[1], width):
        base_ref[:, start : start + width] = convolve(
            table_ref[...], lateral[:, start : start + width], classes, class_count
        )


def base_own_kernel(
    class_count, core_ref, pair_ref, rows_ref, table_ref, wide_ref, cls_ref, mix_ref, cls_out_ref,
    base_ref, even_ref, *odd_ref,
):
    base_kernel(class_count, core_ref, rows_ref, table_ref, wide_ref, cls_ref, base_ref)

    @pl.when(pair_ref[0] > 0)
    def _():
        lateral = outlet_lateral(0, rows_ref, mix_ref).astype(BF)
        classes = tiled(cls_out_ref[0, 0:1, :], even_ref.shape[1])
        even_ref[...] = convolve(table_ref[...], lateral, classes, class_count)
        if odd_ref:
            odd_ref[0][...] = outlet_lateral(1, rows_ref, mix_ref)


def routed_parts(class_count, top, core_ref, inflow_ref, table_ref, cls_ref):
    inflow = inflow_ref[...]
    if top:
        inflow = jnp.where(core_ref[0] == 0, jnp.zeros((), BF), inflow)
    classes = tiled(cls_ref[0:1, :], inflow.shape[1])
    return split(convolve(table_ref[...], inflow, classes, class_count))


def mine(top, pair_ref):
    return pl.when((pair_ref[0] == 0) == top)


def assemble(hours, high, low, base_ref, link_ref, members, reaches):
    lanes, width = link_ref.shape[0] // 2, link_ref.shape[1]
    flows = []
    for part in range(high.shape[1] // lanes):
        cut = slice(part * lanes, (part + 1) * lanes)
        both = jnp.concatenate([high[hours, cut], low[hours, cut]], axis=1)
        total = mm(both, link_ref[...]) + base_ref[hours, part * width : (part + 1) * width]
        flows.append(total.astype(BF))
    return jnp.concatenate(flows, axis=1).reshape(hours.stop - hours.start, members, reaches)


def early_kernel(
    class_count, top, core_ref, pair_ref, inflow_ref, base_ref, table_ref, link_ref, cls_ref,
    out_ref,
):
    hours, members, reaches = out_ref.shape

    @mine(top, pair_ref)
    def _():
        high, low = routed_parts(class_count, top, core_ref, inflow_ref, table_ref, cls_ref)
        out_ref[...] = assemble(slice(0, hours), high, low, base_ref, link_ref, members, reaches)


def other_kernel(
    class_count, core_ref, pair_ref, rows_ref, table_ref, wide_ref, cls_ref, inflow_ref, base_own_ref,
    link_ref, cls_target_ref, base_ref, done_ref,
):
    base_kernel(class_count, core_ref, rows_ref, table_ref, wide_ref, cls_ref, base_ref)
    early_kernel(
        class_count, True, core_ref, pair_ref, inflow_ref, base_own_ref, table_ref, link_ref,
        cls_target_ref, done_ref,
    )


def late_kernel(
    class_count, top, core_ref, pair_ref, done_ref, inflow_ref, base_ref, table_ref, link_ref,
    cls_ref, *rest,
):
    out_ref, ready, sems = rest[-3:]
    hours, members, reaches = done_ref.shape

    @mine(top, pair_ref)
    def _():
        core = core_ref[0]

        def place(which):
            return pl.ds(pl.multiple_of(which * members, members), members)

        copies = [pltpu.make_async_copy(done_ref, out_ref.at[:, place(core)], sems.at[0])]
        copies[0].start()
        high, low = routed_parts(class_count, top, core_ref, inflow_ref, table_ref, cls_ref)
        for start in range(0, hours, LANES):
            part = slice(start, min(start + LANES, hours))
            ready[part] = assemble(part, high, low, base_ref, link_ref, members, reaches)
            span = pl.ds(start, part.stop - start)
            copies.append(
                pltpu.make_async_copy(
                    ready.at[span], out_ref.at[span, place(1 - core)], sems.at[len(copies)]
                )
            )
            copies[-1].start()
        for copy in copies:
            copy.wait()


def local(
    runoff, send_rows, remap_index, remap_weight, class_id, kernel_shape, kernel_rate, outlets, incidence
):
    hours, members, grid = runoff.shape
    regions = lax.axis_size("row") * lax.axis_size("side")
    pairs = lax.axis_size("pair")
    class_count = kernel_shape.shape[0]
    reaches, columns = remap_index.shape
    recv = send_rows.size
    slot = recv // regions
    outs = outlets.size
    half = members // 2
    kap = recv * SUB
    wide = half * outs
    core = lax.axis_index("core").astype(jnp.int32)
    core_arg = core.reshape(1)
    pair = lax.axis_index("pair")
    pair_arg = pair.astype(jnp.int32).reshape(1)
    swap = [(0, 1), (1, 0)]
    anywhere = pl.BlockSpec(memory_space=pl.ANY)

    def struct(shape, dtype):
        return jax.ShapeDtypeStruct(shape, dtype)

    send = call(
        functools.partial(pack_kernel, slot),
        struct((regions, 2, half * slot, hours), BF),
        limit=FULL_VMEM,
        in_specs=[anywhere] * 2,
        out_specs=anywhere,
        scratch_shapes=[
            pltpu.VMEM((members, grid, hours), F32),
            pltpu.VMEM((1, recv), jnp.int32),
            pltpu.VMEM((regions, 2, half * slot, hours), BF),
            pltpu.SemaphoreType.DMA((3,)),
            pltpu.SemaphoreType.DMA((2,)),
        ],
    )(jnp.transpose(runoff, (1, 2, 0)), send_rows.reshape(1, recv))
    received = lax.all_to_all(
        send.reshape(regions * 2, half * slot, hours), ("side", "row", "core"), 0, 0
    ).reshape(regions, 2, half * slot, hours)
    raw = call(
        raw_kernel,
        struct((32 + outs, reaches), F32),
        in_specs=vmem(5),
        out_specs=vmem(1)[0],
    )(
        remap_index.T,
        remap_weight.T,
        class_id.T,
        outlets.reshape(1, outs),
        incidence.reshape(outs, reaches),
    )
    other = lax.ppermute(raw, "core", swap)
    table, mix, passing, cls_out, wide_mix, link, cls_target, cls_own = call(
        functools.partial(prep_kernel, slot, columns),
        (
            struct((hours, class_count * BLOCK), BF),
            struct((2, 2 * kap, SUB * outs), BF),
            struct((2, MB * outs, MB * outs), BF),
            struct((2, 8, MB * outs), F32),
            struct((2 * kap, SUB * reaches), BF),
            struct((2 * SUB * outs, SUB * reaches), BF),
            struct((8, MB * outs), F32),
            struct((8, reaches), F32),
        ),
        in_specs=[SCALAR] + vmem(4),
        out_specs=tuple(vmem(8)),
    )(core_arg, raw, other, kernel_rate.reshape(1, class_count), kernel_shape)

    panel_shape = struct((hours, wide), BF)
    float_shape = struct((hours, wide), F32)
    panel, first, rows_send = call(
        functools.partial(head_kernel, class_count),
        (panel_shape, panel_shape, struct((regions, half * slot, hours), BF)),
        in_specs=[SCALAR] * 2 + vmem(5),
        out_specs=tuple(vmem(3)),
    )(core_arg, pair_arg, received, table, mix, passing, cls_out)
    inflow = lax.ppermute(panel, "pair", [(0, 1), (1, 0)]) if pairs > 1 else panel
    rows_other = lax.ppermute(rows_send, "core", swap)
    first_other = lax.ppermute(first, "core", swap)

    base_shape = struct((hours, half * reaches), F32)
    shapes = [base_shape, float_shape] + [float_shape] * (pairs > 2)
    base_own, even, *odd = call(
        functools.partial(base_own_kernel, class_count),
        tuple(shapes),
        in_specs=[SCALAR] * 2 + vmem(6),
        out_specs=tuple(vmem(len(shapes))),
    )(core_arg, pair_arg, received, table, wide_mix, cls_own, mix, cls_out)
    base_other, done_first = call(
        functools.partial(other_kernel, class_count),
        (base_shape, struct((hours, half, reaches), BF)),
        in_specs=[SCALAR] * 2 + vmem(8),
        out_specs=tuple(vmem(2)),
    )(core_arg, pair_arg, rows_other, table, wide_mix, cls_own, first, base_own, link, cls_target)


    for step in range(1, pairs - 1):
        panel = call(
            functools.partial(hop_kernel, class_count),
            panel_shape,
            in_specs=vmem(6),
            out_specs=vmem(1)[0],
        )(inflow, table, passing, cls_out, even, odd[0])
        arriving = lax.ppermute(panel, "pair", [(step, step + 1), (step + 1, step)])
        inflow = jnp.where(pair == step + 1, arriving, inflow)

    def early(top, own):
        return call(
            functools.partial(early_kernel, class_count, top),
            struct((hours, half, reaches), BF),
            in_specs=[SCALAR] * 2 + vmem(5),
            out_specs=vmem(1)[0],
        )(core_arg, pair_arg, own, base_own, table, link, cls_target)

    def late(top, done, gotten, before):
        return call(
            functools.partial(late_kernel, class_count, top),
            struct((hours, members, reaches), BF),
            in_specs=[SCALAR] * 2 + vmem(6) + [anywhere] * len(before),
            out_specs=anywhere,
            scratch_shapes=[
                pltpu.VMEM((hours, half, reaches), BF),
                pltpu.SemaphoreType.DMA((1 + -(-hours // LANES),)),
            ],
            input_output_aliases={8: 0} if before else {},
        )(core_arg, pair_arg, done, gotten, base_other, table, link, cls_target, *before)

    own, given = call(
        functools.partial(last_hop_kernel, class_count),
        (panel_shape, panel_shape),
        in_specs=[SCALAR] * 2 + vmem(5) + [anywhere],
        out_specs=tuple(vmem(2)),
    )(core_arg, pair_arg, inflow, table, passing, cls_out, even, done_first)
    gotten = lax.ppermute(given, "core", swap)
    out = late(True, done_first, first_other, [])
    return late(False, early(False, own), gotten, [out])


def solution(mesh):
    regions, orders = mesh.shape["region"], mesh.shape["order"]
    split_mesh = Mesh(
        mesh.devices.reshape(regions // SIDE, SIDE, orders // 2, 2), ("row", "side", "pair", "core")
    )
    region = ("row", "side")
    order = ("pair", "core")
    every = region + order
    return jax.shard_map(
        local,
        mesh=split_mesh,
        in_specs=(
            P(None, None, every),
            P(region, order, None),
            P(every, None),
            P(every, None),
            P(every, None),
            P(),
            P(),
            P(region, order, None),
            P(region, order, None, None),
        ),
        out_specs=P(None, None, every),
        check_vma=False,
    )
```

```python
import functools
import jax
import jax.numpy as jnp
from jax import lax
from jax.experimental import pallas as pl
from jax.experimental.pallas import tpu as pltpu
from jax.sharding import Mesh, PartitionSpec as P

BF = jnp.bfloat16
F32 = jnp.float32
MB = 8
SUB = 4
LANES = 128
SIDE = 2
BLOCK = 32
CHUNK = 256
VMEM_LIMIT = 20 * 1024 * 1024
FULL_VMEM = 56 * 1024 * 1024


def iota(shape, dim):
    return lax.broadcasted_iota(jnp.int32, shape, dim)


def mm(a, b):
    return jnp.dot(a, b, preferred_element_type=F32)


def one_hot(condition):
    return jnp.where(condition, 1.0, 0.0).astype(BF)


def split(value):
    high = value.astype(BF)
    return high, (value - high.astype(F32)).astype(BF)


def call(kernel, out_shape, limit=VMEM_LIMIT, **extra):
    return pl.pallas_call(
        kernel,
        out_shape=out_shape,
        compiler_params=pltpu.CompilerParams(vmem_limit_bytes=limit),
        cost_estimate=pl.CostEstimate(flops=1, bytes_accessed=1, transcendentals=0),
        **extra,
    )


def vmem(count):
    return [pl.BlockSpec(memory_space=pltpu.VMEM)] * count


SCALAR = pl.BlockSpec(memory_space=pltpu.SMEM)


def region_at(place, regions):
    rows = regions // SIDE
    return (place % rows) * SIDE + place // rows


def convolve(table, value, classes, class_count):
    hours, width = value.shape
    columns = []
    for begin in range(0, width, CHUNK):
        cut = slice(begin, min(begin + CHUNK, width))
        masks = [one_hot(classes[:, cut] == float(k)) for k in range(class_count)]
        total = None
        for start in range(0, hours, BLOCK):
            block = value[start : start + BLOCK, cut]
            short = BLOCK - block.shape[0]
            if short:
                block = jnp.concatenate([block, jnp.zeros((short, block.shape[1]), BF)], axis=0)
            parts = jnp.concatenate([block * mask for mask in masks], axis=0)
            added = mm(table[: hours - start], parts)
            if start == 0:
                total = added
            else:
                total = jnp.concatenate([total[:start], total[start:] + added], axis=0)
        columns.append(total)
    return jnp.concatenate(columns, axis=1)


def pack_kernel(slot, x_ref, rows_ref, send_ref, held, rows_held, ready, arrived, sent):
    members, grid, hours = x_ref.shape
    blocks = members // MB
    regions = send_ref.shape[0]
    per = MB * slot

    half = members // 2

    def fetch(core):
        place = pl.ds(core * half, half)
        return pltpu.make_async_copy(x_ref.at[place], held.at[place], arrived.at[core])

    def deliver(core):
        return pltpu.make_async_copy(ready.at[:, core], send_ref.at[:, core], sent.at[core])

    first = pltpu.make_async_copy(rows_ref, rows_held, arrived.at[2])
    first.start()
    for core in range(2):
        fetch(core).start()
    first.wait()
    count = regions * per
    recv = rows_ref.shape[1]
    row = iota((count, recv), 0)
    wanted = region_at(row // per, regions) * slot + row % slot
    rows = rows_held[...].astype(F32)
    chosen = jnp.sum(jnp.where(iota((count, recv), 1) == wanted, rows, 0.0), axis=1, keepdims=True)
    lane = iota((count, MB * grid), 1)
    member = (iota((count, MB * grid), 0) // slot) % MB
    select = one_hot((lane // grid == member) & ((lane % grid).astype(F32) == chosen))
    for core in range(2):
        fetch(core).wait()
        for inner in range(blocks // 2):
            begin = core * half + inner * MB
            x = held[begin : begin + MB].reshape(MB * grid, hours).astype(BF)
            y = mm(select, x).astype(BF).reshape(regions, per, hours)
            ready[:, core, inner * per : (inner + 1) * per, :] = y
        deliver(core).start()
    for core in range(2):
        deliver(core).wait()


def raw_kernel(idx_ref, w_ref, cls_ref, outl_ref, inc_ref, raw_ref):
    raw_ref[...] = jnp.zeros_like(raw_ref)
    raw_ref[0 : idx_ref.shape[0], :] = idx_ref[...].astype(F32)
    raw_ref[8 : 8 + w_ref.shape[0], :] = w_ref[...]
    raw_ref[16:17, :] = cls_ref[...].astype(F32)
    raw_ref[24:25, 0 : outl_ref.shape[1]] = outl_ref[...].astype(F32)
    raw_ref[32:, :] = inc_ref[...].astype(F32)


def prep_kernel(
    slot, columns, core_ref, own_ref, other_ref, rate_ref, shape_ref,
    table_ref, mix_ref, pass_ref, cls_out_ref, wide_ref, link_ref, cls_target_ref, cls_own_ref,
):
    core = core_ref[0]
    class_count, hours = shape_ref.shape
    padded = -(-hours // LANES) * LANES
    kap = mix_ref.shape[1] // 2
    recv = kap // SUB
    per = SUB * slot
    outs = own_ref.shape[0] - 32
    reaches = own_ref.shape[1]
    wide = MB * outs
    narrow = SUB * outs

    lag = iota((class_count, hours), 1).astype(F32)
    square = (class_count, class_count)
    rate = jnp.where(iota(square, 0) == iota(square, 1), rate_ref[...], 0.0)
    rate = jnp.sum(rate, axis=1, keepdims=True)
    hydro = (rate * shape_ref[...] * jnp.exp(-rate * lag)).astype(BF)
    reverse = one_hot((iota((hours, padded), 0) + iota((hours, padded), 1)) % padded == 0)
    turned = mm(hydro, reverse)
    later = iota((padded, BLOCK), 1) <= iota((padded, BLOCK), 0)
    for k in range(class_count):
        rolled = pltpu.roll(
            jnp.broadcast_to(turned[k : k + 1, :], (padded, padded)), 0, 1, stride=1, stride_axis=0
        )
        rolled = jnp.where(later, rolled[:, :BLOCK], 0.0)
        table_ref[:, k * BLOCK : (k + 1) * BLOCK] = rolled[:hours].astype(BF)

    row_p = iota((kap, recv), 0)
    spot = region_at(row_p // per, recv // slot) * slot + row_p % slot
    expand = one_hot(spot == iota((kap, recv), 1))

    def owner(width):
        return (iota((kap, width), 0) // slot) % SUB

    def tile(width):
        return one_hot(iota((outs, width), 0) == iota((outs, width), 1) % outs)

    def weights(raw):
        total = jnp.zeros((recv, reaches), F32)
        for j in range(columns):
            hit = iota((recv, reaches), 0).astype(F32) == raw[j : j + 1, :]
            total = total + jnp.where(hit, raw[8 + j : 9 + j, :], 0.0)
        return split(total)

    own = own_ref[...]
    for level in range(2):
        raw = jnp.where(core == level, own, other_ref[...])
        lanes = mm(raw[24:32, :outs].astype(BF), tile(wide))[0:1, :]
        pick = one_hot(iota((reaches, wide), 0).astype(F32) == lanes)
        for part, weight in enumerate(weights(raw)):
            spread = mm(expand, mm(weight, pick[:, :narrow]).astype(BF))
            spread = jnp.where(owner(narrow) == iota((kap, narrow), 1) // outs, spread, 0.0)
            mix_ref[level, part * kap : (part + 1) * kap] = spread.astype(BF)
        moved = jnp.concatenate([mm(raw[32:, :].astype(BF), pick)] * MB, axis=0)
        here = iota((wide, wide), 0) // outs == iota((wide, wide), 1) // outs
        pass_ref[level] = jnp.where(here, moved, 0.0).astype(BF)
        cls_out_ref[level] = mm(raw[16:24, :].astype(BF), pick)

    for part, weight in enumerate(weights(own)):
        spread = mm(expand, weight)
        for m in range(SUB):
            piece = jnp.where(owner(reaches) == m, spread, 0.0).astype(BF)
            wide_ref[part * kap : (part + 1) * kap, m * reaches : (m + 1) * reaches] = piece
    cls_own_ref[...] = own[16:24, :]
    cls_target_ref[...] = lax.dot_general(
        own[16:24, :].astype(BF),
        jnp.concatenate([own[32:, :]] * MB, axis=0).astype(BF),
        (((1,), (1,)), ((), ())),
        preferred_element_type=F32,
    )
    stacked = jnp.concatenate([own[32:, :]] * SUB, axis=0)
    who = iota((narrow, reaches), 0) // outs
    for m in range(SUB):
        piece = jnp.where(who == m, stacked, 0.0).astype(BF)
        for part in range(2):
            link_ref[part * narrow : (part + 1) * narrow, m * reaches : (m + 1) * reaches] = piece


def side_by_side(parts, right):
    product = mm(jnp.concatenate(parts, axis=0), right)
    count = parts[0].shape[0]
    rows = [product[i * count : (i + 1) * count] for i in range(len(parts))]
    return jnp.concatenate(rows, axis=1)


def twice(rows_ref, sub, size):
    rows = rows_ref[:, sub * size : (sub + 1) * size, :]
    rows = rows.reshape(rows.shape[0] * size, rows.shape[2]).T
    return jnp.concatenate([rows, rows], axis=1)


def pass_on(panel, pass_matrix):
    width = pass_matrix.shape[0]
    parts = [
        mm(panel[:, start : start + width], pass_matrix).astype(BF)
        for start in range(0, panel.shape[1], width)
    ]
    return jnp.concatenate(parts, axis=1)


def tiled(classes, width):
    return jnp.concatenate([classes] * (width // classes.shape[1]), axis=1)


def outlet_lateral(level, rows_ref, mix_ref):
    regions, _, total, _ = rows_ref.shape
    size = mix_ref.shape[1] // 2 // regions
    rows_ref = rows_ref.at[:, level]
    parts = [mm(twice(rows_ref, sub, size), mix_ref[level]) for sub in range(total // size)]
    return jnp.concatenate(parts, axis=1)


def rows_kernel(core_ref, rows_ref, send_ref):
    send_ref[...] = rows_ref[:, 1 - core_ref[0]]


def head_kernel(
    class_count, pair_ref, rows_ref, table_ref, mix_ref, pass_ref, cls_ref, after_ref,
    panel_ref, first_ref,
):
    @pl.when(pair_ref[0] == 0)
    def _():
        wide = panel_ref.shape[1]
        classes = [tiled(cls_ref[level, 0:1, :], wide) for level in range(2)]
        lateral = [outlet_lateral(level, rows_ref, mix_ref) for level in range(2)]
        first = convolve(table_ref[...], lateral[0].astype(BF), classes[0], class_count).astype(BF)
        first_ref[...] = first
        inflow = (lateral[1] + pass_on(first, pass_ref[1]).astype(F32)).astype(BF)
        panel_ref[...] = convolve(table_ref[...], inflow, classes[1], class_count).astype(BF)


def hop_kernel(class_count, inflow_ref, table_ref, pass_ref, cls_ref, even_ref, odd_ref, panel_ref):
    classes = [tiled(cls_ref[level, 0:1, :], even_ref.shape[1]) for level in range(2)]
    moved = pass_on(inflow_ref[...], pass_ref[0])
    even = even_ref[...] + convolve(table_ref[...], moved, classes[0], class_count)
    moved = odd_ref[...] + pass_on(even.astype(BF), pass_ref[1]).astype(F32)
    panel_ref[...] = convolve(table_ref[...], moved.astype(BF), classes[1], class_count).astype(BF)


def last_hop_kernel(class_count, core_ref, pair_ref, inflow_ref, table_ref, pass_ref, cls_ref, even_ref, *rest):
    own_ref, send_ref = rest[-2:]

    @pl.when(pair_ref[0] > 0)
    def _():
        arrived = inflow_ref[...]
        classes = tiled(cls_ref[0, 0:1, :], even_ref.shape[1])
        moved = pass_on(arrived, pass_ref[0])
        even = even_ref[...] + convolve(table_ref[...], moved, classes, class_count)
        even = even.astype(BF)
        first = core_ref[0] == 0
        own_ref[...] = jnp.where(first, arrived, even)
        send_ref[...] = jnp.where(first, even, arrived)


def base_kernel(class_count, core_ref, rows_ref, table_ref, wide_ref, cls_ref, base_ref):
    if len(rows_ref.shape) == 4:
        rows_ref = rows_ref.at[:, core_ref[0]]
    regions, total, _ = rows_ref.shape
    size = wide_ref.shape[0] // 2 // regions
    width = wide_ref.shape[1]
    parts = [twice(rows_ref, sub, size) for sub in range(total // size)]
    classes = tiled(cls_ref[0:1, :], width)
    lateral = side_by_side(parts, wide_ref[...]).astype(BF)
    for start in range(0, base_ref.shape[1], width):
        base_ref[:, start : start + width] = convolve(
            table_ref[...], lateral[:, start : start + width], classes, class_count
        )


def base_own_kernel(
    class_count, core_ref, pair_ref, rows_ref, table_ref, wide_ref, cls_ref, mix_ref, cls_out_ref,
    base_ref, even_ref, *odd_ref,
):
    base_kernel(class_count, core_ref, rows_ref, table_ref, wide_ref, cls_ref, base_ref)

    @pl.when(pair_ref[0] > 0)
    def _():
        lateral = outlet_lateral(0, rows_ref, mix_ref).astype(BF)
        classes = tiled(cls_out_ref[0, 0:1, :], even_ref.shape[1])
        even_ref[...] = convolve(table_ref[...], lateral, classes, class_count)
        if odd_ref:
            odd_ref[0][...] = outlet_lateral(1, rows_ref, mix_ref)


def routed_parts(class_count, top, core_ref, inflow_ref, table_ref, cls_ref):
    inflow = inflow_ref[...]
    if top:
        inflow = jnp.where(core_ref[0] == 0, jnp.zeros((), BF), inflow)
    classes = tiled(cls_ref[0:1, :], inflow.shape[1])
    return split(convolve(table_ref[...], inflow, classes, class_count))


def mine(top, pair_ref):
    return pl.when((pair_ref[0] == 0) == top)


def assemble(hours, high, low, base_ref, link_ref, members, reaches):
    lanes, width = link_ref.shape[0] // 2, link_ref.shape[1]
    flows = []
    for part in range(high.shape[1] // lanes):
        cut = slice(part * lanes, (part + 1) * lanes)
        both = jnp.concatenate([high[hours, cut], low[hours, cut]], axis=1)
        total = mm(both, link_ref[...]) + base_ref[hours, part * width : (part + 1) * width]
        flows.append(total.astype(BF))
    return jnp.concatenate(flows, axis=1).reshape(hours.stop - hours.start, members, reaches)


def early_kernel(
    class_count, top, core_ref, pair_ref, inflow_ref, base_ref, table_ref, link_ref, cls_ref,
    out_ref,
):
    hours, members, reaches = out_ref.shape

    @mine(top, pair_ref)
    def _():
        high, low = routed_parts(class_count, top, core_ref, inflow_ref, table_ref, cls_ref)
        out_ref[...] = assemble(slice(0, hours), high, low, base_ref, link_ref, members, reaches)


def late_kernel(
    class_count, top, core_ref, pair_ref, done_ref, inflow_ref, base_ref, table_ref, link_ref,
    cls_ref, *rest,
):
    out_ref, ready, sems = rest[-3:]
    hours, members, reaches = done_ref.shape

    @mine(top, pair_ref)
    def _():
        core = core_ref[0]

        def place(which):
            return pl.ds(pl.multiple_of(which * members, members), members)

        copies = [pltpu.make_async_copy(done_ref, out_ref.at[:, place(core)], sems.at[0])]
        copies[0].start()
        high, low = routed_parts(class_count, top, core_ref, inflow_ref, table_ref, cls_ref)
        for start in range(0, hours, LANES):
            part = slice(start, min(start + LANES, hours))
            ready[part] = assemble(part, high, low, base_ref, link_ref, members, reaches)
            span = pl.ds(start, part.stop - start)
            copies.append(
                pltpu.make_async_copy(
                    ready.at[span], out_ref.at[span, place(1 - core)], sems.at[len(copies)]
                )
            )
            copies[-1].start()
        for copy in copies:
            copy.wait()


def local(
    runoff, send_rows, remap_index, remap_weight, class_id, kernel_shape, kernel_rate, outlets, incidence
):
    hours, members, grid = runoff.shape
    regions = lax.axis_size("row") * lax.axis_size("side")
    pairs = lax.axis_size("pair")
    class_count = kernel_shape.shape[0]
    reaches, columns = remap_index.shape
    recv = send_rows.size
    slot = recv // regions
    outs = outlets.size
    half = members // 2
    kap = recv * SUB
    wide = half * outs
    core = lax.axis_index("core").astype(jnp.int32)
    core_arg = core.reshape(1)
    pair = lax.axis_index("pair")
    pair_arg = pair.astype(jnp.int32).reshape(1)
    swap = [(0, 1), (1, 0)]
    anywhere = pl.BlockSpec(memory_space=pl.ANY)

    def struct(shape, dtype):
        return jax.ShapeDtypeStruct(shape, dtype)

    send = call(
        functools.partial(pack_kernel, slot),
        struct((regions, 2, half * slot, hours), BF),
        limit=FULL_VMEM,
        in_specs=[anywhere] * 2,
        out_specs=anywhere,
        scratch_shapes=[
            pltpu.VMEM((members, grid, hours), F32),
            pltpu.VMEM((1, recv), jnp.int32),
            pltpu.VMEM((regions, 2, half * slot, hours), BF),
            pltpu.SemaphoreType.DMA((3,)),
            pltpu.SemaphoreType.DMA((2,)),
        ],
    )(jnp.transpose(runoff, (1, 2, 0)), send_rows.reshape(1, recv))
    received = lax.all_to_all(
        send.reshape(regions * 2, half * slot, hours), ("side", "row", "core"), 0, 0
    ).reshape(regions, 2, half * slot, hours)
    raw = call(
        raw_kernel,
        struct((32 + outs, reaches), F32),
        in_specs=vmem(5),
        out_specs=vmem(1)[0],
    )(
        remap_index.T,
        remap_weight.T,
        class_id.T,
        outlets.reshape(1, outs),
        incidence.reshape(outs, reaches),
    )
    other = lax.ppermute(raw, "core", swap)
    table, mix, passing, cls_out, wide_mix, link, cls_target, cls_own = call(
        functools.partial(prep_kernel, slot, columns),
        (
            struct((hours, class_count * BLOCK), BF),
            struct((2, 2 * kap, SUB * outs), BF),
            struct((2, MB * outs, MB * outs), BF),
            struct((2, 8, MB * outs), F32),
            struct((2 * kap, SUB * reaches), BF),
            struct((2 * SUB * outs, SUB * reaches), BF),
            struct((8, MB * outs), F32),
            struct((8, reaches), F32),
        ),
        in_specs=[SCALAR] + vmem(4),
        out_specs=tuple(vmem(8)),
    )(core_arg, raw, other, kernel_rate.reshape(1, class_count), kernel_shape)

    panel_shape = struct((hours, wide), BF)
    float_shape = struct((hours, wide), F32)
    rows_send = call(
        rows_kernel,
        struct((regions, half * slot, hours), BF),
        in_specs=[SCALAR] + vmem(1),
        out_specs=vmem(1)[0],
    )(core_arg, received)
    panel, first = call(
        functools.partial(head_kernel, class_count),
        (panel_shape, panel_shape),
        in_specs=[SCALAR] + vmem(6),
        out_specs=tuple(vmem(2)),
    )(pair_arg, received, table, mix, passing, cls_out, rows_send)
    inflow = lax.ppermute(panel, "pair", [(0, 1), (1, 0)]) if pairs > 1 else panel
    rows_other = lax.ppermute(rows_send, "core", swap)
    first_other = lax.ppermute(first, "core", swap)

    base_shape = struct((hours, half * reaches), F32)
    shapes = [base_shape, float_shape] + [float_shape] * (pairs > 2)
    base_own, even, *odd = call(
        functools.partial(base_own_kernel, class_count),
        tuple(shapes),
        in_specs=[SCALAR] * 2 + vmem(6),
        out_specs=tuple(vmem(len(shapes))),
    )(core_arg, pair_arg, received, table, wide_mix, cls_own, mix, cls_out)
    base_other = call(
        functools.partial(base_kernel, class_count),
        base_shape,
        in_specs=[SCALAR] + vmem(4),
        out_specs=vmem(1)[0],
    )(core_arg, rows_other, table, wide_mix, cls_own)


    for step in range(1, pairs - 1):
        panel = call(
            functools.partial(hop_kernel, class_count),
            panel_shape,
            in_specs=vmem(6),
            out_specs=vmem(1)[0],
        )(inflow, table, passing, cls_out, even, odd[0])
        arriving = lax.ppermute(panel, "pair", [(step, step + 1), (step + 1, step)])
        inflow = jnp.where(pair == step + 1, arriving, inflow)

    def early(top, own):
        return call(
            functools.partial(early_kernel, class_count, top),
            struct((hours, half, reaches), BF),
            in_specs=[SCALAR] * 2 + vmem(5),
            out_specs=vmem(1)[0],
        )(core_arg, pair_arg, own, base_own, table, link, cls_target)

    def late(top, done, gotten, before):
        return call(
            functools.partial(late_kernel, class_count, top),
            struct((hours, members, reaches), BF),
            in_specs=[SCALAR] * 2 + vmem(6) + [anywhere] * len(before),
            out_specs=anywhere,
            scratch_shapes=[
                pltpu.VMEM((hours, half, reaches), BF),
                pltpu.SemaphoreType.DMA((1 + -(-hours // LANES),)),
            ],
            input_output_aliases={8: 0} if before else {},
        )(core_arg, pair_arg, done, gotten, base_other, table, link, cls_target, *before)

    done_first = early(True, first)
    own, given = call(
        functools.partial(last_hop_kernel, class_count),
        (panel_shape, panel_shape),
        in_specs=[SCALAR] * 2 + vmem(5) + [anywhere] * 2,
        out_specs=tuple(vmem(2)),
    )(core_arg, pair_arg, inflow, table, passing, cls_out, even, done_first, base_other)
    gotten = lax.ppermute(given, "core", swap)
    out = late(True, done_first, first_other, [])
    return late(False, early(False, own), gotten, [out])


def solution(mesh):
    regions, orders = mesh.shape["region"], mesh.shape["order"]
    split_mesh = Mesh(
        mesh.devices.reshape(regions // SIDE, SIDE, orders // 2, 2), ("row", "side", "pair", "core")
    )
    region = ("row", "side")
    order = ("pair", "core")
    every = region + order
    return jax.shard_map(
        local,
        mesh=split_mesh,
        in_specs=(
            P(None, None, every),
            P(region, order, None),
            P(every, None),
            P(every, None),
            P(every, None),
            P(),
            P(),
            P(region, order, None),
            P(region, order, None, None),
        ),
        out_specs=P(None, None, every),
        check_vma=False,
    )
```

```python
import functools
import jax
import jax.numpy as jnp
from jax import lax
from jax.experimental import pallas as pl
from jax.experimental.pallas import tpu as pltpu
from jax.sharding import Mesh, PartitionSpec as P

BF = jnp.bfloat16
F32 = jnp.float32
MB = 8
SUB = 4
LANES = 128
SIDE = 2
BLOCK = 32
CHUNK = 256
VMEM_LIMIT = 20 * 1024 * 1024
FULL_VMEM = 56 * 1024 * 1024


def iota(shape, dim):
    return lax.broadcasted_iota(jnp.int32, shape, dim)


def mm(a, b):
    return jnp.dot(a, b, preferred_element_type=F32)


def one_hot(condition):
    return jnp.where(condition, 1.0, 0.0).astype(BF)


def split(value):
    high = value.astype(BF)
    return high, (value - high.astype(F32)).astype(BF)


def call(kernel, out_shape, limit=VMEM_LIMIT, **extra):
    return pl.pallas_call(
        kernel,
        out_shape=out_shape,
        compiler_params=pltpu.CompilerParams(vmem_limit_bytes=limit),
        cost_estimate=pl.CostEstimate(flops=1, bytes_accessed=1, transcendentals=0),
        **extra,
    )


def vmem(count):
    return [pl.BlockSpec(memory_space=pltpu.VMEM)] * count


SCALAR = pl.BlockSpec(memory_space=pltpu.SMEM)


def region_at(place, regions):
    rows = regions // SIDE
    return (place % rows) * SIDE + place // rows


def convolve(table, value, classes, class_count):
    hours, width = value.shape
    columns = []
    for begin in range(0, width, CHUNK):
        cut = slice(begin, min(begin + CHUNK, width))
        masks = [one_hot(classes[:, cut] == float(k)) for k in range(class_count)]
        total = None
        for start in range(0, hours, BLOCK):
            block = value[start : start + BLOCK, cut]
            short = BLOCK - block.shape[0]
            if short:
                block = jnp.concatenate([block, jnp.zeros((short, block.shape[1]), BF)], axis=0)
            parts = jnp.concatenate([block * mask for mask in masks], axis=0)
            added = mm(table[: hours - start], parts)
            if start == 0:
                total = added
            else:
                total = jnp.concatenate([total[:start], total[start:] + added], axis=0)
        columns.append(total)
    return jnp.concatenate(columns, axis=1)


def pack_kernel(slot, x_ref, rows_ref, send_ref, held, rows_held, ready, arrived, sent):
    members, grid, hours = x_ref.shape
    blocks = members // MB
    regions = send_ref.shape[0]
    per = MB * slot

    half = members // 2

    def fetch(core):
        place = pl.ds(core * half, half)
        return pltpu.make_async_copy(x_ref.at[place], held.at[place], arrived.at[core])

    def deliver(core):
        return pltpu.make_async_copy(ready.at[:, core], send_ref.at[:, core], sent.at[core])

    first = pltpu.make_async_copy(rows_ref, rows_held, arrived.at[2])
    first.start()
    for core in range(2):
        fetch(core).start()
    first.wait()
    count = regions * per
    recv = rows_ref.shape[1]
    row = iota((count, recv), 0)
    wanted = region_at(row // per, regions) * slot + row % slot
    rows = rows_held[...].astype(F32)
    chosen = jnp.sum(jnp.where(iota((count, recv), 1) == wanted, rows, 0.0), axis=1, keepdims=True)
    lane = iota((count, MB * grid), 1)
    member = (iota((count, MB * grid), 0) // slot) % MB
    select = one_hot((lane // grid == member) & ((lane % grid).astype(F32) == chosen))
    for core in range(2):
        fetch(core).wait()
        for inner in range(blocks // 2):
            begin = core * half + inner * MB
            x = held[begin : begin + MB].reshape(MB * grid, hours).astype(BF)
            y = mm(select, x).astype(BF).reshape(regions, per, hours)
            ready[:, core, inner * per : (inner + 1) * per, :] = y
        deliver(core).start()
    for core in range(2):
        deliver(core).wait()


def raw_kernel(idx_ref, w_ref, cls_ref, outl_ref, inc_ref, raw_ref):
    raw_ref[...] = jnp.zeros_like(raw_ref)
    raw_ref[0 : idx_ref.shape[0], :] = idx_ref[...].astype(F32)
    raw_ref[8 : 8 + w_ref.shape[0], :] = w_ref[...]
    raw_ref[16:17, :] = cls_ref[...].astype(F32)
    raw_ref[24:25, 0 : outl_ref.shape[1]] = outl_ref[...].astype(F32)
    raw_ref[32:, :] = inc_ref[...].astype(F32)


def prep_kernel(
    slot, columns, core_ref, own_ref, other_ref, rate_ref, shape_ref,
    table_ref, mix_ref, pass_ref, cls_out_ref, wide_ref, link_ref, cls_target_ref, cls_own_ref,
):
    core = core_ref[0]
    class_count, hours = shape_ref.shape
    padded = -(-hours // LANES) * LANES
    kap = mix_ref.shape[1] // 2
    recv = kap // SUB
    per = SUB * slot
    outs = own_ref.shape[0] - 32
    reaches = own_ref.shape[1]
    wide = MB * outs
    narrow = SUB * outs

    lag = iota((class_count, hours), 1).astype(F32)
    square = (class_count, class_count)
    rate = jnp.where(iota(square, 0) == iota(square, 1), rate_ref[...], 0.0)
    rate = jnp.sum(rate, axis=1, keepdims=True)
    hydro = (rate * shape_ref[...] * jnp.exp(-rate * lag)).astype(BF)
    reverse = one_hot((iota((hours, padded), 0) + iota((hours, padded), 1)) % padded == 0)
    turned = mm(hydro, reverse)
    later = iota((padded, BLOCK), 1) <= iota((padded, BLOCK), 0)
    for k in range(class_count):
        rolled = pltpu.roll(
            jnp.broadcast_to(turned[k : k + 1, :], (padded, padded)), 0, 1, stride=1, stride_axis=0
        )
        rolled = jnp.where(later, rolled[:, :BLOCK], 0.0)
        table_ref[:, k * BLOCK : (k + 1) * BLOCK] = rolled[:hours].astype(BF)

    row_p = iota((kap, recv), 0)
    spot = region_at(row_p // per, recv // slot) * slot + row_p % slot
    expand = one_hot(spot == iota((kap, recv), 1))

    def owner(width):
        return (iota((kap, width), 0) // slot) % SUB

    def tile(width):
        return one_hot(iota((outs, width), 0) == iota((outs, width), 1) % outs)

    def weights(raw):
        total = jnp.zeros((recv, reaches), F32)
        for j in range(columns):
            hit = iota((recv, reaches), 0).astype(F32) == raw[j : j + 1, :]
            total = total + jnp.where(hit, raw[8 + j : 9 + j, :], 0.0)
        return split(total)

    own = own_ref[...]
    for level in range(2):
        raw = jnp.where(core == level, own, other_ref[...])
        lanes = mm(raw[24:32, :outs].astype(BF), tile(wide))[0:1, :]
        pick = one_hot(iota((reaches, wide), 0).astype(F32) == lanes)
        for part, weight in enumerate(weights(raw)):
            spread = mm(expand, mm(weight, pick[:, :narrow]).astype(BF))
            spread = jnp.where(owner(narrow) == iota((kap, narrow), 1) // outs, spread, 0.0)
            mix_ref[level, part * kap : (part + 1) * kap] = spread.astype(BF)
        moved = jnp.concatenate([mm(raw[32:, :].astype(BF), pick)] * MB, axis=0)
        here = iota((wide, wide), 0) // outs == iota((wide, wide), 1) // outs
        pass_ref[level] = jnp.where(here, moved, 0.0).astype(BF)
        cls_out_ref[level] = mm(raw[16:24, :].astype(BF), pick)

    for part, weight in enumerate(weights(own)):
        spread = mm(expand, weight)
        for m in range(SUB):
            piece = jnp.where(owner(reaches) == m, spread, 0.0).astype(BF)
            wide_ref[part * kap : (part + 1) * kap, m * reaches : (m + 1) * reaches] = piece
    cls_own_ref[...] = own[16:24, :]
    cls_target_ref[...] = lax.dot_general(
        own[16:24, :].astype(BF),
        jnp.concatenate([own[32:, :]] * MB, axis=0).astype(BF),
        (((1,), (1,)), ((), ())),
        preferred_element_type=F32,
    )
    stacked = jnp.concatenate([own[32:, :]] * SUB, axis=0)
    who = iota((narrow, reaches), 0) // outs
    for m in range(SUB):
        piece = jnp.where(who == m, stacked, 0.0).astype(BF)
        for part in range(2):
            link_ref[part * narrow : (part + 1) * narrow, m * reaches : (m + 1) * reaches] = piece


def side_by_side(parts, right):
    product = mm(jnp.concatenate(parts, axis=0), right)
    count = parts[0].shape[0]
    rows = [product[i * count : (i + 1) * count] for i in range(len(parts))]
    return jnp.concatenate(rows, axis=1)


def twice(rows_ref, sub, size):
    rows = rows_ref[:, sub * size : (sub + 1) * size, :]
    rows = rows.reshape(rows.shape[0] * size, rows.shape[2]).T
    return jnp.concatenate([rows, rows], axis=1)


def pass_on(panel, pass_matrix):
    width = pass_matrix.shape[0]
    parts = [
        mm(panel[:, start : start + width], pass_matrix).astype(BF)
        for start in range(0, panel.shape[1], width)
    ]
    return jnp.concatenate(parts, axis=1)


def tiled(classes, width):
    return jnp.concatenate([classes] * (width // classes.shape[1]), axis=1)


def outlet_lateral(level, rows_ref, mix_ref):
    regions, _, total, _ = rows_ref.shape
    size = mix_ref.shape[1] // 2 // regions
    rows_ref = rows_ref.at[:, level]
    parts = [mm(twice(rows_ref, sub, size), mix_ref[level]) for sub in range(total // size)]
    return jnp.concatenate(parts, axis=1)


def rows_kernel(core_ref, rows_ref, send_ref):
    send_ref[...] = rows_ref[:, 1 - core_ref[0]]


def head_kernel(
    class_count, pair_ref, rows_ref, table_ref, mix_ref, pass_ref, cls_ref, after_ref,
    panel_ref, first_ref,
):
    @pl.when(pair_ref[0] == 0)
    def _():
        wide = panel_ref.shape[1]
        classes = [tiled(cls_ref[level, 0:1, :], wide) for level in range(2)]
        lateral = [outlet_lateral(level, rows_ref, mix_ref) for level in range(2)]
        first = convolve(table_ref[...], lateral[0].astype(BF), classes[0], class_count).astype(BF)
        first_ref[...] = first
        inflow = (lateral[1] + pass_on(first, pass_ref[1]).astype(F32)).astype(BF)
        panel_ref[...] = convolve(table_ref[...], inflow, classes[1], class_count).astype(BF)


def hop_kernel(class_count, inflow_ref, table_ref, pass_ref, cls_ref, even_ref, odd_ref, panel_ref):
    classes = [tiled(cls_ref[level, 0:1, :], even_ref.shape[1]) for level in range(2)]
    moved = pass_on(inflow_ref[...], pass_ref[0])
    even = even_ref[...] + convolve(table_ref[...], moved, classes[0], class_count)
    moved = odd_ref[...] + pass_on(even.astype(BF), pass_ref[1]).astype(F32)
    panel_ref[...] = convolve(table_ref[...], moved.astype(BF), classes[1], class_count).astype(BF)


def last_hop_kernel(class_count, core_ref, pair_ref, inflow_ref, table_ref, pass_ref, cls_ref, even_ref, *rest):
    own_ref, send_ref = rest[-2:]

    @pl.when(pair_ref[0] > 0)
    def _():
        arrived = inflow_ref[...]
        classes = tiled(cls_ref[0, 0:1, :], even_ref.shape[1])
        moved = pass_on(arrived, pass_ref[0])
        even = even_ref[...] + convolve(table_ref[...], moved, classes, class_count)
        even = even.astype(BF)
        first = core_ref[0] == 0
        own_ref[...] = jnp.where(first, arrived, even)
        send_ref[...] = jnp.where(first, even, arrived)


def base_kernel(class_count, core_ref, rows_ref, table_ref, wide_ref, cls_ref, base_ref):
    if len(rows_ref.shape) == 4:
        rows_ref = rows_ref.at[:, core_ref[0]]
    regions, total, _ = rows_ref.shape
    size = wide_ref.shape[0] // 2 // regions
    width = wide_ref.shape[1]
    parts = [twice(rows_ref, sub, size) for sub in range(total // size)]
    classes = tiled(cls_ref[0:1, :], width)
    lateral = side_by_side(parts, wide_ref[...]).astype(BF)
    for start in range(0, base_ref.shape[1], width):
        base_ref[:, start : start + width] = convolve(
            table_ref[...], lateral[:, start : start + width], classes, class_count
        )


def base_own_kernel(
    class_count, core_ref, pair_ref, rows_ref, table_ref, wide_ref, cls_ref, mix_ref, cls_out_ref,
    base_ref, even_ref, *odd_ref,
):
    base_kernel(class_count, core_ref, rows_ref, table_ref, wide_ref, cls_ref, base_ref)

    @pl.when(pair_ref[0] > 0)
    def _():
        lateral = outlet_lateral(0, rows_ref, mix_ref).astype(BF)
        classes = tiled(cls_out_ref[0, 0:1, :], even_ref.shape[1])
        even_ref[...] = convolve(table_ref[...], lateral, classes, class_count)
        if odd_ref:
            odd_ref[0][...] = outlet_lateral(1, rows_ref, mix_ref)


def routed_parts(class_count, top, core_ref, inflow_ref, table_ref, cls_ref):
    inflow = inflow_ref[...]
    if top:
        inflow = jnp.where(core_ref[0] == 0, jnp.zeros((), BF), inflow)
    classes = tiled(cls_ref[0:1, :], inflow.shape[1])
    return split(convolve(table_ref[...], inflow, classes, class_count))


def mine(top, pair_ref):
    return pl.when((pair_ref[0] == 0) == top)


def assemble(hours, high, low, base_ref, link_ref, members, reaches):
    lanes, width = link_ref.shape[0] // 2, link_ref.shape[1]
    flows = []
    for part in range(high.shape[1] // lanes):
        cut = slice(part * lanes, (part + 1) * lanes)
        both = jnp.concatenate([high[hours, cut], low[hours, cut]], axis=1)
        total = mm(both, link_ref[...]) + base_ref[hours, part * width : (part + 1) * width]
        flows.append(total.astype(BF))
    return jnp.concatenate(flows, axis=1).reshape(hours.stop - hours.start, members, reaches)


def early_kernel(
    class_count, top, core_ref, pair_ref, inflow_ref, base_ref, table_ref, link_ref, cls_ref,
    out_ref,
):
    hours, members, reaches = out_ref.shape

    @mine(top, pair_ref)
    def _():
        high, low = routed_parts(class_count, top, core_ref, inflow_ref, table_ref, cls_ref)
        out_ref[...] = assemble(slice(0, hours), high, low, base_ref, link_ref, members, reaches)


def other_kernel(
    class_count, core_ref, pair_ref, rows_ref, table_ref, wide_ref, cls_ref, inflow_ref, base_own_ref,
    link_ref, cls_target_ref, base_ref, done_ref,
):
    base_kernel(class_count, core_ref, rows_ref, table_ref, wide_ref, cls_ref, base_ref)
    early_kernel(
        class_count, True, core_ref, pair_ref, inflow_ref, base_own_ref, table_ref, link_ref,
        cls_target_ref, done_ref,
    )


def late_kernel(
    class_count, top, core_ref, pair_ref, done_ref, inflow_ref, base_ref, table_ref, link_ref,
    cls_ref, *rest,
):
    out_ref, ready, sems = rest[-3:]
    hours, members, reaches = done_ref.shape

    @mine(top, pair_ref)
    def _():
        core = core_ref[0]

        def place(which):
            return pl.ds(pl.multiple_of(which * members, members), members)

        copies = [pltpu.make_async_copy(done_ref, out_ref.at[:, place(core)], sems.at[0])]
        copies[0].start()
        high, low = routed_parts(class_count, top, core_ref, inflow_ref, table_ref, cls_ref)
        for start in range(0, hours, LANES):
            part = slice(start, min(start + LANES, hours))
            ready[part] = assemble(part, high, low, base_ref, link_ref, members, reaches)
            span = pl.ds(start, part.stop - start)
            copies.append(
                pltpu.make_async_copy(
                    ready.at[span], out_ref.at[span, place(1 - core)], sems.at[len(copies)]
                )
            )
            copies[-1].start()
        for copy in copies:
            copy.wait()


def local(
    runoff, send_rows, remap_index, remap_weight, class_id, kernel_shape, kernel_rate, outlets, incidence
):
    hours, members, grid = runoff.shape
    regions = lax.axis_size("row") * lax.axis_size("side")
    pairs = lax.axis_size("pair")
    class_count = kernel_shape.shape[0]
    reaches, columns = remap_index.shape
    recv = send_rows.size
    slot = recv // regions
    outs = outlets.size
    half = members // 2
    kap = recv * SUB
    wide = half * outs
    core = lax.axis_index("core").astype(jnp.int32)
    core_arg = core.reshape(1)
    pair = lax.axis_index("pair")
    pair_arg = pair.astype(jnp.int32).reshape(1)
    swap = [(0, 1), (1, 0)]
    anywhere = pl.BlockSpec(memory_space=pl.ANY)

    def struct(shape, dtype):
        return jax.ShapeDtypeStruct(shape, dtype)

    send = call(
        functools.partial(pack_kernel, slot),
        struct((regions, 2, half * slot, hours), BF),
        limit=FULL_VMEM,
        in_specs=[anywhere] * 2,
        out_specs=anywhere,
        scratch_shapes=[
            pltpu.VMEM((members, grid, hours), F32),
            pltpu.VMEM((1, recv), jnp.int32),
            pltpu.VMEM((regions, 2, half * slot, hours), BF),
            pltpu.SemaphoreType.DMA((3,)),
            pltpu.SemaphoreType.DMA((2,)),
        ],
    )(jnp.transpose(runoff, (1, 2, 0)), send_rows.reshape(1, recv))
    received = lax.all_to_all(
        send.reshape(regions * 2, half * slot, hours), ("side", "row", "core"), 0, 0
    ).reshape(regions, 2, half * slot, hours)
    raw = call(
        raw_kernel,
        struct((32 + outs, reaches), F32),
        in_specs=vmem(5),
        out_specs=vmem(1)[0],
    )(
        remap_index.T,
        remap_weight.T,
        class_id.T,
        outlets.reshape(1, outs),
        incidence.reshape(outs, reaches),
    )
    other = lax.ppermute(raw, "core", swap)
    table, mix, passing, cls_out, wide_mix, link, cls_target, cls_own = call(
        functools.partial(prep_kernel, slot, columns),
        (
            struct((hours, class_count * BLOCK), BF),
            struct((2, 2 * kap, SUB * outs), BF),
            struct((2, MB * outs, MB * outs), BF),
            struct((2, 8, MB * outs), F32),
            struct((2 * kap, SUB * reaches), BF),
            struct((2 * SUB * outs, SUB * reaches), BF),
            struct((8, MB * outs), F32),
            struct((8, reaches), F32),
        ),
        in_specs=[SCALAR] + vmem(4),
        out_specs=tuple(vmem(8)),
    )(core_arg, raw, other, kernel_rate.reshape(1, class_count), kernel_shape)

    panel_shape = struct((hours, wide), BF)
    float_shape = struct((hours, wide), F32)
    rows_send = call(
        rows_kernel,
        struct((regions, half * slot, hours), BF),
        in_specs=[SCALAR] + vmem(1),
        out_specs=vmem(1)[0],
    )(core_arg, received)
    panel, first = call(
        functools.partial(head_kernel, class_count),
        (panel_shape, panel_shape),
        in_specs=[SCALAR] + vmem(6),
        out_specs=tuple(vmem(2)),
    )(pair_arg, received, table, mix, passing, cls_out, rows_send)
    inflow = lax.ppermute(panel, "pair", [(0, 1), (1, 0)]) if pairs > 1 else panel
    rows_other = lax.ppermute(rows_send, "core", swap)
    first_other = lax.ppermute(first, "core", swap)

    base_shape = struct((hours, half * reaches), F32)
    shapes = [base_shape, float_shape] + [float_shape] * (pairs > 2)
    base_own, even, *odd = call(
        functools.partial(base_own_kernel, class_count),
        tuple(shapes),
        in_specs=[SCALAR] * 2 + vmem(6),
        out_specs=tuple(vmem(len(shapes))),
    )(core_arg, pair_arg, received, table, wide_mix, cls_own, mix, cls_out)
    base_other, done_first = call(
        functools.partial(other_kernel, class_count),
        (base_shape, struct((hours, half, reaches), BF)),
        in_specs=[SCALAR] * 2 + vmem(8),
        out_specs=tuple(vmem(2)),
    )(core_arg, pair_arg, rows_other, table, wide_mix, cls_own, first, base_own, link, cls_target)


    for step in range(1, pairs - 1):
        panel = call(
            functools.partial(hop_kernel, class_count),
            panel_shape,
            in_specs=vmem(6),
            out_specs=vmem(1)[0],
        )(inflow, table, passing, cls_out, even, odd[0])
        arriving = lax.ppermute(panel, "pair", [(step, step + 1), (step + 1, step)])
        inflow = jnp.where(pair == step + 1, arriving, inflow)

    def early(top, own):
        return call(
            functools.partial(early_kernel, class_count, top),
            struct((hours, half, reaches), BF),
            in_specs=[SCALAR] * 2 + vmem(5),
            out_specs=vmem(1)[0],
        )(core_arg, pair_arg, own, base_own, table, link, cls_target)

    def late(top, done, gotten, before):
        return call(
            functools.partial(late_kernel, class_count, top),
            struct((hours, members, reaches), BF),
            in_specs=[SCALAR] * 2 + vmem(6) + [anywhere] * len(before),
            out_specs=anywhere,
            scratch_shapes=[
                pltpu.VMEM((hours, half, reaches), BF),
                pltpu.SemaphoreType.DMA((1 + -(-hours // LANES),)),
            ],
            input_output_aliases={8: 0} if before else {},
        )(core_arg, pair_arg, done, gotten, base_other, table, link, cls_target, *before)

    own, given = call(
        functools.partial(last_hop_kernel, class_count),
        (panel_shape, panel_shape),
        in_specs=[SCALAR] * 2 + vmem(5) + [anywhere],
        out_specs=tuple(vmem(2)),
    )(core_arg, pair_arg, inflow, table, passing, cls_out, even, done_first)
    gotten = lax.ppermute(given, "core", swap)
    out = late(True, done_first, first_other, [])
    return late(False, early(False, own), gotten, [out])


def solution(mesh):
    regions, orders = mesh.shape["region"], mesh.shape["order"]
    split_mesh = Mesh(
        mesh.devices.reshape(regions // SIDE, SIDE, orders // 2, 2), ("row", "side", "pair", "core")
    )
    region = ("row", "side")
    order = ("pair", "core")
    every = region + order
    return jax.shard_map(
        local,
        mesh=split_mesh,
        in_specs=(
            P(None, None, every),
            P(region, order, None),
            P(every, None),
            P(every, None),
            P(every, None),
            P(),
            P(),
            P(region, order, None),
            P(region, order, None, None),
        ),
        out_specs=P(None, None, every),
        check_vma=False,
    )
```
